512 devices in a mesh: dp: 32 (over y, z_hi, core), tensor: 16 (over z_lo, x).
Axes of the slice: x: 4, y: 8, z: 8 (z_hi: 2, z_lo: 4; z = z_hi * 4 + z_lo), core: 2. Of those that a mesh axis runs over, the one named last changes fastest.
Arguments:
- queries: bfloat16 [30720, 8192], P('dp', 'tensor'), may hold values from -6 to 6
- features: bfloat16 [32, 128, 7680], P('dp'), may hold values from -6 to 6
- key_weight: bfloat16 [7680, 1024], P('dp', 'tensor'), may hold values from -0.0625 to 0.0625
- value_weight: bfloat16 [7680, 1024], P('dp', 'tensor'), may hold values from -0.0625 to 0.0625
- query_gain: float32 [128], replicated, may hold values from 0.25 to 1.75
- key_gain: float32 [128], replicated, may hold values from 0.25 to 1.75
- out_grad: bfloat16 [30720, 8192], P('dp', 'tensor'), may hold values from -6 to 6
- tile_counts: int32 [32], P('dp'), may hold values from 1 to 4, as said below
Outputs:
- query_grad: bfloat16 [30720, 8192], P('dp', 'tensor')
- feature_grad: bfloat16 [32, 128, 7680], P('dp', None, 'tensor')
- key_weight_grad: float32 [7680, 1024], P('dp', 'tensor')
- value_weight_grad: float32 [7680, 1024], P('dp', 'tensor')
The draws below stay inside these ranges and needn't reach their ends.
Inputs may be any that keep to these rules, and one draw needn't show every extreme that they name: Each sample's text attends to its first 32 * tile_counts image tokens; some sample has 4 tiles.
All inputs are finite; a program needn't handle non-finite values.
Results may differ from the reference program's by a relative error of at most 0.025.
Values may be sent and summed in bfloat16 or wider, within the bound.
A program may use at most 64 MiB of HBM per device.

```python
import math
from functools import partial
import jax
import jax.numpy as jnp
from jax import lax

FEAT = 7680
HD = 128
QH = 64
KVH = 8
GROUP = 8
TOK_DEV = 960
TILES = 4
TILE_ROWS = 32
IMG = 128
SAMPLES = 32
TOKENS = 30720
N_TENSOR = 16


def draw_tile_counts(key, part):
    key = jax.random.fold_in(key, 11)
    first_key, second_key = jax.random.split(key)
    counts = jax.random.randint(first_key, (SAMPLES,), 1, TILES + 1)
    spots = jax.random.randint(second_key, (2,), 0, SAMPLES)
    counts = counts.at[spots[1]].set(1)
    counts = counts.at[spots[0]].set(TILES)
    return counts.astype(jnp.int32)


def block_scale(key, extent, cuts, smallest, top_value):
    factor_of = 1.0
    for dim, shards_of in cuts:
        steps = jax.random.uniform(jax.random.fold_in(jax.random.fold_in(key, 6), dim), (shards_of,), jnp.float32, smallest / len(cuts), top_value / len(cuts))
        factor_of = factor_of * jnp.repeat(jnp.exp(steps), extent[dim] // shards_of).reshape((-1,) + (1,) * (len(extent) - 1 - dim))
    return factor_of


def noise(own_key, dims, width, most, shards=(), held_as=jnp.bfloat16):
    values = width * jax.random.normal(own_key, dims, jnp.float32)
    if shards:
        values = values * block_scale(own_key, dims, shards, -0.22, 0.18)
    return jnp.clip(values, -most, most).astype(held_as)


def setup_inputs(seed: int = 0) -> dict:
    seeds = jax.random.split(jax.random.key(seed), 9)
    queries = noise(seeds[0], (TOKENS, QH * HD), 1.0, 6.0, ((0, 32), (1, 16)))
    features = noise(seeds[1], (SAMPLES, IMG, FEAT), 1.0, 6.0, ((0, 32),))
    key_weight = noise(seeds[2], (FEAT, KVH * HD), FEAT ** -0.5, 0.0625, ((0, 32), (1, 16)))
    value_weight = noise(seeds[3], (FEAT, KVH * HD), FEAT ** -0.5, 0.0625, ((0, 32), (1, 16)))
    query_gain = jnp.clip(1.0 + 0.15 * jax.random.normal(seeds[4], (HD,), jnp.float32), 0.25, 1.75)
    key_gain = jnp.clip(1.0 + 0.15 * jax.random.normal(seeds[5], (HD,), jnp.float32), 0.25, 1.75)
    out_grad = noise(seeds[6], (TOKENS, QH * HD), 1.0, 6.0, ((0, 32), (1, 16)))
    tile_counts = draw_tile_counts(jax.random.fold_in(seeds[8], 71), 0)
    return {"queries": queries, "features": features, "key_weight": key_weight, "value_weight": value_weight, "query_gain": query_gain, "key_gain": key_gain, "out_grad": out_grad, "tile_counts": tile_counts}


EPS = 1e-05
HIGHEST = lax.Precision.HIGHEST

def round_trip(inputs):
    return lax.optimization_barrier(inputs.astype(jnp.bfloat16)).astype(jnp.float32)

def norm_rows(inputs, gain):
    scaling = lax.rsqrt(lax.optimization_barrier(jnp.mean(inputs * inputs, -1, keepdims=True)) + EPS)
    return (inputs * scaling * gain, scaling)

def norm_back(inputs, scaling, gain, upstream):
    weighted = upstream * gain
    return scaling * weighted - inputs * scaling ** 3 * lax.optimization_barrier(jnp.mean(weighted * inputs, -1, keepdims=True))

def sample_backward(operands, query_gain, key_gain):
    query_rows, upstream_rows, keys_pre, value_rows, tile_count = operands
    inverse = 1.0 / math.sqrt(HD)
    query_float = query_rows.astype(jnp.float32)
    normed_q, q_scaling = norm_rows(query_float, query_gain)
    query_bf = round_trip(normed_q).reshape(TOK_DEV, KVH, GROUP, HD)
    key_float = keys_pre.astype(jnp.float32)
    normed_k, k_scaling = norm_rows(key_float, key_gain)
    key_bf = round_trip(normed_k)
    value_float = value_rows.astype(jnp.float32)
    upstream = upstream_rows.astype(jnp.float32).reshape(TOK_DEV, KVH, GROUP, HD)
    scores = jnp.einsum('tkgd,ikd->tkgi', query_bf, key_bf, precision=HIGHEST) * inverse
    live_keys = (jnp.arange(IMG) < tile_count * TILE_ROWS).astype(jnp.float32)
    exponent = jnp.exp(scores) * live_keys
    probabilities = exponent / lax.optimization_barrier(jnp.sum(exponent, -1, keepdims=True))
    probs_bf = round_trip(probabilities)
    attended = jnp.einsum('tkgi,ikd->tkgd', probs_bf, value_float, precision=HIGHEST)
    row_delta = lax.optimization_barrier(jnp.sum(upstream * attended, -1, keepdims=True))
    value_grad = jnp.einsum('tkgi,tkgd->ikd', probs_bf, upstream, precision=HIGHEST)
    prob_grad = jnp.einsum('tkgd,ikd->tkgi', upstream, value_float, precision=HIGHEST)
    score_grad = round_trip(probabilities * (prob_grad - row_delta))
    normed_q_grad = jnp.einsum('tkgi,ikd->tkgd', score_grad, key_bf, precision=HIGHEST) * inverse
    normed_k_grad = jnp.einsum('tkgi,tkgd->ikd', score_grad, query_bf, precision=HIGHEST) * inverse
    query_grad = norm_back(query_float, q_scaling, query_gain, normed_q_grad.reshape(TOK_DEV, QH, HD))
    key_grad = norm_back(key_float, k_scaling, key_gain, normed_k_grad)
    return (query_grad.astype(jnp.bfloat16), key_grad, value_grad)

def split_blocks(matrix):
    column_width = KVH * HD // N_TENSOR
    return matrix.reshape(matrix.shape[0], N_TENSOR, column_width).transpose(1, 0, 2)

def sample_blocks(matrix):
    return matrix.reshape(SAMPLES, IMG, matrix.shape[-1])

def add_block(running, block_set):
    key_block, value_block, key_cols, value_cols = block_set
    term = jnp.dot(key_block, key_cols.T, preferred_element_type=jnp.float32)
    term = term + jnp.dot(value_block, value_cols.T, preferred_element_type=jnp.float32)
    return (running + round_trip(term), None)

def add_sample(running, block_set):
    feature_block, key_block, value_block = block_set
    contract = (((0,), (0,)), ((), ()))
    key_term = lax.dot_general(feature_block, key_block, contract, preferred_element_type=jnp.float32)
    value_term = lax.dot_general(feature_block, value_block, contract, preferred_element_type=jnp.float32)
    return ((running[0] + round_trip(key_term), running[1] + round_trip(value_term)), None)

def reference(queries, features, key_weight, value_weight, query_gain, key_gain, out_grad, tile_counts):
    flattened = features.reshape(SAMPLES * IMG, FEAT)
    keys_pre = jnp.dot(flattened, key_weight, preferred_element_type=jnp.float32).astype(jnp.bfloat16)
    value_rows = jnp.dot(flattened, value_weight, preferred_element_type=jnp.float32).astype(jnp.bfloat16)
    operands = (queries.reshape(SAMPLES, TOK_DEV, QH, HD), out_grad.reshape(SAMPLES, TOK_DEV, QH, HD), keys_pre.reshape(SAMPLES, IMG, KVH, HD), value_rows.reshape(SAMPLES, IMG, KVH, HD), tile_counts)
    query_grad, key_grad, value_grad = lax.map(partial(sample_backward, query_gain=query_gain, key_gain=key_gain), operands)
    key_sent = key_grad.astype(jnp.bfloat16).reshape(SAMPLES * IMG, KVH * HD)
    value_sent = value_grad.astype(jnp.bfloat16).reshape(SAMPLES * IMG, KVH * HD)
    feature_sum, ignored = lax.scan(add_block, jnp.zeros((SAMPLES * IMG, FEAT), jnp.float32), (split_blocks(key_sent), split_blocks(value_sent), split_blocks(key_weight), split_blocks(value_weight)))
    zeros_w = jnp.zeros((FEAT, KVH * HD), jnp.float32)
    weight_sums, ignored = lax.scan(add_sample, (zeros_w, zeros_w), (sample_blocks(flattened), sample_blocks(key_sent), sample_blocks(value_sent)))
    return (query_grad.reshape(TOKENS, QH * HD), feature_sum.astype(jnp.bfloat16).reshape(SAMPLES, IMG, FEAT), weight_sums[0], weight_sums[1])
```

```python
import functools
import math

import jax
import jax.numpy as jnp
from jax import lax
from jax.experimental import pallas as pl
from jax.experimental.pallas import tpu as pltpu
from jax.sharding import PartitionSpec as P

TILE_ROWS = 32
EPS = 1e-05
HD = 128
Y, X, ZL = 8, 4, 4
CH = 160
HOPS = {(0, 0): 4, (0, 1): 3, (1, 0): 3, (1, 1): 4}
F32 = jnp.float32
BF16 = jnp.bfloat16
NT = (((1,), (1,)), ((), ()))
TN = (((0,), (0,)), ((), ()))


def dot(a, b, dims=(((1,), (0,)), ((), ()))):
    return lax.dot_general(a, b, dims, preferred_element_type=F32)


def kernel(
    tc_ref, q_hbm, feat_hbm, kwt_hbm, vwt_hbm, qg_hbm, kg_hbm, do_hbm,
    dq_hbm, ft_hbm, kgw_hbm, vgw_hbm,
    q_s, do_s, dq_s, feat_s, featT, wbuf, dsT, qn_s, w2_s, own_s, par_s, kbf_s, vbf_s, far_s,
    farr_s, g4_s, fterm, wterm, xr_s, yr_s, x1_s, x2_s, hz_s, hzr_s, vg_s, kg_s,
    kwt_s, vwt_s, qg_s, kg_in_s, ft_s, kgw_s, vgw_s,
    loc_sem, ag_ss, ag_rs, agz_ss, agz_rs, agc_ss, agc_rs, p_ss, p_rs,
    c_ss, c_rs, y_ss, y_rs, x_ss, x_rs, zf_ss, zf_rs, wc_ss, wc_rs, gz_ss, gz_rs, h_ss, h_rs,
):
    d = lax.axis_index("dp")
    t = lax.axis_index("tensor")
    y, zh, core = d // 4, (d // 2) % 2, d % 2
    zl, x = t // 4, t % 4
    low = (t % 2) == 0

    def at_y(step):
        return (((y + step + Y) % Y) * 4 + zh * 2 + core, t)

    right, left = at_y(1), at_y(-1)
    far_core = (d + 1 - 2 * core, t)
    far_z = (d + 2 - 4 * zh, t)
    partner = (d, t + 1 - 2 * (t % 2))
    x_right = (d, zl * 4 + (x + 1) % X)
    x_left = (d, zl * 4 + (x + X - 1) % X)
    z_to = [(d, ((zl + k) % ZL) * 4 + x) for k in (1, 2, 3)]

    barrier = pltpu.get_barrier_semaphore()
    peers = [right, left, far_core, far_z, x_right, x_left] + z_to
    for peer in peers:
        pl.semaphore_signal(barrier, inc=1, device_id=peer, device_id_type=pl.DeviceIdType.MESH)

    tokens = q_s.shape[0]
    heads = q_s.shape[1] // HD
    width = CH * heads
    fetched = (
        (kwt_hbm, kwt_s), (vwt_hbm, vwt_s), (feat_hbm, feat_s), (q_hbm, q_s), (do_hbm, do_s),
        (qg_hbm, qg_s), (kg_hbm, kg_in_s),
    )
    copies = [
        pltpu.make_async_copy(src, dst, loc_sem.at[i]) for i, (src, dst) in enumerate(fetched)
    ]
    for copy in copies:
        copy.start()

    sent = []

    def send(src, dst, ssem, rsem, dev):
        copy = pltpu.make_async_remote_copy(
            src_ref=src, dst_ref=dst, send_sem=ssem, recv_sem=rsem,
            device_id=dev, device_id_type=pl.DeviceIdType.MESH,
        )
        copy.start()
        sent.append(copy)
        return copy

    copies[0].wait()
    copies[1].wait()
    shard = jnp.concatenate((kwt_s[...], vwt_s[...]), 0).astype(F32)
    rows = shard.shape[1]
    shard = jnp.concatenate((shard, jnp.zeros((HD, 256 - rows), F32)), 1)
    mine = 2 * y + zh
    wbuf[mine, core] = jnp.transpose(shard)[:rows].astype(BF16)

    pl.semaphore_wait(barrier, len(peers))

    def c_of(step, stream):
        zz = zh if stream == 0 else 1 - zh
        return 2 * ((y + step + Y) % Y) + zz

    def gather_send(stream, way, hop):
        c = c_of((1 - hop) if way == 0 else (hop - 1), stream)
        ref = wbuf.at[c, core]
        return send(ref, ref, ag_ss.at[stream, way, hop - 1], ag_rs.at[stream, way, hop - 1],
                    right if way == 0 else left)

    across = []

    def core_send(c):
        ref = wbuf.at[c, core]
        i = len(across)
        across.append(send(ref, ref, agc_ss.at[i], agc_rs.at[i], far_core))

    def z_copy(c):
        dest = c // ZL
        return dest, pltpu.make_async_remote_copy(
            src_ref=wbuf.at[c, core], dst_ref=w2_s.at[zl, c % ZL, core],
            send_sem=zf_ss.at[c], recv_sem=zf_rs.at[zl, c % ZL],
            device_id=(d, dest * X + x), device_id_type=pl.DeviceIdType.MESH,
        )

    def z_send(c):
        dest, copy = z_copy(c)

        @pl.when(dest != zl)
        def _():
            copy.start()

    ag = {}
    for way in (0, 1):
        ag[0, way, 1] = gather_send(0, way, 1)
    ref = wbuf.at[mine, core]
    zcopy = send(ref, ref, agz_ss, agz_rs, far_z)
    core_send(mine)
    z_send(mine)

    copies[2].wait()
    copies[3].wait()
    copies[5].wait()
    copies[6].wait()
    inverse = 1.0 / math.sqrt(HD)
    qg = qg_s[...]
    kg = kg_in_s[...]

    def transpose_part(part):
        for i in range(part * 12, part * 12 + 12):
            featT[i * 128:(i + 1) * 128, :] = jnp.transpose(
                feat_s[:, i * 128:(i + 1) * 128].astype(F32)
            ).astype(BF16)

    def stack(ref, chunk):
        at = slice(chunk * CH, (chunk + 1) * CH)
        return jnp.concatenate([ref[at, h * HD:(h + 1) * HD] for h in range(heads)], 0)

    def query_norm(chunk):
        xq = stack(q_s, chunk).astype(F32)
        r = lax.rsqrt(jnp.mean(xq * xq, -1, keepdims=True) + EPS)
        qn_s[chunk * width:(chunk + 1) * width, :] = (xq * r * qg).astype(BF16)

    def gather_step(stream, hop):
        for way in (0, 1):
            if hop > HOPS[stream, way]:
                continue
            ag[stream, way, hop].wait_recv()
            if hop < HOPS[stream, way]:
                ag[stream, way, hop + 1] = gather_send(stream, way, hop + 1)
            c = c_of(-hop if way == 0 else hop, stream)
            core_send(c)
            z_send(c)

    for hop in range(1, 6):
        if hop <= 4:
            transpose_part(hop - 1)
            gather_step(0, hop)
        if hop == 1:
            zcopy.wait_recv()
            for way in (0, 1):
                ag[1, way, 1] = gather_send(1, way, 1)
            core_send(c_of(0, 1))
            z_send(c_of(0, 1))
        else:
            gather_step(1, hop - 1)
        query_norm(hop - 1)
    for copy in across:
        copy.wait_recv()

    proj = jnp.zeros((HD, HD), F32)
    for part in range(4):
        cols = feat_s[:, part * 1920:(part + 1) * 1920]
        proj += dot(cols, wbuf[part * 4:(part + 1) * 4].reshape(1920, HD))
    own_s[...] = proj.astype(BF16)
    pcopy = send(own_s, par_s, p_ss.at[0], p_rs.at[0], partner)
    copies[4].wait()
    transpose_part(4)
    query_norm(5)
    lane = lax.broadcasted_iota(jnp.int32, (HD, HD), 1)
    half = lane < 64
    lowf = jnp.where(low, 1.0, 0.0).astype(F32)
    own = own_s[...].astype(F32)
    pcopy.wait_recv()
    other = par_s[...].astype(F32)
    first = own * lowf + other * (1.0 - lowf)
    second = other * lowf + own * (1.0 - lowf)
    keys = jnp.where(half, first, pltpu.roll(second, 64, 1))
    values = jnp.where(half, pltpu.roll(first, 64, 1), second)
    k_scale = lax.rsqrt(jnp.mean(keys * keys, -1, keepdims=True) + EPS)
    kbf_s[...] = (keys * k_scale * kg).astype(BF16)
    vbf_s[...] = values.astype(BF16)
    live = (
        lax.broadcasted_iota(jnp.int32, (HD, 1), 0) < tc_ref[0] * TILE_ROWS
    ).astype(F32)
    vg_s[...] = jnp.zeros_like(vg_s)
    kg_s[...] = jnp.zeros_like(kg_s)

    def attend(chunk, carry):
        at = pl.ds(pl.multiple_of(chunk * CH, CH), CH)
        wide = pl.ds(pl.multiple_of(chunk * width, width), width)
        qn = qn_s[wide, :]
        do = jnp.concatenate([do_s[at, h * HD:(h + 1) * HD] for h in range(heads)], 0)
        e = jnp.exp(dot(kbf_s[...], qn, NT) * inverse) * live
        p = e * (1.0 / jnp.sum(e, 0, keepdims=True))
        pb = p.astype(BF16)
        vg_s[...] += dot(pb, do)
        pg = dot(vbf_s[...], do, NT)
        delta = jnp.sum(pb.astype(F32) * pg, 0, keepdims=True)
        ds = (p * (pg - delta)).astype(BF16)
        dsT[:, wide] = ds
        kg_s[...] += dot(ds, qn)
        return carry

    lax.fori_loop(0, tokens // CH, attend, 0, unroll=2)

    weighted = kg_s[...] * (inverse * kg)
    key_grad = k_scale * weighted - keys * (
        k_scale * k_scale * k_scale * jnp.mean(weighted * keys, -1, keepdims=True)
    )
    value_grad = vg_s[...]
    low_part = jnp.where(half, key_grad, pltpu.roll(value_grad, 64, 1))
    high_part = jnp.where(half, pltpu.roll(key_grad, 64, 1), value_grad)
    far_s[...] = (high_part * lowf + low_part * (1.0 - lowf)).astype(BF16)
    own_grad = low_part * lowf + high_part * (1.0 - lowf)
    fcopy = send(far_s, farr_s, p_ss.at[1], p_rs.at[1], partner)

    def query_back(chunk):
        xq = stack(q_s, chunk).astype(F32)
        r = lax.rsqrt(jnp.mean(xq * xq, -1, keepdims=True) + EPS)
        ds = dsT[:, chunk * width:(chunk + 1) * width]
        u = dot(ds, kbf_s[...], TN) * (inverse * qg)
        m = jnp.mean(u * xq, -1, keepdims=True)
        back = (r * u - xq * (r * r * r * m)).astype(BF16)
        for h in range(heads):
            dq_s[chunk * CH:(chunk + 1) * CH, h * HD:(h + 1) * HD] = back[h * CH:(h + 1) * CH]

    query_back(0)
    fcopy.wait_recv()
    g4_s[zl] = (own_grad + farr_s[...].astype(F32)).astype(BF16)
    g = g4_s[zl]
    gz = []
    for k in (1, 2, 0):
        gz.append(send(g4_s.at[zl], g4_s.at[zl], gz_ss.at[k], gz_rs.at[k], z_to[k]))

    order = (4, 3, 5, 2, 6, 1, 7, 0)
    crossing = {}
    for i, step in enumerate(order):
        yy = (y + step) % Y
        pair = featT[pl.ds(pl.multiple_of(yy * 960, 960), 960), :]
        wterm[pl.ds(2 * yy, 2)] = dot(pair, g).astype(BF16).reshape(2, 2, 240, HD)
        crossing[step] = send(
            wterm.at[pl.ds(2 * yy, 2), 1 - core], xr_s.at[pl.ds(2 * yy, 2)],
            c_ss.at[i], c_rs.at[i], far_core,
        )

    def feature_term(xx):
        total = dot(wbuf[zl * X + xx].reshape(480, HD), g, NT)
        for dz in (1, 2, 3):
            src = (zl + dz) % ZL
            total += dot(w2_s[src, xx].reshape(480, HD), g4_s[src], NT)
        return total

    x2, xp, xm = (x + 2) % X, (x + 1) % X, (x + 3) % X
    xs = {}

    def x_send(name, slot, src, dst, dev):
        xs[name] = send(src, dst, x_ss.at[slot], x_rs.at[slot], dev)

    def x_start():
        for copy in gz + wc:
            copy.wait_recv()
        for xx in (x2, xp, xm):
            fterm[xx] = feature_term(xx).astype(BF16).reshape(2, 240, HD)
            if xx is x2:
                x_send("r1", 0, fterm.at[x2, 0], x1_s.at[0], x_right)
                x_send("l1", 1, fterm.at[x2, 1], x1_s.at[1], x_left)
            elif xx is xp:
                x_send("r2", 2, fterm.at[xp, 1], x2_s.at[0, 1], x_right)
            else:
                x_send("l2", 3, fterm.at[xm, 0], x2_s.at[1, 0], x_left)

    wc = []

    def w2_across():
        for dz in (1, 3, 2):
            src = (zl + dz) % ZL
            for i in range(4):
                ref = w2_s.at[src, i, core]
                pltpu.make_async_remote_copy(
                    src_ref=ref, dst_ref=ref, send_sem=zf_ss.at[0], recv_sem=zf_rs.at[src, i],
                    device_id=far_core, device_id_type=pl.DeviceIdType.MESH,
                ).wait_recv()
                wc.append(send(ref, ref, wc_ss.at[dz - 1, i], wc_rs.at[dz - 1, i], far_core))

    slots = {}
    for key in ((0, 0), (1, 1), (0, 1), (1, 0)):
        for hop in range(1, HOPS[key] + 1):
            slots[key + (hop,)] = len(slots)
    ys = {}

    def merge(step, streams=(0, 1)):
        crossing[step % Y].wait_recv()
        for stream in streams:
            c = c_of(step, stream)
            total = wterm[c, core].astype(F32) + xr_s[c].astype(F32)
            wterm[c, core] = total.astype(BF16)

    def ring_send(stream, way, hop):
        step = HOPS[stream, way] - hop + 1
        c = c_of(step if way == 0 else -step, stream)
        slot = slots[stream, way, hop]
        if hop > 1:
            ys[stream, way, hop - 1].wait_recv()
            last = slots[stream, way, hop - 1]
            wterm[c, core] = (
                wterm[c, core].astype(F32) + yr_s[last].astype(F32)
            ).astype(BF16)
        ys[stream, way, hop] = send(
            wterm.at[c, core], yr_s.at[slot], y_ss.at[slot], y_rs.at[slot],
            right if way == 0 else left,
        )

    def x_relay():
        for name, way, xx in (("r", 0, xp), ("l", 1, xm)):
            xs[name + "1"].wait_recv()
            fterm[xx, way] = (
                fterm[xx, way].astype(F32) + x1_s[way].astype(F32)).astype(BF16)
            x_send(name + "3", 4 + way, fterm.at[xx, way], x2_s.at[way, way],
                   x_right if way == 0 else x_left)

    merge(4)
    ring_send(0, 0, 1)
    ring_send(1, 1, 1)
    merge(3)
    ring_send(1, 0, 1)
    merge(5)
    ring_send(0, 1, 1)
    w2_across()
    merge(2)
    merge(6)
    query_back(1)
    ring_send(0, 0, 2)
    ring_send(1, 1, 2)
    ring_send(1, 0, 2)
    ring_send(0, 1, 2)
    merge(1)
    merge(7)
    merge(0)
    x_start()
    ring_send(0, 0, 3)
    ring_send(1, 1, 3)
    ring_send(1, 0, 3)
    ring_send(0, 1, 3)
    own_term = feature_term(x)
    x_relay()
    query_back(2)
    query_back(3)
    ring_send(0, 0, 4)
    ring_send(1, 1, 4)
    for name in ("r2", "l2", "r3", "l3"):
        xs[name].wait_recv()
    own_term += x2_s[0].reshape(480, HD).astype(F32) + x2_s[1].reshape(480, HD).astype(F32)
    ft_s[...] = own_term.astype(BF16)
    query_back(4)
    query_back(5)
    outs = [
        pltpu.make_async_copy(dq_s, dq_hbm, loc_sem.at[7]),
        pltpu.make_async_copy(ft_s, ft_hbm, loc_sem.at[8]),
        pltpu.make_async_copy(kgw_s, kgw_hbm, loc_sem.at[9]),
        pltpu.make_async_copy(vgw_s, vgw_hbm, loc_sem.at[10]),
    ]
    outs[0].start()
    outs[1].start()

    def final_rows(stream):
        c = c_of(0, stream)
        total = wterm[c, core].astype(F32)
        for way in (0, 1):
            hop = HOPS[stream, way]
            ys[stream, way, hop].wait_recv()
            total += yr_s[slots[stream, way, hop]].astype(F32)
        return total

    hz_s[...] = final_rows(1).astype(BF16)
    hcopy = send(hz_s, hzr_s, h_ss, h_rs, far_z)
    own_rows = final_rows(0)
    hcopy.wait_recv()
    own_rows += hzr_s[...].astype(F32)
    padded = jnp.concatenate((own_rows, jnp.zeros((256 - rows, HD), F32)), 0)
    turned = jnp.transpose(padded)
    kgw_s[...] = turned[:64, :rows]
    vgw_s[...] = turned[64:, :rows]
    outs[2].start()
    outs[3].start()
    for dz in (1, 2, 3):
        for i in range(4):
            z_copy(4 * ((zl + dz) % ZL) + i)[1].wait_send()
    for copy in sent:
        copy.wait_send()
    for copy in outs:
        copy.wait()


def copy_out(a, b, c, e, a_out, b_out, c_out, e_out, sems):
    copies = [
        pltpu.make_async_copy(src, dst, sems.at[i])
        for i, (src, dst) in enumerate(((a, a_out), (b, b_out), (c, c_out), (e, e_out)))
    ]
    for copy in copies:
        copy.start()
    for copy in copies:
        copy.wait()


def shards(
    queries, features, key_weight, value_weight, query_gain, key_gain, out_grad, tile_counts
):
    samples, own_rows, feature_width = features.shape
    tokens, q_width = queries.shape
    rows, column_half = key_weight.shape
    anyspec = pl.BlockSpec(memory_space=pl.ANY)
    dma = pltpu.SemaphoreType.DMA
    piece = (rows, HD)
    scratch = [
        pltpu.VMEM((tokens, q_width), BF16),
        pltpu.VMEM((tokens, q_width), BF16),
        pltpu.VMEM((tokens, q_width), BF16),
        pltpu.VMEM((own_rows, feature_width), BF16),
        pltpu.VMEM((feature_width, own_rows), BF16),
        pltpu.VMEM((16, 2) + piece, BF16),
        pltpu.VMEM((HD, tokens * q_width // HD), BF16),
        pltpu.VMEM((tokens * q_width // HD, HD), BF16),
        pltpu.VMEM((ZL, X, 2) + piece, BF16),
    ]
    scratch += [pltpu.VMEM((HD, HD), BF16)] * 6
    scratch += [
        pltpu.VMEM((ZL, HD, HD), BF16),
        pltpu.VMEM((X, 2) + piece, BF16),
        pltpu.VMEM((16, 2) + piece, BF16),
        pltpu.VMEM((16,) + piece, BF16),
        pltpu.VMEM((14,) + piece, BF16),
        pltpu.VMEM((2,) + piece, BF16),
        pltpu.VMEM((2, 2) + piece, BF16),
        pltpu.VMEM(piece, BF16),
        pltpu.VMEM(piece, BF16),
        pltpu.VMEM((HD, HD), F32),
        pltpu.VMEM((HD, HD), F32),
        pltpu.VMEM((column_half, rows), BF16),
        pltpu.VMEM((column_half, rows), BF16),
        pltpu.VMEM((1, HD), F32),
        pltpu.VMEM((1, HD), F32),
        pltpu.VMEM((2 * rows, own_rows), BF16),
        pltpu.VMEM((column_half, rows), F32),
        pltpu.VMEM((column_half, rows), F32),
        dma((11,)),
        dma((2, 2, 4)), dma((2, 2, 4)), dma, dma, dma((16,)), dma((16,)), dma((2,)), dma((2,)),
        dma((8,)), dma((8,)), dma((14,)), dma((14,)), dma((6,)), dma((6,)),
        dma((16,)), dma((4, 4)), dma((3, 4)), dma((3, 4)), dma((3,)), dma((3,)), dma, dma,
    ]
    out_shape = (
        jax.ShapeDtypeStruct((tokens, q_width), BF16),
        jax.ShapeDtypeStruct((2 * rows, own_rows), BF16),
        jax.ShapeDtypeStruct((column_half, rows), F32),
        jax.ShapeDtypeStruct((column_half, rows), F32),
    )
    results = pl.pallas_call(
        kernel,
        out_shape=out_shape,
        in_specs=[pl.BlockSpec(memory_space=pltpu.SMEM)] + [anyspec] * 7,
        out_specs=(anyspec,) * 4,
        scratch_shapes=scratch,
        compiler_params=pltpu.CompilerParams(
            collective_id=0, has_side_effects=True, vmem_limit_bytes=62 * 1024 * 1024
        ),
        cost_estimate=pl.CostEstimate(
            flops=1600000000, bytes_accessed=8000000, transcendentals=500000
        ),
    )(
        tile_counts, queries, features.reshape(own_rows, feature_width), key_weight.T,
        value_weight.T, query_gain.reshape(1, HD), key_gain.reshape(1, HD), out_grad,
    )
    query_grad, feature_t, key_t, value_t = pl.pallas_call(
        copy_out,
        out_shape=out_shape,
        in_specs=[anyspec] * 4,
        out_specs=(anyspec,) * 4,
        scratch_shapes=[dma((4,))],
        compiler_params=pltpu.CompilerParams(vmem_limit_bytes=62 * 1024 * 1024),
        cost_estimate=pl.CostEstimate(flops=0, bytes_accessed=3000000, transcendentals=0),
    )(*results)
    return (query_grad, feature_t.T.reshape(samples, own_rows, 2 * rows), key_t.T, value_t.T)


def solution(mesh):
    placed = (
        P("dp", "tensor"),
        P("dp", None, None),
        P("dp", "tensor"),
        P("dp", "tensor"),
        P(),
        P(),
        P("dp", "tensor"),
        P("dp"),
    )
    return jax.shard_map(
        shards,
        mesh=mesh,
        in_specs=placed,
        out_specs=(
            P("dp", "tensor"),
            P("dp", None, "tensor"),
            P("dp", "tensor"),
            P("dp", "tensor"),
        ),
        check_vma=False,
    )
```

```python
import functools
import math

import jax
import jax.numpy as jnp
from jax import lax
from jax.experimental import pallas as pl
from jax.experimental.pallas import tpu as pltpu
from jax.sharding import PartitionSpec as P

TILE_ROWS = 32
EPS = 1e-05
HD = 128
Y, X, ZL = 8, 4, 4
CH = 160
HOPS = {(0, 0): 4, (0, 1): 3, (1, 0): 3, (1, 1): 4}
F32 = jnp.float32
BF16 = jnp.bfloat16
NT = (((1,), (1,)), ((), ()))
TN = (((0,), (0,)), ((), ()))


def dot(a, b, dims=(((1,), (0,)), ((), ()))):
    return lax.dot_general(a, b, dims, preferred_element_type=F32)


def kernel(
    tc_ref, q_hbm, feat_hbm, kwt_hbm, vwt_hbm, qg_hbm, kg_hbm, do_hbm,
    dq_hbm, ft_hbm, kgw_hbm, vgw_hbm,
    q_s, do_s, dq_s, feat_s, featT, wbuf, dsT, qn_s, w2_s, own_s, par_s, kbf_s, vbf_s, far_s,
    farr_s, g4_s, go_s, fterm, wterm, fx_s, yr_s, x1_s, x2_s, hz_s, hzr_s, vg_s, kg_s,
    kwt_s, vwt_s, qg_s, kg_in_s, ft_s, kgw_s, vgw_s,
    loc_sem, ag_ss, ag_rs, agz_ss, agz_rs, agc_ss, agc_rs, p_ss, p_rs,
    c_ss, c_rs, y_ss, y_rs, x_ss, x_rs, zf_ss, zf_rs, wc_ss, wc_rs, gz_ss, gz_rs, h_ss, h_rs,
):
    d = lax.axis_index("dp")
    t = lax.axis_index("tensor")
    y, zh, core = d // 4, (d // 2) % 2, d % 2
    zl, x = t // 4, t % 4
    low = (t % 2) == 0

    def at_y(step):
        return (((y + step + Y) % Y) * 4 + zh * 2 + core, t)

    right, left = at_y(1), at_y(-1)
    far_core = (d + 1 - 2 * core, t)
    far_z = (d + 2 - 4 * zh, t)
    partner = (d, t + 1 - 2 * (t % 2))
    x_right = (d, zl * 4 + (x + 1) % X)
    x_left = (d, zl * 4 + (x + X - 1) % X)
    z_to = [(d, ((zl + k) % ZL) * 4 + x) for k in (1, 2, 3)]

    barrier = pltpu.get_barrier_semaphore()
    peers = [right, left, far_core, far_z, x_right, x_left] + z_to
    for peer in peers:
        pl.semaphore_signal(barrier, inc=1, device_id=peer, device_id_type=pl.DeviceIdType.MESH)

    tokens = q_s.shape[0]
    heads = q_s.shape[1] // HD
    width = CH * heads
    fetched = (
        (kwt_hbm, kwt_s), (vwt_hbm, vwt_s), (feat_hbm, feat_s), (q_hbm, q_s), (do_hbm, do_s),
        (qg_hbm, qg_s), (kg_hbm, kg_in_s),
    )
    copies = [
        pltpu.make_async_copy(src, dst, loc_sem.at[i]) for i, (src, dst) in enumerate(fetched)
    ]
    for copy in copies:
        copy.start()

    sent = []

    def send(src, dst, ssem, rsem, dev):
        copy = pltpu.make_async_remote_copy(
            src_ref=src, dst_ref=dst, send_sem=ssem, recv_sem=rsem,
            device_id=dev, device_id_type=pl.DeviceIdType.MESH,
        )
        copy.start()
        sent.append(copy)
        return copy

    copies[0].wait()
    copies[1].wait()
    shard = jnp.concatenate((kwt_s[...], vwt_s[...]), 0).astype(F32)
    rows = shard.shape[1]
    shard = jnp.concatenate((shard, jnp.zeros((HD, 256 - rows), F32)), 1)
    mine = 2 * y + zh
    wbuf[mine, core] = jnp.transpose(shard)[:rows].astype(BF16)

    pl.semaphore_wait(barrier, len(peers))

    def c_of(step, stream):
        zz = zh if stream == 0 else 1 - zh
        return 2 * ((y + step + Y) % Y) + zz

    def gather_send(stream, way, hop):
        c = c_of((1 - hop) if way == 0 else (hop - 1), stream)
        ref = wbuf.at[c, core]
        return send(ref, ref, ag_ss.at[stream, way, hop - 1], ag_rs.at[stream, way, hop - 1],
                    right if way == 0 else left)

    across = []

    def core_send(c):
        ref = wbuf.at[c, core]
        i = len(across)
        across.append(send(ref, ref, agc_ss.at[i], agc_rs.at[i], far_core))

    def z_copy(c):
        dest = c // ZL
        return dest, pltpu.make_async_remote_copy(
            src_ref=wbuf.at[c, core], dst_ref=w2_s.at[zl, c % ZL, core],
            send_sem=zf_ss.at[c], recv_sem=zf_rs.at[zl, c % ZL],
            device_id=(d, dest * X + x), device_id_type=pl.DeviceIdType.MESH,
        )

    def z_send(c):
        dest, copy = z_copy(c)

        @pl.when(dest != zl)
        def _():
            copy.start()

    ag = {}
    for way in (0, 1):
        ag[0, way, 1] = gather_send(0, way, 1)
    ref = wbuf.at[mine, core]
    zcopy = send(ref, ref, agz_ss, agz_rs, far_z)
    core_send(mine)
    z_send(mine)

    copies[2].wait()
    copies[3].wait()
    copies[5].wait()
    copies[6].wait()
    inverse = 1.0 / math.sqrt(HD)
    qg = qg_s[...]
    kg = kg_in_s[...]

    shared = []

    def transpose_part(part):
        cols = feat_s[:, part * 1920:(part + 1) * 1920]
        group = pl.ds(part * 4, 4)
        featT[group] = jnp.transpose(cols).reshape(4, 2, 240, HD)
        shared.append(send(
            featT.at[group, 1 - core], fx_s.at[group], c_ss.at[part], c_rs.at[part], far_core))

    def stack(ref, chunk):
        at = slice(chunk * CH, (chunk + 1) * CH)
        return jnp.concatenate([ref[at, h * HD:(h + 1) * HD] for h in range(heads)], 0)

    def query_norm(chunk):
        xq = stack(q_s, chunk).astype(F32)
        r = lax.rsqrt(jnp.mean(xq * xq, -1, keepdims=True) + EPS)
        qn_s[chunk * width:(chunk + 1) * width, :] = (xq * r * qg).astype(BF16)

    def gather_step(stream, hop):
        for way in (0, 1):
            if hop > HOPS[stream, way]:
                continue
            ag[stream, way, hop].wait_recv()
            if hop < HOPS[stream, way]:
                ag[stream, way, hop + 1] = gather_send(stream, way, hop + 1)
            c = c_of(-hop if way == 0 else hop, stream)
            core_send(c)
            z_send(c)

    arrived = 0

    def project(parts):
        total = jnp.zeros((HD, HD), F32)
        for part in parts:
            at = (y // 2 + part) % 4
            cols = feat_s[:, pl.ds(pl.multiple_of(at * 1920, 1920), 1920)]
            total += dot(cols, wbuf[pl.ds(4 * at, 4)].reshape(1920, HD))
        return total

    proj = jnp.zeros((HD, HD), F32)
    for hop in range(1, 6):
        if hop <= 4:
            transpose_part(hop - 1)
            gather_step(0, hop)
        if hop == 1:
            zcopy.wait_recv()
            for way in (0, 1):
                ag[1, way, 1] = gather_send(1, way, 1)
            core_send(c_of(0, 1))
            z_send(c_of(0, 1))
        else:
            gather_step(1, hop - 1)
        if hop <= 4:
            query_norm(hop - 1)
        if hop >= 3:
            until, parts = {3: (8, (0,)), 4: (15, (1, 3)), 5: (16, (2,))}[hop]
            for copy in across[arrived:until]:
                copy.wait_recv()
            arrived = until
            proj += project(parts)
    own_s[...] = proj.astype(BF16)
    pcopy = send(own_s, par_s, p_ss.at[0], p_rs.at[0], partner)
    copies[4].wait()
    query_norm(4)
    query_norm(5)
    lane = lax.broadcasted_iota(jnp.int32, (HD, HD), 1)
    half = lane < 64
    lowf = jnp.where(low, 1.0, 0.0).astype(F32)
    own = own_s[...].astype(F32)
    pcopy.wait_recv()
    other = par_s[...].astype(F32)
    first = own * lowf + other * (1.0 - lowf)
    second = other * lowf + own * (1.0 - lowf)
    keys = jnp.where(half, first, pltpu.roll(second, 64, 1))
    values = jnp.where(half, pltpu.roll(first, 64, 1), second)
    k_scale = lax.rsqrt(jnp.mean(keys * keys, -1, keepdims=True) + EPS)
    kbf_s[...] = (keys * k_scale * kg).astype(BF16)
    vbf_s[...] = values.astype(BF16)
    live = (
        lax.broadcasted_iota(jnp.int32, (HD, 1), 0) < tc_ref[0] * TILE_ROWS
    ).astype(F32)
    vg_s[...] = jnp.zeros_like(vg_s)
    kg_s[...] = jnp.zeros_like(kg_s)

    def attend(chunk, carry):
        at = pl.ds(pl.multiple_of(chunk * CH, CH), CH)
        wide = pl.ds(pl.multiple_of(chunk * width, width), width)
        qn = qn_s[wide, :]
        do = jnp.concatenate([do_s[at, h * HD:(h + 1) * HD] for h in range(heads)], 0)
        e = jnp.exp(dot(kbf_s[...], qn, NT) * inverse) * live
        p = e * (1.0 / jnp.sum(e, 0, keepdims=True))
        pb = p.astype(BF16)
        vg_s[...] += dot(pb, do)
        pg = dot(vbf_s[...], do, NT)
        delta = jnp.sum(pb.astype(F32) * pg, 0, keepdims=True)
        ds = (p * (pg - delta)).astype(BF16)
        dsT[:, wide] = ds
        kg_s[...] += dot(ds, qn)
        return carry

    lax.fori_loop(0, tokens // CH, attend, 0, unroll=3)

    weighted = kg_s[...] * (inverse * kg)
    key_grad = k_scale * weighted - keys * (
        k_scale * k_scale * k_scale * jnp.mean(weighted * keys, -1, keepdims=True)
    )
    value_grad = vg_s[...]
    low_part = jnp.where(half, key_grad, pltpu.roll(value_grad, 64, 1))
    high_part = jnp.where(half, pltpu.roll(key_grad, 64, 1), value_grad)
    far_s[...] = (high_part * lowf + low_part * (1.0 - lowf)).astype(BF16)
    own_grad = low_part * lowf + high_part * (1.0 - lowf)
    fcopy = send(far_s, farr_s, p_ss.at[1], p_rs.at[1], partner)

    def query_back(chunk):
        xq = stack(q_s, chunk).astype(F32)
        r = lax.rsqrt(jnp.mean(xq * xq, -1, keepdims=True) + EPS)
        ds = dsT[:, chunk * width:(chunk + 1) * width]
        u = dot(ds, kbf_s[...], TN) * (inverse * qg)
        m = jnp.mean(u * xq, -1, keepdims=True)
        back = (r * u - xq * (r * r * r * m)).astype(BF16)
        for h in range(heads):
            dq_s[chunk * CH:(chunk + 1) * CH, h * HD:(h + 1) * HD] = back[h * CH:(h + 1) * CH]

    query_back(0)
    fcopy.wait_recv()
    g4_s[zl] = (own_grad + farr_s[...].astype(F32)).astype(BF16)
    g = g4_s[zl]
    gcopy = send(g4_s.at[zl], go_s, c_ss.at[4], c_rs.at[4], far_core)
    gz = []
    for k in (1, 2, 0):
        gz.append(send(g4_s.at[zl], g4_s.at[zl], gz_ss.at[k], gz_rs.at[k], z_to[k]))

    query_back(1)
    gcopy.wait_recv()
    go = go_s[...]
    for copy in shared:
        copy.wait_recv()

    def weight_term(step):
        for stream in (1, 0):
            c = c_of(step, stream)
            wterm[c] = (dot(featT[c, core], g) + dot(fx_s[c], go)).astype(BF16)

    def feature_term(xx):
        total = dot(wbuf[zl * X + xx].reshape(480, HD), g, NT)
        for dz in (1, 2, 3):
            src = (zl + dz) % ZL
            total += dot(w2_s[src, xx].reshape(480, HD), g4_s[src], NT)
        return total

    x2, xp, xm = (x + 2) % X, (x + 1) % X, (x + 3) % X
    xs = {}

    def x_send(name, slot, src, dst, dev):
        xs[name] = send(src, dst, x_ss.at[slot], x_rs.at[slot], dev)

    def x_start():
        for copy in gz + wc:
            copy.wait_recv()
        for xx in (x2, xp, xm):
            fterm[xx] = feature_term(xx).astype(BF16).reshape(2, 240, HD)
            if xx is x2:
                x_send("r1", 0, fterm.at[x2, 0], x1_s.at[0], x_right)
                x_send("l1", 1, fterm.at[x2, 1], x1_s.at[1], x_left)
            elif xx is xp:
                x_send("r2", 2, fterm.at[xp, 1], x2_s.at[0, 1], x_right)
            else:
                x_send("l2", 3, fterm.at[xm, 0], x2_s.at[1, 0], x_left)

    wc = []

    def w2_across():
        for dz in (1, 3, 2):
            src = (zl + dz) % ZL
            for i in range(4):
                ref = w2_s.at[src, i, core]
                pltpu.make_async_remote_copy(
                    src_ref=ref, dst_ref=ref, send_sem=zf_ss.at[0], recv_sem=zf_rs.at[src, i],
                    device_id=far_core, device_id_type=pl.DeviceIdType.MESH,
                ).wait_recv()
                wc.append(send(ref, ref, wc_ss.at[dz - 1, i], wc_rs.at[dz - 1, i], far_core))

    slots = {}
    for key in ((0, 0), (1, 1), (0, 1), (1, 0)):
        for hop in range(1, HOPS[key] + 1):
            slots[key + (hop,)] = len(slots)
    ys = {}

    def ring_send(stream, way, hop):
        step = HOPS[stream, way] - hop + 1
        c = c_of(step if way == 0 else -step, stream)
        slot = slots[stream, way, hop]
        if hop > 1:
            ys[stream, way, hop - 1].wait_recv()
            last = slots[stream, way, hop - 1]
            wterm[c] = (wterm[c].astype(F32) + yr_s[last].astype(F32)).astype(BF16)
        ys[stream, way, hop] = send(
            wterm.at[c], yr_s.at[slot], y_ss.at[slot], y_rs.at[slot],
            right if way == 0 else left,
        )

    def x_relay():
        for name, way, xx in (("r", 0, xp), ("l", 1, xm)):
            xs[name + "1"].wait_recv()
            fterm[xx, way] = (
                fterm[xx, way].astype(F32) + x1_s[way].astype(F32)).astype(BF16)
            x_send(name + "3", 4 + way, fterm.at[xx, way], x2_s.at[way, way],
                   x_right if way == 0 else x_left)

    def ring_hop(hop):
        for stream, way in ((1, 1), (1, 0), (0, 0), (0, 1)):
            if hop <= HOPS[stream, way]:
                ring_send(stream, way, hop)

    weight_term(4)
    ring_send(1, 1, 1)
    ring_send(0, 0, 1)
    weight_term(3)
    ring_send(1, 0, 1)
    weight_term(5)
    ring_send(0, 1, 1)
    weight_term(2)
    weight_term(6)
    w2_across()
    ring_hop(2)
    weight_term(1)
    weight_term(7)
    weight_term(0)
    x_start()
    ring_hop(3)
    own_term = feature_term(x)
    x_relay()
    query_back(2)
    query_back(3)
    ring_hop(4)
    for name in ("r2", "l2", "r3", "l3"):
        xs[name].wait_recv()
    own_term += x2_s[0].reshape(480, HD).astype(F32) + x2_s[1].reshape(480, HD).astype(F32)
    ft_s[...] = own_term.astype(BF16)
    query_back(4)
    query_back(5)
    outs = [
        pltpu.make_async_copy(dq_s, dq_hbm, loc_sem.at[7]),
        pltpu.make_async_copy(ft_s, ft_hbm, loc_sem.at[8]),
        pltpu.make_async_copy(kgw_s, kgw_hbm, loc_sem.at[9]),
        pltpu.make_async_copy(vgw_s, vgw_hbm, loc_sem.at[10]),
    ]
    outs[0].start()
    outs[1].start()

    def final_rows(stream):
        c = c_of(0, stream)
        total = wterm[c].astype(F32)
        for way in (0, 1):
            hop = HOPS[stream, way]
            ys[stream, way, hop].wait_recv()
            total += yr_s[slots[stream, way, hop]].astype(F32)
        return total

    hz_s[...] = final_rows(1).astype(BF16)
    hcopy = send(hz_s, hzr_s, h_ss, h_rs, far_z)
    own_rows = final_rows(0)
    hcopy.wait_recv()
    own_rows += hzr_s[...].astype(F32)
    padded = jnp.concatenate((own_rows, jnp.zeros((256 - rows, HD), F32)), 0)
    turned = jnp.transpose(padded)
    kgw_s[...] = turned[:64, :rows]
    vgw_s[...] = turned[64:, :rows]
    outs[2].start()
    outs[3].start()
    for dz in (1, 2, 3):
        for i in range(4):
            z_copy(4 * ((zl + dz) % ZL) + i)[1].wait_send()
    for copy in sent:
        copy.wait_send()
    for copy in outs:
        copy.wait()


def copy_out(a, b, c, e, a_out, b_out, c_out, e_out, a_s, b_s, c_s, e_s, in_sems, out_sems):
    refs = [(b, b_s, b_out), (c, c_s, c_out), (e, e_s, e_out)]
    step = a_s.shape[0] // 4
    for i in range(4):
        at = pl.ds(i * step, step)
        refs.append((a.at[at], a_s.at[at], a_out.at[at]))
    loads = [
        pltpu.make_async_copy(src, mid, in_sems.at[i]) for i, (src, mid, dst) in enumerate(refs)
    ]
    stores = [
        pltpu.make_async_copy(mid, dst, out_sems.at[i]) for i, (src, mid, dst) in enumerate(refs)
    ]
    for copy in loads:
        copy.start()
    for load, store in zip(loads, stores):
        load.wait()
        store.start()
    for copy in stores:
        copy.wait()


def shards(
    queries, features, key_weight, value_weight, query_gain, key_gain, out_grad, tile_counts
):
    samples, own_rows, feature_width = features.shape
    tokens, q_width = queries.shape
    rows, column_half = key_weight.shape
    anyspec = pl.BlockSpec(memory_space=pl.ANY)
    dma = pltpu.SemaphoreType.DMA
    piece = (rows, HD)
    scratch = [
        pltpu.VMEM((tokens, q_width), BF16),
        pltpu.VMEM((tokens, q_width), BF16),
        pltpu.VMEM((tokens, q_width), BF16),
        pltpu.VMEM((own_rows, feature_width), BF16),
        pltpu.VMEM((16, 2) + piece, BF16),
        pltpu.VMEM((16, 2) + piece, BF16),
        pltpu.VMEM((HD, tokens * q_width // HD), BF16),
        pltpu.VMEM((tokens * q_width // HD, HD), BF16),
        pltpu.VMEM((ZL, X, 2) + piece, BF16),
    ]
    scratch += [pltpu.VMEM((HD, HD), BF16)] * 6
    scratch += [
        pltpu.VMEM((ZL, HD, HD), BF16),
        pltpu.VMEM((HD, HD), BF16),
        pltpu.VMEM((X, 2) + piece, BF16),
        pltpu.VMEM((16,) + piece, BF16),
        pltpu.VMEM((16,) + piece, BF16),
        pltpu.VMEM((14,) + piece, BF16),
        pltpu.VMEM((2,) + piece, BF16),
        pltpu.VMEM((2, 2) + piece, BF16),
        pltpu.VMEM(piece, BF16),
        pltpu.VMEM(piece, BF16),
        pltpu.VMEM((HD, HD), F32),
        pltpu.VMEM((HD, HD), F32),
        pltpu.VMEM((column_half, rows), BF16),
        pltpu.VMEM((column_half, rows), BF16),
        pltpu.VMEM((1, HD), F32),
        pltpu.VMEM((1, HD), F32),
        pltpu.VMEM((2 * rows, own_rows), BF16),
        pltpu.VMEM((column_half, rows), F32),
        pltpu.VMEM((column_half, rows), F32),
        dma((11,)),
        dma((2, 2, 4)), dma((2, 2, 4)), dma, dma, dma((16,)), dma((16,)), dma((2,)), dma((2,)),
        dma((8,)), dma((8,)), dma((14,)), dma((14,)), dma((6,)), dma((6,)),
        dma((16,)), dma((4, 4)), dma((3, 4)), dma((3, 4)), dma((3,)), dma((3,)), dma, dma,
    ]
    out_shape = (
        jax.ShapeDtypeStruct((tokens, q_width), BF16),
        jax.ShapeDtypeStruct((2 * rows, own_rows), BF16),
        jax.ShapeDtypeStruct((column_half, rows), F32),
        jax.ShapeDtypeStruct((column_half, rows), F32),
    )
    results = pl.pallas_call(
        kernel,
        out_shape=out_shape,
        in_specs=[pl.BlockSpec(memory_space=pltpu.SMEM)] + [anyspec] * 7,
        out_specs=(anyspec,) * 4,
        scratch_shapes=scratch,
        compiler_params=pltpu.CompilerParams(
            collective_id=0, has_side_effects=True, vmem_limit_bytes=62 * 1024 * 1024
        ),
        cost_estimate=pl.CostEstimate(
            flops=1600000000, bytes_accessed=8000000, transcendentals=500000
        ),
    )(
        tile_counts, queries, features.reshape(own_rows, feature_width), key_weight.T,
        value_weight.T, query_gain.reshape(1, HD), key_gain.reshape(1, HD), out_grad,
    )
    query_grad, feature_t, key_t, value_t = pl.pallas_call(
        copy_out,
        out_shape=out_shape,
        in_specs=[anyspec] * 4,
        out_specs=(anyspec,) * 4,
        scratch_shapes=[pltpu.VMEM(o.shape, o.dtype) for o in out_shape] + [dma((7,)), dma((7,))],
        compiler_params=pltpu.CompilerParams(vmem_limit_bytes=62 * 1024 * 1024),
        cost_estimate=pl.CostEstimate(flops=0, bytes_accessed=3000000, transcendentals=0),
    )(*results)
    return (query_grad, feature_t.T.reshape(samples, own_rows, 2 * rows), key_t.T, value_t.T)


def solution(mesh):
    placed = (
        P("dp", "tensor"),
        P("dp", None, None),
        P("dp", "tensor"),
        P("dp", "tensor"),
        P(),
        P(),
        P("dp", "tensor"),
        P("dp"),
    )
    return jax.shard_map(
        shards,
        mesh=mesh,
        in_specs=placed,
        out_specs=(
            P("dp", "tensor"),
            P("dp", None, "tensor"),
            P("dp", "tensor"),
            P("dp", "tensor"),
        ),
        check_vma=False,
    )
```

```python
import functools
import math

import jax
import jax.numpy as jnp
from jax import lax
from jax.experimental import pallas as pl
from jax.experimental.pallas import tpu as pltpu
from jax.sharding import PartitionSpec as P

TILE_ROWS = 32
EPS = 1e-05
HD = 128
Y, X, ZL = 8, 4, 4
CH = 160
HOPS = {(0, 0): 4, (0, 1): 3, (1, 0): 3, (1, 1): 4}
F32 = jnp.float32
BF16 = jnp.bfloat16
NT = (((1,), (1,)), ((), ()))
TN = (((0,), (0,)), ((), ()))


def dot(a, b, dims=(((1,), (0,)), ((), ()))):
    return lax.dot_general(a, b, dims, preferred_element_type=F32)


def kernel(
    tc_ref, q_hbm, feat_hbm, kwt_hbm, vwt_hbm, qg_hbm, kg_hbm, do_hbm,
    dq_hbm, ft_hbm, kgw_hbm, vgw_hbm,
    q_s, do_s, dq_s, feat_s, featT, wbuf, dsT, qn_s, w2_s, own_s, par_s, kbf_s, vbf_s, far_s,
    farr_s, g4_s, go_s, fterm, wterm, fx_s, yr_s, x1_s, x2_s, hz_s, hzr_s, vg_s, kg_s,
    kwt_s, vwt_s, qg_s, kg_in_s, ft_s, kgw_s, vgw_s,
    loc_sem, ag_ss, ag_rs, agz_ss, agz_rs, agc_ss, agc_rs, p_ss, p_rs,
    c_ss, c_rs, y_ss, y_rs, x_ss, x_rs, zf_ss, zf_rs, wc_ss, wc_rs, yp_ss, yp_rs, gz_ss, gz_rs, h_ss, h_rs,
):
    d = lax.axis_index("dp")
    t = lax.axis_index("tensor")
    y, zh, core = d // 4, (d // 2) % 2, d % 2
    zl, x = t // 4, t % 4
    low = (t % 2) == 0
    par = y % 2

    def at_y(step):
        return (((y + step + Y) % Y) * 4 + zh * 2 + core, t)

    right, left = at_y(1), at_y(-1)
    far_core = (d + 1 - 2 * core, t)
    far_z = (d + 2 - 4 * zh, t)
    y_pair = (d + 4 - 8 * par, t)
    partner = (d, t + 1 - 2 * (t % 2))
    x_right = (d, zl * 4 + (x + 1) % X)
    x_left = (d, zl * 4 + (x + X - 1) % X)
    z_to = [(d, ((zl + k) % ZL) * 4 + x) for k in (1, 2, 3)]

    barrier = pltpu.get_barrier_semaphore()
    peers = [right, left, far_core, far_z, x_right, x_left] + z_to
    for peer in peers:
        pl.semaphore_signal(barrier, inc=1, device_id=peer, device_id_type=pl.DeviceIdType.MESH)

    tokens = q_s.shape[0]
    heads = q_s.shape[1] // HD
    width = CH * heads
    fetched = (
        (kwt_hbm, kwt_s), (vwt_hbm, vwt_s), (feat_hbm, feat_s), (q_hbm, q_s), (do_hbm, do_s),
        (qg_hbm, qg_s), (kg_hbm, kg_in_s),
    )
    copies = [
        pltpu.make_async_copy(src, dst, loc_sem.at[i]) for i, (src, dst) in enumerate(fetched)
    ]
    for copy in copies:
        copy.start()

    sent = []

    def send(src, dst, ssem, rsem, dev):
        copy = pltpu.make_async_remote_copy(
            src_ref=src, dst_ref=dst, send_sem=ssem, recv_sem=rsem,
            device_id=dev, device_id_type=pl.DeviceIdType.MESH,
        )
        copy.start()
        sent.append(copy)
        return copy

    copies[0].wait()
    copies[1].wait()
    shard = jnp.concatenate((kwt_s[...], vwt_s[...]), 0).astype(F32)
    rows = shard.shape[1]
    shard = jnp.concatenate((shard, jnp.zeros((HD, 256 - rows), F32)), 1)
    mine = 2 * y + zh
    wbuf[mine, core] = jnp.transpose(shard)[:rows].astype(BF16)

    pl.semaphore_wait(barrier, len(peers))

    def c_of(step, stream):
        zz = zh if stream == 0 else 1 - zh
        return 2 * ((y + step + Y) % Y) + zz

    def gather_send(stream, way, hop):
        c = c_of((1 - hop) if way == 0 else (hop - 1), stream)
        ref = wbuf.at[c, core]
        return send(ref, ref, ag_ss.at[stream, way, hop - 1], ag_rs.at[stream, way, hop - 1],
                    right if way == 0 else left)

    across = []

    def core_send(c):
        ref = wbuf.at[c, core]
        i = len(across)
        across.append(send(ref, ref, agc_ss.at[i], agc_rs.at[i], far_core))

    def z_copy(c):
        dest = c // ZL
        return dest, pltpu.make_async_remote_copy(
            src_ref=wbuf.at[c, core], dst_ref=w2_s.at[zl, c % ZL, core],
            send_sem=zf_ss.at[c], recv_sem=zf_rs.at[zl, c % ZL],
            device_id=(d, dest * X + x), device_id_type=pl.DeviceIdType.MESH,
        )

    def z_send(c):
        dest, copy = z_copy(c)

        @pl.when((dest != zl) & (c % 2 == par))
        def _():
            copy.start()

    ag = {}
    for way in (0, 1):
        ag[0, way, 1] = gather_send(0, way, 1)
    ref = wbuf.at[mine, core]
    zcopy = send(ref, ref, agz_ss, agz_rs, far_z)
    core_send(mine)
    z_send(mine)

    copies[2].wait()
    copies[3].wait()
    copies[5].wait()
    copies[6].wait()
    inverse = 1.0 / math.sqrt(HD)
    qg = qg_s[...]
    kg = kg_in_s[...]

    shared = []

    def transpose_part(part):
        cols = feat_s[:, part * 1920:(part + 1) * 1920]
        group = pl.ds(part * 4, 4)
        featT[group] = jnp.transpose(cols).reshape(4, 2, 240, HD)
        shared.append(send(
            featT.at[group, 1 - core], fx_s.at[group], c_ss.at[part], c_rs.at[part], far_core))

    def stack(ref, chunk):
        at = slice(chunk * CH, (chunk + 1) * CH)
        return jnp.concatenate([ref[at, h * HD:(h + 1) * HD] for h in range(heads)], 0)

    def query_norm(chunk):
        xq = stack(q_s, chunk).astype(F32)
        r = lax.rsqrt(jnp.mean(xq * xq, -1, keepdims=True) + EPS)
        qn_s[chunk * width:(chunk + 1) * width, :] = (xq * r * qg).astype(BF16)

    def gather_step(stream, hop):
        for way in (0, 1):
            if hop > HOPS[stream, way]:
                continue
            ag[stream, way, hop].wait_recv()
            if hop < HOPS[stream, way]:
                ag[stream, way, hop + 1] = gather_send(stream, way, hop + 1)
            c = c_of(-hop if way == 0 else hop, stream)
            core_send(c)
            z_send(c)

    arrived = 0

    def project(parts):
        total = jnp.zeros((HD, HD), F32)
        for part in parts:
            at = (y // 2 + part) % 4
            cols = feat_s[:, pl.ds(pl.multiple_of(at * 1920, 1920), 1920)]
            total += dot(cols, wbuf[pl.ds(4 * at, 4)].reshape(1920, HD))
        return total

    proj = jnp.zeros((HD, HD), F32)
    for hop in range(1, 6):
        if hop <= 4:
            gather_step(0, hop)
            transpose_part(hop - 1)
        if hop == 1:
            zcopy.wait_recv()
            for way in (0, 1):
                ag[1, way, 1] = gather_send(1, way, 1)
            core_send(c_of(0, 1))
            z_send(c_of(0, 1))
        else:
            gather_step(1, hop - 1)
        if hop <= 4:
            query_norm(hop - 1)
        if hop >= 3:
            until, parts = {3: (8, (0,)), 4: (15, (1, 3)), 5: (16, (2,))}[hop]
            for copy in across[arrived:until]:
                copy.wait_recv()
            arrived = until
            proj += project(parts)
    own_s[...] = proj.astype(BF16)
    pcopy = send(own_s, par_s, p_ss.at[0], p_rs.at[0], partner)
    copies[4].wait()
    query_norm(4)
    query_norm(5)
    lane = lax.broadcasted_iota(jnp.int32, (HD, HD), 1)
    half = lane < 64
    lowf = jnp.where(low, 1.0, 0.0).astype(F32)
    own = own_s[...].astype(F32)
    pcopy.wait_recv()
    other = par_s[...].astype(F32)
    first = own * lowf + other * (1.0 - lowf)
    second = other * lowf + own * (1.0 - lowf)
    keys = jnp.where(half, first, pltpu.roll(second, 64, 1))
    values = jnp.where(half, pltpu.roll(first, 64, 1), second)
    k_scale = lax.rsqrt(jnp.mean(keys * keys, -1, keepdims=True) + EPS)
    kbf_s[...] = (keys * k_scale * kg).astype(BF16)
    vbf_s[...] = values.astype(BF16)
    live = (
        lax.broadcasted_iota(jnp.int32, (HD, 1), 0) < tc_ref[0] * TILE_ROWS
    ).astype(F32)
    vg_s[...] = jnp.zeros_like(vg_s)
    kg_s[...] = jnp.zeros_like(kg_s)

    def attend(chunk, carry):
        at = pl.ds(pl.multiple_of(chunk * CH, CH), CH)
        wide = pl.ds(pl.multiple_of(chunk * width, width), width)
        qn = qn_s[wide, :]
        do = jnp.concatenate([do_s[at, h * HD:(h + 1) * HD] for h in range(heads)], 0)
        e = jnp.exp(dot(kbf_s[...], qn, NT) * inverse) * live
        p = e * (1.0 / jnp.sum(e, 0, keepdims=True))
        pb = p.astype(BF16)
        vg_s[...] += dot(pb, do)
        pg = dot(vbf_s[...], do, NT)
        delta = jnp.sum(pb.astype(F32) * pg, 0, keepdims=True)
        ds = (p * (pg - delta)).astype(BF16)
        dsT[:, wide] = ds
        kg_s[...] += dot(ds, qn)
        return carry

    swaps = []
    wc = []
    z_from = [(dz, j, (zl + dz) % ZL) for dz in (1, 3, 2) for j in (0, 1)]

    def w2_send(src, i, dev, ssem, rsem):
        ref = w2_s.at[src, i, core]
        return send(ref, ref, ssem, rsem, dev)

    def swap_pairs():
        for dz, j, src in z_from:
            i = 2 * j + par
            ref = w2_s.at[src, i, core]
            pltpu.make_async_remote_copy(
                src_ref=ref, dst_ref=ref, send_sem=zf_ss.at[0], recv_sem=zf_rs.at[src, i],
                device_id=far_core, device_id_type=pl.DeviceIdType.MESH,
            ).wait_recv()
            swaps.append(w2_send(src, i, y_pair, yp_ss.at[dz - 1, j], yp_rs.at[dz - 1, j]))
            wc.append(w2_send(src, i, far_core, wc_ss.at[dz - 1, j], wc_rs.at[dz - 1, j]))

    def swapped_across():
        for (dz, j, src), copy in zip(z_from, swaps):
            copy.wait_recv()
            wc.append(w2_send(
                src, 2 * j + 1 - par, far_core, wc_ss.at[dz - 1, 2 + j], wc_rs.at[dz - 1, 2 + j]))

    lax.fori_loop(0, 2, attend, 0, unroll=2)
    swap_pairs()
    lax.fori_loop(2, tokens // CH, attend, 0, unroll=2)

    weighted = kg_s[...] * (inverse * kg)
    key_grad = k_scale * weighted - keys * (
        k_scale * k_scale * k_scale * jnp.mean(weighted * keys, -1, keepdims=True)
    )
    value_grad = vg_s[...]
    low_part = jnp.where(half, key_grad, pltpu.roll(value_grad, 64, 1))
    high_part = jnp.where(half, pltpu.roll(key_grad, 64, 1), value_grad)
    far_s[...] = (high_part * lowf + low_part * (1.0 - lowf)).astype(BF16)
    own_grad = low_part * lowf + high_part * (1.0 - lowf)
    fcopy = send(far_s, farr_s, p_ss.at[1], p_rs.at[1], partner)

    def query_back(chunk):
        xq = stack(q_s, chunk).astype(F32)
        r = lax.rsqrt(jnp.mean(xq * xq, -1, keepdims=True) + EPS)
        ds = dsT[:, chunk * width:(chunk + 1) * width]
        u = dot(ds, kbf_s[...], TN) * (inverse * qg)
        m = jnp.mean(u * xq, -1, keepdims=True)
        back = (r * u - xq * (r * r * r * m)).astype(BF16)
        for h in range(heads):
            dq_s[chunk * CH:(chunk + 1) * CH, h * HD:(h + 1) * HD] = back[h * CH:(h + 1) * CH]

    query_back(0)
    fcopy.wait_recv()
    g4_s[zl] = (own_grad + farr_s[...].astype(F32)).astype(BF16)
    g = g4_s[zl]
    gcopy = send(g4_s.at[zl], go_s, c_ss.at[4], c_rs.at[4], far_core)
    gz = []
    for k in (1, 2, 0):
        gz.append(send(g4_s.at[zl], g4_s.at[zl], gz_ss.at[k], gz_rs.at[k], z_to[k]))

    query_back(1)
    gcopy.wait_recv()
    go = go_s[...]
    for copy in shared:
        copy.wait_recv()

    def weight_term(step):
        for stream in (1, 0):
            c = c_of(step, stream)
            wterm[c] = (dot(featT[c, core], g) + dot(fx_s[c], go)).astype(BF16)

    def feature_term(xx):
        total = dot(wbuf[zl * X + xx].reshape(480, HD), g, NT)
        for dz in (1, 2, 3):
            src = (zl + dz) % ZL
            total += dot(w2_s[src, xx].reshape(480, HD), g4_s[src], NT)
        return total

    x2, xp, xm = (x + 2) % X, (x + 1) % X, (x + 3) % X
    xs = {}

    def x_send(name, slot, src, dst, dev):
        xs[name] = send(src, dst, x_ss.at[slot], x_rs.at[slot], dev)

    def x_start():
        for copy in gz + wc:
            copy.wait_recv()
        for xx in (x2, xp, xm):
            fterm[xx] = feature_term(xx).astype(BF16).reshape(2, 240, HD)
            if xx is x2:
                x_send("r1", 0, fterm.at[x2, 0], x1_s.at[0], x_right)
                x_send("l1", 1, fterm.at[x2, 1], x1_s.at[1], x_left)
            elif xx is xp:
                x_send("r2", 2, fterm.at[xp, 1], x2_s.at[0, 1], x_right)
            else:
                x_send("l2", 3, fterm.at[xm, 0], x2_s.at[1, 0], x_left)

    slots = {}
    for key in ((0, 0), (1, 1), (0, 1), (1, 0)):
        for hop in range(1, HOPS[key] + 1):
            slots[key + (hop,)] = len(slots)
    ys = {}

    def ring_send(stream, way, hop):
        step = HOPS[stream, way] - hop + 1
        c = c_of(step if way == 0 else -step, stream)
        slot = slots[stream, way, hop]
        if hop > 1:
            ys[stream, way, hop - 1].wait_recv()
            last = slots[stream, way, hop - 1]
            wterm[c] = (wterm[c].astype(F32) + yr_s[last].astype(F32)).astype(BF16)
        ys[stream, way, hop] = send(
            wterm.at[c], yr_s.at[slot], y_ss.at[slot], y_rs.at[slot],
            right if way == 0 else left,
        )

    def x_relay():
        for name, way, xx in (("r", 0, xp), ("l", 1, xm)):
            xs[name + "1"].wait_recv()
            fterm[xx, way] = (
                fterm[xx, way].astype(F32) + x1_s[way].astype(F32)).astype(BF16)
            x_send(name + "3", 4 + way, fterm.at[xx, way], x2_s.at[way, way],
                   x_right if way == 0 else x_left)

    def ring_hop(hop):
        for stream, way in ((1, 1), (1, 0), (0, 0), (0, 1)):
            if hop <= HOPS[stream, way]:
                ring_send(stream, way, hop)

    weight_term(4)
    ring_send(1, 1, 1)
    ring_send(0, 0, 1)
    weight_term(3)
    ring_send(1, 0, 1)
    weight_term(5)
    ring_send(0, 1, 1)
    weight_term(2)
    weight_term(6)
    weight_term(1)
    weight_term(7)
    weight_term(0)
    ring_hop(2)
    swapped_across()
    query_back(2)
    ring_hop(3)
    x_start()
    own_term = feature_term(x)
    ring_hop(4)
    x_relay()
    query_back(3)
    for name in ("r2", "l2", "r3", "l3"):
        xs[name].wait_recv()
    own_term += x2_s[0].reshape(480, HD).astype(F32) + x2_s[1].reshape(480, HD).astype(F32)
    ft_s[...] = own_term.astype(BF16)
    query_back(4)
    query_back(5)
    outs = [
        pltpu.make_async_copy(dq_s, dq_hbm, loc_sem.at[7]),
        pltpu.make_async_copy(ft_s, ft_hbm, loc_sem.at[8]),
        pltpu.make_async_copy(kgw_s, kgw_hbm, loc_sem.at[9]),
        pltpu.make_async_copy(vgw_s, vgw_hbm, loc_sem.at[10]),
    ]
    outs[0].start()
    outs[1].start()

    def final_rows(stream):
        c = c_of(0, stream)
        total = wterm[c].astype(F32)
        for way in (0, 1):
            hop = HOPS[stream, way]
            ys[stream, way, hop].wait_recv()
            total += yr_s[slots[stream, way, hop]].astype(F32)
        return total

    hz_s[...] = final_rows(1).astype(BF16)
    hcopy = send(hz_s, hzr_s, h_ss, h_rs, far_z)
    own_rows = final_rows(0)
    hcopy.wait_recv()
    own_rows += hzr_s[...].astype(F32)
    padded = jnp.concatenate((own_rows, jnp.zeros((256 - rows, HD), F32)), 0)
    turned = jnp.transpose(padded)
    kgw_s[...] = turned[:64, :rows]
    vgw_s[...] = turned[64:, :rows]
    outs[2].start()
    outs[3].start()
    for dz, j, dest in z_from:
        z_copy(4 * dest + 2 * j + par)[1].wait_send()
    for copy in sent:
        copy.wait_send()
    for copy in outs:
        copy.wait()


def copy_out(a, b, c, e, a_out, b_out, c_out, e_out, a_s, b_s, c_s, e_s, in_sems, out_sems):
    refs = [(b, b_s, b_out), (c, c_s, c_out), (e, e_s, e_out)]
    step = a_s.shape[0] // 4
    for i in range(4):
        at = pl.ds(i * step, step)
        refs.append((a.at[at], a_s.at[at], a_out.at[at]))
    loads = [
        pltpu.make_async_copy(src, mid, in_sems.at[i]) for i, (src, mid, dst) in enumerate(refs)
    ]
    stores = [
        pltpu.make_async_copy(mid, dst, out_sems.at[i]) for i, (src, mid, dst) in enumerate(refs)
    ]
    for copy in loads:
        copy.start()
    for load, store in zip(loads, stores):
        load.wait()
        store.start()
    for copy in stores:
        copy.wait()


def shards(
    queries, features, key_weight, value_weight, query_gain, key_gain, out_grad, tile_counts
):
    samples, own_rows, feature_width = features.shape
    tokens, q_width = queries.shape
    rows, column_half = key_weight.shape
    anyspec = pl.BlockSpec(memory_space=pl.ANY)
    dma = pltpu.SemaphoreType.DMA
    piece = (rows, HD)
    scratch = [
        pltpu.VMEM((tokens, q_width), BF16),
        pltpu.VMEM((tokens, q_width), BF16),
        pltpu.VMEM((tokens, q_width), BF16),
        pltpu.VMEM((own_rows, feature_width), BF16),
        pltpu.VMEM((16, 2) + piece, BF16),
        pltpu.VMEM((16, 2) + piece, BF16),
        pltpu.VMEM((HD, tokens * q_width // HD), BF16),
        pltpu.VMEM((tokens * q_width // HD, HD), BF16),
        pltpu.VMEM((ZL, X, 2) + piece, BF16),
    ]
    scratch += [pltpu.VMEM((HD, HD), BF16)] * 6
    scratch += [
        pltpu.VMEM((ZL, HD, HD), BF16),
        pltpu.VMEM((HD, HD), BF16),
        pltpu.VMEM((X, 2) + piece, BF16),
        pltpu.VMEM((16,) + piece, BF16),
        pltpu.VMEM((16,) + piece, BF16),
        pltpu.VMEM((14,) + piece, BF16),
        pltpu.VMEM((2,) + piece, BF16),
        pltpu.VMEM((2, 2) + piece, BF16),
        pltpu.VMEM(piece, BF16),
        pltpu.VMEM(piece, BF16),
        pltpu.VMEM((HD, HD), F32),
        pltpu.VMEM((HD, HD), F32),
        pltpu.VMEM((column_half, rows), BF16),
        pltpu.VMEM((column_half, rows), BF16),
        pltpu.VMEM((1, HD), F32),
        pltpu.VMEM((1, HD), F32),
        pltpu.VMEM((2 * rows, own_rows), BF16),
        pltpu.VMEM((column_half, rows), F32),
        pltpu.VMEM((column_half, rows), F32),
        dma((11,)),
        dma((2, 2, 4)), dma((2, 2, 4)), dma, dma, dma((16,)), dma((16,)), dma((2,)), dma((2,)),
        dma((8,)), dma((8,)), dma((14,)), dma((14,)), dma((6,)), dma((6,)),
        dma((16,)), dma((4, 4)), dma((3, 4)), dma((3, 4)), dma((3, 2)), dma((3, 2)), dma((3,)), dma((3,)), dma, dma,
    ]
    out_shape = (
        jax.ShapeDtypeStruct((tokens, q_width), BF16),
        jax.ShapeDtypeStruct((2 * rows, own_rows), BF16),
        jax.ShapeDtypeStruct((column_half, rows), F32),
        jax.ShapeDtypeStruct((column_half, rows), F32),
    )
    results = pl.pallas_call(
        kernel,
        out_shape=out_shape,
        in_specs=[pl.BlockSpec(memory_space=pltpu.SMEM)] + [anyspec] * 7,
        out_specs=(anyspec,) * 4,
        scratch_shapes=scratch,
        compiler_params=pltpu.CompilerParams(
            collective_id=0, has_side_effects=True, vmem_limit_bytes=62 * 1024 * 1024
        ),
        cost_estimate=pl.CostEstimate(
            flops=1600000000, bytes_accessed=8000000, transcendentals=500000
        ),
    )(
        tile_counts, queries, features.reshape(own_rows, feature_width), key_weight.T,
        value_weight.T, query_gain.reshape(1, HD), key_gain.reshape(1, HD), out_grad,
    )
    query_grad, feature_t, key_t, value_t = pl.pallas_call(
        copy_out,
        out_shape=out_shape,
        in_specs=[anyspec] * 4,
        out_specs=(anyspec,) * 4,
        scratch_shapes=[pltpu.VMEM(o.shape, o.dtype) for o in out_shape] + [dma((7,)), dma((7,))],
        compiler_params=pltpu.CompilerParams(vmem_limit_bytes=62 * 1024 * 1024),
        cost_estimate=pl.CostEstimate(flops=0, bytes_accessed=3000000, transcendentals=0),
    )(*results)
    return (query_grad, feature_t.T.reshape(samples, own_rows, 2 * rows), key_t.T, value_t.T)


def solution(mesh):
    placed = (
        P("dp", "tensor"),
        P("dp", None, None),
        P("dp", "tensor"),
        P("dp", "tensor"),
        P(),
        P(),
        P("dp", "tensor"),
        P("dp"),
    )
    return jax.shard_map(
        shards,
        mesh=mesh,
        in_specs=placed,
        out_specs=(
            P("dp", "tensor"),
            P("dp", None, "tensor"),
            P("dp", "tensor"),
            P("dp", "tensor"),
        ),
        check_vma=False,
    )
```

```python
import functools
import math

import jax
import jax.numpy as jnp
from jax import lax
from jax.experimental import pallas as pl
from jax.experimental.pallas import tpu as pltpu
from jax.sharding import PartitionSpec as P

TILE_ROWS = 32
EPS = 1e-05
HD = 128
Y, X, ZL = 8, 4, 4
CH = 160
HOPS = {(0, 0): 4, (0, 1): 3, (1, 0): 3, (1, 1): 4}
PIECES = ((0, 240), (0, 128), (128, 112))
F32 = jnp.float32
BF16 = jnp.bfloat16
NT = (((1,), (1,)), ((), ()))
TN = (((0,), (0,)), ((), ()))


def dot(a, b, dims=(((1,), (0,)), ((), ()))):
    return lax.dot_general(a, b, dims, preferred_element_type=F32)


def kernel(
    tc_ref, q_hbm, feat_hbm, kwt_hbm, vwt_hbm, qg_hbm, kg_hbm, do_hbm,
    dq_hbm, ft_hbm, kgw_hbm, vgw_hbm,
    q_s, do_s, dq_s, feat_s, featT, wbuf, dsT, qn_s, w2_s, own_s, par_s, kbf_s, vbf_s, far_s,
    farr_s, g4_s, own_grad_s, other_grad_s, fterm, wterm, fx_s, yr_s, x1_s, x2_s, hz_s, hzr_s, vg_s, kg_s,
    kwt_s, vwt_s, qg_s, kg_in_s, ft_s, kgw_s, vgw_s,
    loc_sem, ag_ss, ag_rs, agz_ss, agz_rs, agc_ss, agc_rs, p_ss, p_rs,
    c_ss, c_rs, y_ss, y_rs, x_ss, x_rs, zf_ss, zf_rs, wc_ss, wc_rs, gz_ss, gz_rs, h_ss, h_rs,
):
    d = lax.axis_index("dp")
    t = lax.axis_index("tensor")
    y, zh, core = d // 4, (d // 2) % 2, d % 2
    zl, x = t // 4, t % 4
    low = (t % 2) == 0

    def at_y(step):
        return (((y + step + Y) % Y) * 4 + zh * 2 + core, t)

    right, left = at_y(1), at_y(-1)
    far_core = (d + 1 - 2 * core, t)
    far_z = (d + 2 - 4 * zh, t)
    partner = (d, t + 1 - 2 * (t % 2))
    diagonal = (d + 1 - 2 * core, t + 1 - 2 * (t % 2))
    x_right = (d, zl * 4 + (x + 1) % X)
    x_left = (d, zl * 4 + (x + X - 1) % X)
    z_to = [(d, ((zl + k) % ZL) * 4 + x) for k in (1, 2, 3)]

    barrier = pltpu.get_barrier_semaphore()
    peers = [right, left, far_core, far_z, x_right, x_left, diagonal] + z_to
    for peer in peers:
        pl.semaphore_signal(barrier, inc=1, device_id=peer, device_id_type=pl.DeviceIdType.MESH)

    tokens = q_s.shape[0]
    heads = q_s.shape[1] // HD
    width = CH * heads
    chunks = tokens // CH
    fetched = (
        (kwt_hbm, kwt_s), (vwt_hbm, vwt_s), (feat_hbm, feat_s), (q_hbm, q_s), (do_hbm, do_s),
        (qg_hbm, qg_s), (kg_hbm, kg_in_s),
    )
    copies = [
        pltpu.make_async_copy(src, dst, loc_sem.at[i]) for i, (src, dst) in enumerate(fetched)
    ]
    for copy in copies:
        copy.start()

    sent = []

    def drain(later=()):
        kept = [copy for copy in sent if any(copy is one for one in later)]
        for copy in sent:
            if not any(copy is one for one in later):
                copy.wait_send()
        sent[:] = kept

    def send(src, dst, ssem, rsem, dev):
        copy = pltpu.make_async_remote_copy(
            src_ref=src, dst_ref=dst, send_sem=ssem, recv_sem=rsem,
            device_id=dev, device_id_type=pl.DeviceIdType.MESH,
        )
        copy.start()
        sent.append(copy)
        return copy

    copies[0].wait()
    copies[1].wait()
    shard = jnp.concatenate((kwt_s[...], vwt_s[...]), 0).astype(F32)
    rows = shard.shape[1]
    shard = jnp.concatenate((shard, jnp.zeros((HD, 256 - rows), F32)), 1)
    mine = 2 * y + zh
    wbuf[mine, core] = jnp.transpose(shard)[:rows].astype(BF16)

    pl.semaphore_wait(barrier, len(peers))

    def c_of(step, stream):
        zz = zh if stream == 0 else 1 - zh
        return 2 * ((y + step + Y) % Y) + zz

    def piece_of(c, part):
        return wbuf.at[c, core, pl.ds(*PIECES[part])]

    def gather_send(part, way, hop):
        c = c_of((1 - hop) if way == 0 else (hop - 1), min(part, 1))
        ref = piece_of(c, part)
        return send(ref, ref, ag_ss.at[part, way, hop - 1], ag_rs.at[part, way, hop - 1],
                    right if way == 0 else left)

    across = []

    def core_send(c, part):
        ref = piece_of(c, part)
        i = len(across)
        across.append(send(ref, ref, agc_ss.at[i], agc_rs.at[i], far_core))

    def z_copy(c):
        dest = c // ZL
        return dest, pltpu.make_async_remote_copy(
            src_ref=wbuf.at[c, core], dst_ref=w2_s.at[zl, c % ZL, core],
            send_sem=zf_ss.at[c], recv_sem=zf_rs.at[zl, c % ZL],
            device_id=(d, dest * X + x), device_id_type=pl.DeviceIdType.MESH,
        )

    def z_send(c):
        dest, copy = z_copy(c)

        @pl.when(dest != zl)
        def _():
            copy.start()

    ag = {}
    for way in (0, 1):
        ag[0, way, 1] = gather_send(0, way, 1)
    zcopies = {}
    for part in (1, 2):
        ref = piece_of(mine, part)
        zcopies[part] = send(ref, ref, agz_ss.at[part - 1], agz_rs.at[part - 1], far_z)
    core_send(mine, 0)
    z_send(mine)

    copies[2].wait()
    copies[3].wait()
    copies[5].wait()
    copies[6].wait()
    inverse = 1.0 / math.sqrt(HD)
    qg = qg_s[...]
    kg = kg_in_s[...]

    def shared_copy(part):
        group = pl.ds(part * 4, 4)
        return pltpu.make_async_remote_copy(
            src_ref=featT.at[group, 1 - core], dst_ref=fx_s.at[group],
            send_sem=c_ss.at[part], recv_sem=c_rs.at[part],
            device_id=far_core, device_id_type=pl.DeviceIdType.MESH,
        )

    def transpose_part(part, carry):
        cols = feat_s[:, pl.ds(pl.multiple_of(part * 1920, 1920), 1920)]
        featT[pl.ds(part * 4, 4)] = jnp.transpose(cols).reshape(4, 2, 240, HD)
        shared_copy(part).start()
        return carry

    def stack(ref, chunk):
        at = pl.ds(pl.multiple_of(chunk * CH, CH), CH)
        return jnp.concatenate([ref[at, h * HD:(h + 1) * HD] for h in range(heads)], 0)

    def wide(chunk):
        return pl.ds(pl.multiple_of(chunk * width, width), width)

    def query_norm(chunk, carry):
        xq = stack(q_s, chunk).astype(F32)
        r = lax.rsqrt(jnp.mean(xq * xq, -1, keepdims=True) + EPS)
        qn_s[wide(chunk), :] = (xq * r * qg).astype(BF16)
        return carry

    def gather_step(part, hop):
        for way in (1, 0):
            if hop > HOPS[min(part, 1), way]:
                continue
            ag[part, way, hop].wait_recv()
            if hop < HOPS[min(part, 1), way]:
                ag[part, way, hop + 1] = gather_send(part, way, hop + 1)
            c = c_of(-hop if way == 0 else hop, min(part, 1))
            core_send(c, part)
            if part != 1:
                z_send(c)

    arrived = 0

    def project(part, total):
        at = (y // 2 + part) % 4
        cols = feat_s[:, pl.ds(pl.multiple_of(at * 1920, 1920), 1920)]
        return total + dot(cols, wbuf[pl.ds(4 * at, 4)].reshape(1920, HD))

    proj = jnp.zeros((HD, HD), F32)
    lax.fori_loop(0, 4, transpose_part, 0)
    for hop in range(1, 6):
        if hop <= 4:
            gather_step(0, hop)
        if hop == 1:
            for part in (1, 2):
                zcopies[part].wait_recv()
                for way in (1, 0):
                    ag[part, way, 1] = gather_send(part, way, 1)
                core_send(c_of(0, 1), part)
            z_send(c_of(0, 1))
            lax.fori_loop(0, chunks, query_norm, 0)
        else:
            gather_step(1, hop - 1)
            gather_step(2, hop - 1)
        if hop >= 4:
            first_part, end_part = {4: (3, 6), 5: (6, 7)}[hop]
            for copy in across[arrived:]:
                copy.wait_recv()
            arrived = len(across)
            proj = lax.fori_loop(first_part, end_part, project, proj)
    own_s[...] = proj.astype(BF16)
    pcopy = send(own_s, par_s, p_ss.at[0], p_rs.at[0], partner)
    copies[4].wait()
    lane = lax.broadcasted_iota(jnp.int32, (HD, HD), 1)
    half = lane < 64
    lowf = jnp.where(low, 1.0, 0.0).astype(F32)
    own = own_s[...].astype(F32)
    pcopy.wait_recv()
    other = par_s[...].astype(F32)
    first = own * lowf + other * (1.0 - lowf)
    second = other * lowf + own * (1.0 - lowf)
    keys = jnp.where(half, first, pltpu.roll(second, 64, 1))
    values = jnp.where(half, pltpu.roll(first, 64, 1), second)
    k_scale = lax.rsqrt(jnp.mean(keys * keys, -1, keepdims=True) + EPS)
    kbf_s[...] = (keys * k_scale * kg).astype(BF16)
    vbf_s[...] = values.astype(BF16)
    live = (
        lax.broadcasted_iota(jnp.int32, (HD, 1), 0) < tc_ref[0] * TILE_ROWS
    ).astype(F32)
    vg_s[...] = jnp.zeros_like(vg_s)
    kg_s[...] = jnp.zeros_like(kg_s)

    def attend(chunk, carry):
        qn = qn_s[wide(chunk), :]
        do = stack(do_s, chunk)
        e = jnp.exp(dot(kbf_s[...], qn, NT) * inverse) * live
        p = e * (1.0 / jnp.sum(e, 0, keepdims=True))
        pb = p.astype(BF16)
        vg_s[...] += dot(pb, do)
        pg = dot(vbf_s[...], do, NT)
        delta = jnp.sum(pb.astype(F32) * pg, 0, keepdims=True)
        ds = (p * (pg - delta)).astype(BF16)
        dsT[:, wide(chunk)] = ds
        kg_s[...] += dot(ds, qn)
        return carry

    lax.fori_loop(0, chunks, attend, 0, unroll=2)

    weighted = kg_s[...] * (inverse * kg)
    key_grad = k_scale * weighted - keys * (
        k_scale * k_scale * k_scale * jnp.mean(weighted * keys, -1, keepdims=True)
    )
    value_grad = vg_s[...]
    low_part = jnp.where(half, key_grad, pltpu.roll(value_grad, 64, 1))
    high_part = jnp.where(half, pltpu.roll(key_grad, 64, 1), value_grad)
    own_grad_s[...] = low_part * lowf + high_part * (1.0 - lowf)
    far_s[...] = (high_part * lowf + low_part * (1.0 - lowf)).astype(BF16)
    fcopy = send(far_s, farr_s.at[0], p_ss.at[1], p_rs.at[1], partner)
    ocopy = send(own_grad_s, other_grad_s, c_ss.at[4], c_rs.at[4], far_core)
    dcopy = send(far_s, farr_s.at[1], p_ss.at[2], p_rs.at[2], diagonal)

    def query_back(chunk, carry):
        xq = stack(q_s, chunk).astype(F32)
        r = lax.rsqrt(jnp.mean(xq * xq, -1, keepdims=True) + EPS)
        u = dot(dsT[:, wide(chunk)], kbf_s[...], TN) * (inverse * qg)
        m = jnp.mean(u * xq, -1, keepdims=True)
        back = (r * u - xq * (r * r * r * m)).astype(BF16)
        at = pl.ds(pl.multiple_of(chunk * CH, CH), CH)
        for h in range(heads):
            dq_s[at, h * HD:(h + 1) * HD] = back[h * CH:(h + 1) * CH]
        return carry

    drain((fcopy, ocopy, dcopy))
    lax.fori_loop(0, 3, query_back, 0)
    for part in range(4):
        shared_copy(part).wait_send()
    fcopy.wait_recv()
    g4_s[zl] = (own_grad_s[...] + farr_s[0].astype(F32)).astype(BF16)
    g = g4_s[zl]
    gz = []
    for k in (1, 2, 0):
        gz.append(send(g4_s.at[zl], g4_s.at[zl], gz_ss.at[k], gz_rs.at[k], z_to[k]))

    ocopy.wait_recv()
    dcopy.wait_recv()
    go = (other_grad_s[...] + farr_s[1].astype(F32)).astype(BF16)
    for part in range(4):
        shared_copy(part).wait_recv()

    def weight_term(step):
        for stream in (1, 0):
            c = c_of(step, stream)
            wterm[c] = (dot(featT[c, core], g) + dot(fx_s[c], go)).astype(BF16)

    def feature_term(xx):
        total = dot(wbuf[zl * X + xx].reshape(480, HD), g, NT)
        for dz in (1, 2, 3):
            src = (zl + dz) % ZL
            total += dot(w2_s[src, xx].reshape(480, HD), g4_s[src], NT)
        return total

    x2, xp, xm = (x + 2) % X, (x + 1) % X, (x + 3) % X
    xs = {}

    def x_send(name, slot, src, dst, dev):
        xs[name] = send(src, dst, x_ss.at[slot], x_rs.at[slot], dev)

    def x_start():
        for copy in gz + wc:
            copy.wait_recv()
        for xx in (x2, xp, xm):
            fterm[xx] = feature_term(xx).astype(BF16).reshape(2, 240, HD)
            if xx is x2:
                x_send("r1", 0, fterm.at[x2, 0], x1_s.at[0], x_right)
                x_send("l1", 1, fterm.at[x2, 1], x1_s.at[1], x_left)
            elif xx is xp:
                x_send("r2", 2, fterm.at[xp, 1], x2_s.at[0, 1], x_right)
            else:
                x_send("l2", 3, fterm.at[xm, 0], x2_s.at[1, 0], x_left)

    wc = []

    def w2_across():
        for dz in (1, 3, 2):
            src = (zl + dz) % ZL
            for i in range(4):
                ref = w2_s.at[src, i, core]
                pltpu.make_async_remote_copy(
                    src_ref=ref, dst_ref=ref, send_sem=zf_ss.at[0], recv_sem=zf_rs.at[src, i],
                    device_id=far_core, device_id_type=pl.DeviceIdType.MESH,
                ).wait_recv()
                wc.append(send(ref, ref, wc_ss.at[dz - 1, i], wc_rs.at[dz - 1, i], far_core))

    slots = {}
    for key in ((0, 0), (1, 1), (0, 1), (1, 0)):
        for hop in range(1, HOPS[key] + 1):
            slots[key + (hop,)] = len(slots)
    ys = {}

    def ring_send(stream, way, hop):
        step = HOPS[stream, way] - hop + 1
        c = c_of(step if way == 0 else -step, stream)
        slot = slots[stream, way, hop]
        if hop > 1:
            ys[stream, way, hop - 1].wait_recv()
            last = slots[stream, way, hop - 1]
            wterm[c] = (wterm[c].astype(F32) + yr_s[last].astype(F32)).astype(BF16)
        ys[stream, way, hop] = send(
            wterm.at[c], yr_s.at[slot], y_ss.at[slot], y_rs.at[slot],
            right if way == 0 else left,
        )

    def x_relay():
        for name, way, xx in (("r", 0, xp), ("l", 1, xm)):
            xs[name + "1"].wait_recv()
            fterm[xx, way] = (
                fterm[xx, way].astype(F32) + x1_s[way].astype(F32)).astype(BF16)
            x_send(name + "3", 4 + way, fterm.at[xx, way], x2_s.at[way, way],
                   x_right if way == 0 else x_left)

    def ring_hop(hop):
        for stream, way in ((1, 1), (1, 0), (0, 0), (0, 1)):
            if hop <= HOPS[stream, way]:
                ring_send(stream, way, hop)

    weight_term(4)
    ring_send(1, 1, 1)
    ring_send(0, 0, 1)
    weight_term(3)
    ring_send(1, 0, 1)
    weight_term(5)
    ring_send(0, 1, 1)
    def later_terms(j, carry):
        weight_term(6 + j)
        return carry

    lax.fori_loop(0, 5, later_terms, 0)
    w2_across()
    ring_hop(2)
    x_start()
    ring_hop(3)
    own_term = feature_term(x)
    x_relay()
    ring_hop(4)
    lax.fori_loop(3, chunks, query_back, 0)
    for name in ("r2", "l2", "r3", "l3"):
        xs[name].wait_recv()
    own_term += x2_s[0].reshape(480, HD).astype(F32) + x2_s[1].reshape(480, HD).astype(F32)
    ft_s[...] = own_term.astype(BF16)
    outs = [
        pltpu.make_async_copy(dq_s, dq_hbm, loc_sem.at[7]),
        pltpu.make_async_copy(ft_s, ft_hbm, loc_sem.at[8]),
        pltpu.make_async_copy(kgw_s, kgw_hbm, loc_sem.at[9]),
        pltpu.make_async_copy(vgw_s, vgw_hbm, loc_sem.at[10]),
    ]
    outs[0].start()
    outs[1].start()

    def final_rows(stream):
        c = c_of(0, stream)
        total = wterm[c].astype(F32)
        for way in (0, 1):
            hop = HOPS[stream, way]
            ys[stream, way, hop].wait_recv()
            total += yr_s[slots[stream, way, hop]].astype(F32)
        return total

    hz_s[...] = final_rows(1).astype(BF16)
    hcopy = send(hz_s, hzr_s, h_ss, h_rs, far_z)
    own_rows = final_rows(0)
    drain((hcopy,))
    for dz in (1, 2, 3):
        for i in range(4):
            z_copy(4 * ((zl + dz) % ZL) + i)[1].wait_send()
    hcopy.wait_recv()
    own_rows += hzr_s[...].astype(F32)
    padded = jnp.concatenate((own_rows, jnp.zeros((256 - rows, HD), F32)), 0)
    turned = jnp.transpose(padded)
    kgw_s[...] = turned[:64, :rows]
    vgw_s[...] = turned[64:, :rows]
    outs[2].start()
    outs[3].start()
    drain()
    for copy in outs:
        copy.wait()


def copy_out(a, b, c, e, a_out, b_out, c_out, e_out, a_s, b_s, c_s, e_s, in_sems, out_sems):
    refs = [(b, b_s, b_out), (c, c_s, c_out), (e, e_s, e_out)]
    step = a_s.shape[0] // 4
    for i in range(4):
        at = pl.ds(i * step, step)
        refs.append((a.at[at], a_s.at[at], a_out.at[at]))
    loads = [
        pltpu.make_async_copy(src, mid, in_sems.at[i]) for i, (src, mid, dst) in enumerate(refs)
    ]
    stores = [
        pltpu.make_async_copy(mid, dst, out_sems.at[i]) for i, (src, mid, dst) in enumerate(refs)
    ]
    for copy in loads:
        copy.start()
    for load, store in zip(loads, stores):
        load.wait()
        store.start()
    for copy in stores:
        copy.wait()


def shards(
    queries, features, key_weight, value_weight, query_gain, key_gain, out_grad, tile_counts
):
    samples, own_rows, feature_width = features.shape
    tokens, q_width = queries.shape
    rows, column_half = key_weight.shape
    anyspec = pl.BlockSpec(memory_space=pl.ANY)
    dma = pltpu.SemaphoreType.DMA
    piece = (rows, HD)
    scratch = [
        pltpu.VMEM((tokens, q_width), BF16),
        pltpu.VMEM((tokens, q_width), BF16),
        pltpu.VMEM((tokens, q_width), BF16),
        pltpu.VMEM((own_rows, feature_width), BF16),
        pltpu.VMEM((16, 2) + piece, BF16),
        pltpu.VMEM((16, 2) + piece, BF16),
        pltpu.VMEM((HD, tokens * q_width // HD), BF16),
        pltpu.VMEM((tokens * q_width // HD, HD), BF16),
        pltpu.VMEM((ZL, X, 2) + piece, BF16),
    ]
    scratch += [pltpu.VMEM((HD, HD), BF16)] * 5
    scratch += [
        pltpu.VMEM((2, HD, HD), BF16),
        pltpu.VMEM((ZL, HD, HD), BF16),
        pltpu.VMEM((HD, HD), F32),
        pltpu.VMEM((HD, HD), F32),
        pltpu.VMEM((X, 2) + piece, BF16),
        pltpu.VMEM((16,) + piece, BF16),
        pltpu.VMEM((16,) + piece, BF16),
        pltpu.VMEM((14,) + piece, BF16),
        pltpu.VMEM((2,) + piece, BF16),
        pltpu.VMEM((2, 2) + piece, BF16),
        pltpu.VMEM(piece, BF16),
        pltpu.VMEM(piece, BF16),
        pltpu.VMEM((HD, HD), F32),
        pltpu.VMEM((HD, HD), F32),
        pltpu.VMEM((column_half, rows), BF16),
        pltpu.VMEM((column_half, rows), BF16),
        pltpu.VMEM((1, HD), F32),
        pltpu.VMEM((1, HD), F32),
        pltpu.VMEM((2 * rows, own_rows), BF16),
        pltpu.VMEM((column_half, rows), F32),
        pltpu.VMEM((column_half, rows), F32),
        dma((11,)),
        dma((3, 2, 4)), dma((3, 2, 4)), dma((2,)), dma((2,)), dma((24,)), dma((24,)), dma((3,)), dma((3,)),
        dma((8,)), dma((8,)), dma((14,)), dma((14,)), dma((6,)), dma((6,)),
        dma((16,)), dma((4, 4)), dma((3, 4)), dma((3, 4)), dma((3,)), dma((3,)), dma, dma,
    ]
    out_shape = (
        jax.ShapeDtypeStruct((tokens, q_width), BF16),
        jax.ShapeDtypeStruct((2 * rows, own_rows), BF16),
        jax.ShapeDtypeStruct((column_half, rows), F32),
        jax.ShapeDtypeStruct((column_half, rows), F32),
    )
    results = pl.pallas_call(
        kernel,
        out_shape=out_shape,
        in_specs=[pl.BlockSpec(memory_space=pltpu.SMEM)] + [anyspec] * 7,
        out_specs=(anyspec,) * 4,
        scratch_shapes=scratch,
        compiler_params=pltpu.CompilerParams(
            collective_id=0, has_side_effects=True, vmem_limit_bytes=62 * 1024 * 1024
        ),
        cost_estimate=pl.CostEstimate(
            flops=1600000000, bytes_accessed=8000000, transcendentals=500000
        ),
    )(
        tile_counts, queries, features.reshape(own_rows, feature_width), key_weight.T,
        value_weight.T, query_gain.reshape(1, HD), key_gain.reshape(1, HD), out_grad,
    )
    query_grad, feature_t, key_t, value_t = pl.pallas_call(
        copy_out,
        out_shape=out_shape,
        in_specs=[anyspec] * 4,
        out_specs=(anyspec,) * 4,
        scratch_shapes=[pltpu.VMEM(o.shape, o.dtype) for o in out_shape] + [dma((7,)), dma((7,))],
        compiler_params=pltpu.CompilerParams(vmem_limit_bytes=62 * 1024 * 1024),
        cost_estimate=pl.CostEstimate(flops=0, bytes_accessed=3000000, transcendentals=0),
    )(*results)
    return (query_grad, feature_t.T.reshape(samples, own_rows, 2 * rows), key_t.T, value_t.T)


def solution(mesh):
    placed = (
        P("dp", "tensor"),
        P("dp", None, None),
        P("dp", "tensor"),
        P("dp", "tensor"),
        P(),
        P(),
        P("dp", "tensor"),
        P("dp"),
    )
    return jax.shard_map(
        shards,
        mesh=mesh,
        in_specs=placed,
        out_specs=(
            P("dp", "tensor"),
            P("dp", None, "tensor"),
            P("dp", "tensor"),
            P("dp", "tensor"),
        ),
        check_vma=False,
    )
```

```python
import functools
import math

import jax
import jax.numpy as jnp
from jax import lax
from jax.experimental import pallas as pl
from jax.experimental.pallas import tpu as pltpu
from jax.sharding import PartitionSpec as P

TILE_ROWS = 32
EPS = 1e-05
HD = 128
Y, X, ZL = 8, 4, 4
CH = 160
HOPS = {(0, 0): 4, (0, 1): 3, (1, 0): 3, (1, 1): 4}
PIECES = ((0, 240), (0, 128), (128, 112))
F32 = jnp.float32
BF16 = jnp.bfloat16
NT = (((1,), (1,)), ((), ()))
TN = (((0,), (0,)), ((), ()))


def dot(a, b, dims=(((1,), (0,)), ((), ()))):
    return lax.dot_general(a, b, dims, preferred_element_type=F32)


def kernel(
    tc_ref, q_hbm, feat_hbm, kwt_hbm, vwt_hbm, qg_hbm, kg_hbm, do_hbm,
    dq_hbm, ft_hbm, kgw_hbm, vgw_hbm,
    q_s, do_s, dq_s, feat_s, featT, wbuf, dsT, qn_s, w2_s, own_s, par_s, kbf_s, vbf_s, far_s,
    farr_s, g4_s, own_grad_s, other_grad_s, fterm, wterm, fx_s, yr_s, x1_s, x2_s, hz_s, hzr_s, vg_s, kg_s,
    kwt_s, vwt_s, qg_s, kg_in_s, ft_s, kgw_s, vgw_s,
    loc_sem, ag_ss, ag_rs, agz_ss, agz_rs, agc_ss, agc_rs, p_ss, p_rs,
    c_ss, c_rs, y_ss, y_rs, x_ss, x_rs, zf_ss, zf_rs, wc_ss, wc_rs, gz_ss, gz_rs, h_ss, h_rs,
):
    d = lax.axis_index("dp")
    t = lax.axis_index("tensor")
    y, zh, core = d // 4, (d // 2) % 2, d % 2
    zl, x = t // 4, t % 4
    low = (t % 2) == 0

    def at_y(step):
        return (((y + step + Y) % Y) * 4 + zh * 2 + core, t)

    right, left = at_y(1), at_y(-1)
    far_core = (d + 1 - 2 * core, t)
    far_z = (d + 2 - 4 * zh, t)
    partner = (d, t + 1 - 2 * (t % 2))
    diagonal = (d + 1 - 2 * core, t + 1 - 2 * (t % 2))
    x_right = (d, zl * 4 + (x + 1) % X)
    x_left = (d, zl * 4 + (x + X - 1) % X)
    z_to = [(d, ((zl + k) % ZL) * 4 + x) for k in (1, 2, 3)]

    barrier = pltpu.get_barrier_semaphore()
    peers = [right, left, far_core, far_z, x_right, x_left, diagonal] + z_to
    for peer in peers:
        pl.semaphore_signal(barrier, inc=1, device_id=peer, device_id_type=pl.DeviceIdType.MESH)

    tokens = q_s.shape[0]
    heads = q_s.shape[1] // HD
    width = CH * heads
    chunks = tokens // CH
    fetched = (
        (kwt_hbm, kwt_s), (vwt_hbm, vwt_s), (feat_hbm, feat_s), (q_hbm, q_s), (do_hbm, do_s),
        (qg_hbm, qg_s), (kg_hbm, kg_in_s),
    )
    copies = [
        pltpu.make_async_copy(src, dst, loc_sem.at[i]) for i, (src, dst) in enumerate(fetched)
    ]
    for copy in copies:
        copy.start()

    sent = []

    def drain(later=()):
        kept = [copy for copy in sent if any(copy is one for one in later)]
        for copy in sent:
            if not any(copy is one for one in later):
                copy.wait_send()
        sent[:] = kept

    def send(src, dst, ssem, rsem, dev):
        copy = pltpu.make_async_remote_copy(
            src_ref=src, dst_ref=dst, send_sem=ssem, recv_sem=rsem,
            device_id=dev, device_id_type=pl.DeviceIdType.MESH,
        )
        copy.start()
        sent.append(copy)
        return copy

    copies[0].wait()
    copies[1].wait()
    shard = jnp.concatenate((kwt_s[...], vwt_s[...]), 0).astype(F32)
    rows = shard.shape[1]
    shard = jnp.concatenate((shard, jnp.zeros((HD, 256 - rows), F32)), 1)
    mine = 2 * y + zh
    wbuf[mine, core] = jnp.transpose(shard)[:rows].astype(BF16)

    pl.semaphore_wait(barrier, len(peers))

    def c_of(step, stream):
        zz = zh if stream == 0 else 1 - zh
        return 2 * ((y + step + Y) % Y) + zz

    def piece_of(c, part):
        return wbuf.at[c, core, pl.ds(*PIECES[part])]

    def gather_send(part, way, hop):
        c = c_of((1 - hop) if way == 0 else (hop - 1), min(part, 1))
        ref = piece_of(c, part)
        return send(ref, ref, ag_ss.at[part, way, hop - 1], ag_rs.at[part, way, hop - 1],
                    right if way == 0 else left)

    across = []

    def core_send(c, part):
        ref = piece_of(c, part)
        i = len(across)
        across.append(send(ref, ref, agc_ss.at[i], agc_rs.at[i], far_core))

    def z_copy(c):
        dest = c // ZL
        return dest, pltpu.make_async_remote_copy(
            src_ref=wbuf.at[c, core], dst_ref=w2_s.at[zl, c % ZL, core],
            send_sem=zf_ss.at[c], recv_sem=zf_rs.at[zl, c % ZL],
            device_id=(d, dest * X + x), device_id_type=pl.DeviceIdType.MESH,
        )

    def z_send(c):
        dest, copy = z_copy(c)

        @pl.when(dest != zl)
        def _():
            copy.start()

    ag = {}
    zcopies = {}
    for part in (1, 2):
        ref = piece_of(mine, part)
        zcopies[part] = send(ref, ref, agz_ss.at[part - 1], agz_rs.at[part - 1], far_z)
    for way in (0, 1):
        ag[0, way, 1] = gather_send(0, way, 1)
    core_send(mine, 0)

    copies[2].wait()
    copies[3].wait()
    copies[5].wait()
    copies[6].wait()
    inverse = 1.0 / math.sqrt(HD)
    qg = qg_s[...]
    kg = kg_in_s[...]

    def shared_copy(part):
        group = pl.ds(part * 4, 4)
        return pltpu.make_async_remote_copy(
            src_ref=featT.at[group, 1 - core], dst_ref=fx_s.at[group],
            send_sem=c_ss.at[part], recv_sem=c_rs.at[part],
            device_id=far_core, device_id_type=pl.DeviceIdType.MESH,
        )

    def transpose_part(part, carry):
        cols = feat_s[:, pl.ds(pl.multiple_of(part * 1920, 1920), 1920)]
        featT[pl.ds(part * 4, 4)] = jnp.transpose(cols).reshape(4, 2, 240, HD)
        shared_copy(part).start()
        return carry

    def stack(ref, chunk):
        at = pl.ds(pl.multiple_of(chunk * CH, CH), CH)
        return jnp.concatenate([ref[at, h * HD:(h + 1) * HD] for h in range(heads)], 0)

    def wide(chunk):
        return pl.ds(pl.multiple_of(chunk * width, width), width)

    def query_norm(chunk, carry):
        xq = stack(q_s, chunk).astype(F32)
        r = lax.rsqrt(jnp.mean(xq * xq, -1, keepdims=True) + EPS)
        qn_s[wide(chunk), :] = (xq * r * qg).astype(BF16)
        return carry

    def gather_step(part, hop):
        for way in (1, 0):
            if hop > HOPS[min(part, 1), way]:
                continue
            ag[part, way, hop].wait_recv()
            if hop < HOPS[min(part, 1), way]:
                ag[part, way, hop + 1] = gather_send(part, way, hop + 1)
            c = c_of(-hop if way == 0 else hop, min(part, 1))
            core_send(c, part)
            if part == 2 or (part == 0 and hop > 1):
                z_send(c)

    arrived = 0
    marks = []

    def project(part, total):
        at = (y // 2 + part) % 4
        cols = feat_s[:, pl.ds(pl.multiple_of(at * 1920, 1920), 1920)]
        return total + dot(cols, wbuf[pl.ds(4 * at, 4)].reshape(1920, HD))

    proj = jnp.zeros((HD, HD), F32)
    for hop in range(1, 6):
        if hop <= 4:
            gather_step(0, hop)
        if hop == 1:
            for part in (1, 2):
                zcopies[part].wait_recv()
                for way in (1, 0):
                    ag[part, way, 1] = gather_send(part, way, 1)
                core_send(c_of(0, 1), part)
            for c in (mine, c_of(-1, 0), c_of(1, 0), c_of(0, 1)):
                z_send(c)
        else:
            gather_step(1, hop - 1)
            gather_step(2, hop - 1)
        if hop <= 4:
            transpose_part(hop - 1, 0)
            query_norm(hop - 1, 0)
        marks.append(len(across))
        if hop >= 4:
            for mark, first_part, end_part in {4: ((2, 4, 5),), 5: ((3, 5, 6), (3, 7, 8), (4, 6, 7))}[hop]:
                for copy in across[arrived:marks[mark]]:
                    copy.wait_recv()
                arrived = max(arrived, marks[mark])
                for part in range(first_part, end_part):
                    proj = project(part, proj)
    own_s[...] = proj.astype(BF16)
    pcopy = send(own_s, par_s, p_ss.at[0], p_rs.at[0], partner)
    copies[4].wait()
    lax.fori_loop(4, chunks, query_norm, 0)
    lane = lax.broadcasted_iota(jnp.int32, (HD, HD), 1)
    half = lane < 64
    lowf = jnp.where(low, 1.0, 0.0).astype(F32)
    own = own_s[...].astype(F32)
    pcopy.wait_recv()
    other = par_s[...].astype(F32)
    first = own * lowf + other * (1.0 - lowf)
    second = other * lowf + own * (1.0 - lowf)
    keys = jnp.where(half, first, pltpu.roll(second, 64, 1))
    values = jnp.where(half, pltpu.roll(first, 64, 1), second)
    k_scale = lax.rsqrt(jnp.mean(keys * keys, -1, keepdims=True) + EPS)
    kbf_s[...] = (keys * k_scale * kg).astype(BF16)
    vbf_s[...] = values.astype(BF16)
    live = (
        lax.broadcasted_iota(jnp.int32, (HD, 1), 0) < tc_ref[0] * TILE_ROWS
    ).astype(F32)
    vg_s[...] = jnp.zeros_like(vg_s)
    kg_s[...] = jnp.zeros_like(kg_s)

    def attend(chunk, carry):
        qn = qn_s[wide(chunk), :]
        do = stack(do_s, chunk)
        e = jnp.exp(dot(kbf_s[...], qn, NT) * inverse) * live
        p = e * (1.0 / jnp.sum(e, 0, keepdims=True))
        pb = p.astype(BF16)
        vg_s[...] += dot(pb, do)
        pg = dot(vbf_s[...], do, NT)
        delta = jnp.sum(pb.astype(F32) * pg, 0, keepdims=True)
        ds = (p * (pg - delta)).astype(BF16)
        dsT[:, wide(chunk)] = ds
        kg_s[...] += dot(ds, qn)
        return carry

    lax.fori_loop(0, chunks, attend, 0, unroll=2)

    weighted = kg_s[...] * (inverse * kg)
    key_grad = k_scale * weighted - keys * (
        k_scale * k_scale * k_scale * jnp.mean(weighted * keys, -1, keepdims=True)
    )
    value_grad = vg_s[...]
    low_part = jnp.where(half, key_grad, pltpu.roll(value_grad, 64, 1))
    high_part = jnp.where(half, pltpu.roll(key_grad, 64, 1), value_grad)
    own_grad_s[...] = low_part * lowf + high_part * (1.0 - lowf)
    far_s[...] = (high_part * lowf + low_part * (1.0 - lowf)).astype(BF16)
    fcopy = send(far_s, farr_s.at[0], p_ss.at[1], p_rs.at[1], partner)
    ocopy = send(own_grad_s, other_grad_s, c_ss.at[4], c_rs.at[4], far_core)
    dcopy = send(far_s, farr_s.at[1], p_ss.at[2], p_rs.at[2], diagonal)

    def query_back(chunk, carry):
        xq = stack(q_s, chunk).astype(F32)
        r = lax.rsqrt(jnp.mean(xq * xq, -1, keepdims=True) + EPS)
        u = dot(dsT[:, wide(chunk)], kbf_s[...], TN) * (inverse * qg)
        m = jnp.mean(u * xq, -1, keepdims=True)
        back = (r * u - xq * (r * r * r * m)).astype(BF16)
        at = pl.ds(pl.multiple_of(chunk * CH, CH), CH)
        for h in range(heads):
            dq_s[at, h * HD:(h + 1) * HD] = back[h * CH:(h + 1) * CH]
        return carry

    drain((fcopy, ocopy, dcopy))
    lax.fori_loop(0, 3, query_back, 0)
    for part in range(4):
        shared_copy(part).wait_send()
    fcopy.wait_recv()
    g4_s[zl] = (own_grad_s[...] + farr_s[0].astype(F32)).astype(BF16)
    g = g4_s[zl]
    gz = []
    for k in (1, 2, 0):
        gz.append(send(g4_s.at[zl], g4_s.at[zl], gz_ss.at[k], gz_rs.at[k], z_to[k]))

    ocopy.wait_recv()
    dcopy.wait_recv()
    go = (other_grad_s[...] + farr_s[1].astype(F32)).astype(BF16)
    for part in range(4):
        shared_copy(part).wait_recv()

    def weight_term(step):
        for stream in (1, 0):
            c = c_of(step, stream)
            wterm[c] = (dot(featT[c, core], g) + dot(fx_s[c], go)).astype(BF16)

    def feature_term(xx):
        total = dot(wbuf[zl * X + xx].reshape(480, HD), g, NT)
        for dz in (1, 2, 3):
            src = (zl + dz) % ZL
            total += dot(w2_s[src, xx].reshape(480, HD), g4_s[src], NT)
        return total

    x2, xp, xm = (x + 2) % X, (x + 1) % X, (x + 3) % X
    xs = {}

    def x_send(name, slot, src, dst, dev):
        xs[name] = send(src, dst, x_ss.at[slot], x_rs.at[slot], dev)

    def x_start():
        for copy in gz + wc:
            copy.wait_recv()
        for xx in (x2, xp, xm):
            fterm[xx] = feature_term(xx).astype(BF16).reshape(2, 240, HD)
            if xx is x2:
                x_send("r1", 0, fterm.at[x2, 0], x1_s.at[0], x_right)
                x_send("l1", 1, fterm.at[x2, 1], x1_s.at[1], x_left)
            elif xx is xp:
                x_send("r2", 2, fterm.at[xp, 1], x2_s.at[0, 1], x_right)
            else:
                x_send("l2", 3, fterm.at[xm, 0], x2_s.at[1, 0], x_left)

    wc = []

    def w2_across():
        for dz in (1, 3, 2):
            src = (zl + dz) % ZL
            for i in range(4):
                ref = w2_s.at[src, i, core]
                pltpu.make_async_remote_copy(
                    src_ref=ref, dst_ref=ref, send_sem=zf_ss.at[0], recv_sem=zf_rs.at[src, i],
                    device_id=far_core, device_id_type=pl.DeviceIdType.MESH,
                ).wait_recv()
                wc.append(send(ref, ref, wc_ss.at[dz - 1, i], wc_rs.at[dz - 1, i], far_core))

    slots = {}
    for key in ((0, 0), (1, 1), (0, 1), (1, 0)):
        for hop in range(1, HOPS[key] + 1):
            slots[key + (hop,)] = len(slots)
    ys = {}

    def ring_send(stream, way, hop):
        step = HOPS[stream, way] - hop + 1
        c = c_of(step if way == 0 else -step, stream)
        slot = slots[stream, way, hop]
        if hop > 1:
            ys[stream, way, hop - 1].wait_recv()
            last = slots[stream, way, hop - 1]
            wterm[c] = (wterm[c].astype(F32) + yr_s[last].astype(F32)).astype(BF16)
        ys[stream, way, hop] = send(
            wterm.at[c], yr_s.at[slot], y_ss.at[slot], y_rs.at[slot],
            right if way == 0 else left,
        )

    def x_relay():
        for name, way, xx in (("r", 0, xp), ("l", 1, xm)):
            xs[name + "1"].wait_recv()
            fterm[xx, way] = (
                fterm[xx, way].astype(F32) + x1_s[way].astype(F32)).astype(BF16)
            x_send(name + "3", 4 + way, fterm.at[xx, way], x2_s.at[way, way],
                   x_right if way == 0 else x_left)

    def ring_hop(hop):
        for stream, way in ((1, 1), (1, 0), (0, 0), (0, 1)):
            if hop <= HOPS[stream, way]:
                ring_send(stream, way, hop)

    def final_rows(stream):
        c = c_of(0, stream)
        total = wterm[c].astype(F32)
        for way in (0, 1):
            hop = HOPS[stream, way]
            ys[stream, way, hop].wait_recv()
            total += yr_s[slots[stream, way, hop]].astype(F32)
        return total

    weight_term(4)
    ring_send(1, 1, 1)
    ring_send(0, 0, 1)
    weight_term(3)
    ring_send(1, 0, 1)
    weight_term(5)
    ring_send(0, 1, 1)
    def later_terms(j, carry):
        weight_term(6 + j)
        return carry

    lax.fori_loop(0, 5, later_terms, 0)
    ring_hop(2)
    w2_across()
    ring_hop(3)
    x_start()
    ring_hop(4)
    x_relay()
    hz_s[...] = final_rows(1).astype(BF16)
    hcopy = send(hz_s, hzr_s, h_ss, h_rs, far_z)
    own_term = feature_term(x)
    lax.fori_loop(3, chunks, query_back, 0)
    for name in ("r2", "l2", "r3", "l3"):
        xs[name].wait_recv()
    own_term += x2_s[0].reshape(480, HD).astype(F32) + x2_s[1].reshape(480, HD).astype(F32)
    ft_s[...] = own_term.astype(BF16)
    outs = [
        pltpu.make_async_copy(dq_s, dq_hbm, loc_sem.at[7]),
        pltpu.make_async_copy(ft_s, ft_hbm, loc_sem.at[8]),
        pltpu.make_async_copy(kgw_s, kgw_hbm, loc_sem.at[9]),
        pltpu.make_async_copy(vgw_s, vgw_hbm, loc_sem.at[10]),
    ]
    outs[0].start()
    outs[1].start()

    own_rows = final_rows(0)
    drain((hcopy,))
    for dz in (1, 2, 3):
        for i in range(4):
            z_copy(4 * ((zl + dz) % ZL) + i)[1].wait_send()
    hcopy.wait_recv()
    own_rows += hzr_s[...].astype(F32)
    padded = jnp.concatenate((own_rows, jnp.zeros((256 - rows, HD), F32)), 0)
    turned = jnp.transpose(padded)
    kgw_s[...] = turned[:64, :rows]
    vgw_s[...] = turned[64:, :rows]
    outs[2].start()
    outs[3].start()
    drain()
    for copy in outs:
        copy.wait()


def copy_out(a, b, c, e, a_out, b_out, c_out, e_out, a_s, b_s, c_s, e_s, in_sems, out_sems):
    refs = [(b, b_s, b_out), (c, c_s, c_out), (e, e_s, e_out)]
    step = a_s.shape[0] // 4
    for i in range(4):
        at = pl.ds(i * step, step)
        refs.append((a.at[at], a_s.at[at], a_out.at[at]))
    loads = [
        pltpu.make_async_copy(src, mid, in_sems.at[i]) for i, (src, mid, dst) in enumerate(refs)
    ]
    stores = [
        pltpu.make_async_copy(mid, dst, out_sems.at[i]) for i, (src, mid, dst) in enumerate(refs)
    ]
    for copy in loads:
        copy.start()
    for load, store in zip(loads, stores):
        load.wait()
        store.start()
    for copy in stores:
        copy.wait()


def shards(
    queries, features, key_weight, value_weight, query_gain, key_gain, out_grad, tile_counts
):
    samples, own_rows, feature_width = features.shape
    tokens, q_width = queries.shape
    rows, column_half = key_weight.shape
    anyspec = pl.BlockSpec(memory_space=pl.ANY)
    dma = pltpu.SemaphoreType.DMA
    piece = (rows, HD)
    scratch = [
        pltpu.VMEM((tokens, q_width), BF16),
        pltpu.VMEM((tokens, q_width), BF16),
        pltpu.VMEM((tokens, q_width), BF16),
        pltpu.VMEM((own_rows, feature_width), BF16),
        pltpu.VMEM((16, 2) + piece, BF16),
        pltpu.VMEM((16, 2) + piece, BF16),
        pltpu.VMEM((HD, tokens * q_width // HD), BF16),
        pltpu.VMEM((tokens * q_width // HD, HD), BF16),
        pltpu.VMEM((ZL, X, 2) + piece, BF16),
    ]
    scratch += [pltpu.VMEM((HD, HD), BF16)] * 5
    scratch += [
        pltpu.VMEM((2, HD, HD), BF16),
        pltpu.VMEM((ZL, HD, HD), BF16),
        pltpu.VMEM((HD, HD), F32),
        pltpu.VMEM((HD, HD), F32),
        pltpu.VMEM((X, 2) + piece, BF16),
        pltpu.VMEM((16,) + piece, BF16),
        pltpu.VMEM((16,) + piece, BF16),
        pltpu.VMEM((14,) + piece, BF16),
        pltpu.VMEM((2,) + piece, BF16),
        pltpu.VMEM((2, 2) + piece, BF16),
        pltpu.VMEM(piece, BF16),
        pltpu.VMEM(piece, BF16),
        pltpu.VMEM((HD, HD), F32),
        pltpu.VMEM((HD, HD), F32),
        pltpu.VMEM((column_half, rows), BF16),
        pltpu.VMEM((column_half, rows), BF16),
        pltpu.VMEM((1, HD), F32),
        pltpu.VMEM((1, HD), F32),
        pltpu.VMEM((2 * rows, own_rows), BF16),
        pltpu.VMEM((column_half, rows), F32),
        pltpu.VMEM((column_half, rows), F32),
        dma((11,)),
        dma((3, 2, 4)), dma((3, 2, 4)), dma((2,)), dma((2,)), dma((24,)), dma((24,)), dma((3,)), dma((3,)),
        dma((8,)), dma((8,)), dma((14,)), dma((14,)), dma((6,)), dma((6,)),
        dma((16,)), dma((4, 4)), dma((3, 4)), dma((3, 4)), dma((3,)), dma((3,)), dma, dma,
    ]
    out_shape = (
        jax.ShapeDtypeStruct((tokens, q_width), BF16),
        jax.ShapeDtypeStruct((2 * rows, own_rows), BF16),
        jax.ShapeDtypeStruct((column_half, rows), F32),
        jax.ShapeDtypeStruct((column_half, rows), F32),
    )
    results = pl.pallas_call(
        kernel,
        out_shape=out_shape,
        in_specs=[pl.BlockSpec(memory_space=pltpu.SMEM)] + [anyspec] * 7,
        out_specs=(anyspec,) * 4,
        scratch_shapes=scratch,
        compiler_params=pltpu.CompilerParams(
            collective_id=0, has_side_effects=True, vmem_limit_bytes=62 * 1024 * 1024
        ),
        cost_estimate=pl.CostEstimate(
            flops=1600000000, bytes_accessed=8000000, transcendentals=500000
        ),
    )(
        tile_counts, queries, features.reshape(own_rows, feature_width), key_weight.T,
        value_weight.T, query_gain.reshape(1, HD), key_gain.reshape(1, HD), out_grad,
    )
    query_grad, feature_t, key_t, value_t = pl.pallas_call(
        copy_out,
        out_shape=out_shape,
        in_specs=[anyspec] * 4,
        out_specs=(anyspec,) * 4,
        scratch_shapes=[pltpu.VMEM(o.shape, o.dtype) for o in out_shape] + [dma((7,)), dma((7,))],
        compiler_params=pltpu.CompilerParams(vmem_limit_bytes=62 * 1024 * 1024),
        cost_estimate=pl.CostEstimate(flops=0, bytes_accessed=3000000, transcendentals=0),
    )(*results)
    return (query_grad, feature_t.T.reshape(samples, own_rows, 2 * rows), key_t.T, value_t.T)


def solution(mesh):
    placed = (
        P("dp", "tensor"),
        P("dp", None, None),
        P("dp", "tensor"),
        P("dp", "tensor"),
        P(),
        P(),
        P("dp", "tensor"),
        P("dp"),
    )
    return jax.shard_map(
        shards,
        mesh=mesh,
        in_specs=placed,
        out_specs=(
            P("dp", "tensor"),
            P("dp", None, "tensor"),
            P("dp", "tensor"),
            P("dp", "tensor"),
        ),
        check_vma=False,
    )
```

```python
import functools
import math

import jax
import jax.numpy as jnp
from jax import lax
from jax.experimental import pallas as pl
from jax.experimental.pallas import tpu as pltpu
from jax.sharding import PartitionSpec as P

TILE_ROWS = 32
EPS = 1e-05
HD = 128
Y, X, ZL = 8, 4, 4
CH = 160
HOPS = {(0, 0): 4, (0, 1): 3, (1, 0): 3, (1, 1): 4}
PIECES = ((0, 240), (0, 128), (128, 112))
F32 = jnp.float32
BF16 = jnp.bfloat16
NT = (((1,), (1,)), ((), ()))
TN = (((0,), (0,)), ((), ()))


def dot(a, b, dims=(((1,), (0,)), ((), ()))):
    return lax.dot_general(a, b, dims, preferred_element_type=F32)


def kernel(
    tc_ref, q_hbm, feat_hbm, kwt_hbm, vwt_hbm, qg_hbm, kg_hbm, do_hbm,
    dq_hbm, ft_hbm, kgw_hbm, vgw_hbm,
    q_s, do_s, dq_s, feat_s, featT, wbuf, dsT, qn_s, w2_s, own_s, par_s, kbf_s, vbf_s, far_s,
    farr_s, g4_s, own_grad_s, other_grad_s, fterm, wterm, fx_s, yr_s, x1_s, x2_s, hz_s, hzr_s, vg_s, kg_s,
    kwt_s, vwt_s, qg_s, kg_in_s, ft_s, kgw_s, vgw_s,
    loc_sem, ag_ss, ag_rs, agz_ss, agz_rs, agc_ss, agc_rs, p_ss, p_rs,
    c_ss, c_rs, y_ss, y_rs, x_ss, x_rs, zf_ss, zf_rs, wc_ss, wc_rs, gz_ss, gz_rs, h_ss, h_rs,
):
    d = lax.axis_index("dp")
    t = lax.axis_index("tensor")
    y, zh, core = d // 4, (d // 2) % 2, d % 2
    zl, x = t // 4, t % 4
    low = (t % 2) == 0

    def at_y(step):
        return (((y + step + Y) % Y) * 4 + zh * 2 + core, t)

    right, left = at_y(1), at_y(-1)
    far_core = (d + 1 - 2 * core, t)
    far_z = (d + 2 - 4 * zh, t)
    partner = (d, t + 1 - 2 * (t % 2))
    diagonal = (d + 1 - 2 * core, t + 1 - 2 * (t % 2))
    x_right = (d, zl * 4 + (x + 1) % X)
    x_left = (d, zl * 4 + (x + X - 1) % X)
    z_to = [(d, ((zl + k) % ZL) * 4 + x) for k in (1, 2, 3)]

    barrier = pltpu.get_barrier_semaphore()
    peers = [right, left, far_core, far_z, x_right, x_left, diagonal] + z_to
    for peer in peers:
        pl.semaphore_signal(barrier, inc=1, device_id=peer, device_id_type=pl.DeviceIdType.MESH)

    tokens = q_s.shape[0]
    heads = q_s.shape[1] // HD
    width = CH * heads
    chunks = tokens // CH
    fetched = (
        (kwt_hbm, kwt_s), (vwt_hbm, vwt_s), (feat_hbm, feat_s), (q_hbm, q_s), (do_hbm, do_s),
        (qg_hbm, qg_s), (kg_hbm, kg_in_s),
    )
    copies = [
        pltpu.make_async_copy(src, dst, loc_sem.at[i]) for i, (src, dst) in enumerate(fetched)
    ]
    for copy in copies:
        copy.start()

    sent = []

    def drain(later=()):
        kept = [copy for copy in sent if any(copy is one for one in later)]
        for copy in sent:
            if not any(copy is one for one in later):
                copy.wait_send()
        sent[:] = kept

    def send(src, dst, ssem, rsem, dev):
        copy = pltpu.make_async_remote_copy(
            src_ref=src, dst_ref=dst, send_sem=ssem, recv_sem=rsem,
            device_id=dev, device_id_type=pl.DeviceIdType.MESH,
        )
        copy.start()
        sent.append(copy)
        return copy

    copies[0].wait()
    copies[1].wait()
    shard = jnp.concatenate((kwt_s[...], vwt_s[...]), 0).astype(F32)
    rows = shard.shape[1]
    shard = jnp.concatenate((shard, jnp.zeros((HD, 256 - rows), F32)), 1)
    mine = 2 * y + zh
    wbuf[mine, core] = jnp.transpose(shard)[:rows].astype(BF16)

    pl.semaphore_wait(barrier, len(peers))

    def c_of(step, stream):
        zz = zh if stream == 0 else 1 - zh
        return 2 * ((y + step + Y) % Y) + zz

    def piece_of(c, part):
        return wbuf.at[c, core, pl.ds(*PIECES[part])]

    def gather_send(part, way, hop):
        c = c_of((1 - hop) if way == 0 else (hop - 1), min(part, 1))
        ref = piece_of(c, part)
        return send(ref, ref, ag_ss.at[part, way, hop - 1], ag_rs.at[part, way, hop - 1],
                    right if way == 0 else left)

    across = []

    def core_send(c, part):
        ref = piece_of(c, part)
        i = len(across)
        across.append(send(ref, ref, agc_ss.at[i], agc_rs.at[i], far_core))

    def z_copy(c):
        dest = c // ZL
        return dest, pltpu.make_async_remote_copy(
            src_ref=wbuf.at[c, core], dst_ref=w2_s.at[zl, c % ZL, core],
            send_sem=zf_ss.at[c], recv_sem=zf_rs.at[zl, c % ZL],
            device_id=(d, dest * X + x), device_id_type=pl.DeviceIdType.MESH,
        )

    def z_send(c):
        dest, copy = z_copy(c)

        @pl.when(dest != zl)
        def _():
            copy.start()

    ag = {}
    zcopies = {}
    for part in (1, 2):
        ref = piece_of(mine, part)
        zcopies[part] = send(ref, ref, agz_ss.at[part - 1], agz_rs.at[part - 1], far_z)
    for way in (0, 1):
        ag[0, way, 1] = gather_send(0, way, 1)
    core_send(mine, 0)

    copies[2].wait()
    copies[3].wait()
    copies[5].wait()
    copies[6].wait()
    inverse = 1.0 / math.sqrt(HD)
    qg = qg_s[...]
    kg = kg_in_s[...]

    def shared_copy(part):
        group = pl.ds(part * 4, 4)
        return pltpu.make_async_remote_copy(
            src_ref=featT.at[group, 1 - core], dst_ref=fx_s.at[group],
            send_sem=c_ss.at[part], recv_sem=c_rs.at[part],
            device_id=far_core, device_id_type=pl.DeviceIdType.MESH,
        )

    def transpose_part(part, carry):
        cols = feat_s[:, pl.ds(pl.multiple_of(part * 1920, 1920), 1920)]
        featT[pl.ds(part * 4, 4)] = jnp.transpose(cols).reshape(4, 2, 240, HD)
        return carry

    def stack(ref, chunk):
        at = pl.ds(pl.multiple_of(chunk * CH, CH), CH)
        return jnp.concatenate([ref[at, h * HD:(h + 1) * HD] for h in range(heads)], 0)

    def wide(chunk):
        return pl.ds(pl.multiple_of(chunk * width, width), width)

    def query_norm(chunk, carry):
        xq = stack(q_s, chunk).astype(F32)
        r = lax.rsqrt(jnp.mean(xq * xq, -1, keepdims=True) + EPS)
        qn_s[wide(chunk), :] = (xq * r * qg).astype(BF16)
        return carry

    def gather_step(part, hop):
        for way in (1, 0):
            if hop > HOPS[min(part, 1), way]:
                continue
            ag[part, way, hop].wait_recv()
            if hop < HOPS[min(part, 1), way]:
                ag[part, way, hop + 1] = gather_send(part, way, hop + 1)
            c = c_of(-hop if way == 0 else hop, min(part, 1))
            core_send(c, part)
            if part == 2 or (part == 0 and hop > 1):
                z_send(c)

    arrived = 0
    marks = []

    def project(part, total):
        at = (y // 2 + part) % 4
        cols = feat_s[:, pl.ds(pl.multiple_of(at * 1920, 1920), 1920)]
        return total + dot(cols, wbuf[pl.ds(4 * at, 4)].reshape(1920, HD))

    proj = jnp.zeros((HD, HD), F32)
    for hop in range(1, 6):
        if hop <= 4:
            gather_step(0, hop)
        if hop == 1:
            for part in (1, 2):
                zcopies[part].wait_recv()
                for way in (1, 0):
                    ag[part, way, 1] = gather_send(part, way, 1)
                core_send(c_of(0, 1), part)
            for c in (mine, c_of(-1, 0), c_of(1, 0), c_of(0, 1)):
                z_send(c)
        else:
            gather_step(1, hop - 1)
            gather_step(2, hop - 1)
        if hop <= 4:
            transpose_part(hop - 1, 0)
            query_norm(hop - 1, 0)
        marks.append(len(across))
        if hop >= 4:
            for mark, first_part, end_part in {4: ((2, 4, 5),), 5: ((3, 5, 6), (3, 7, 8), (4, 6, 7))}[hop]:
                for copy in across[arrived:marks[mark]]:
                    copy.wait_recv()
                arrived = max(arrived, marks[mark])
                for part in range(first_part, end_part):
                    proj = project(part, proj)
    own_s[...] = proj.astype(BF16)
    pcopy = send(own_s, par_s, p_ss.at[0], p_rs.at[0], partner)
    for part in range(4):
        shared_copy(part).start()
    copies[4].wait()
    lax.fori_loop(4, chunks, query_norm, 0)
    lane = lax.broadcasted_iota(jnp.int32, (HD, HD), 1)
    half = lane < 64
    lowf = jnp.where(low, 1.0, 0.0).astype(F32)
    own = own_s[...].astype(F32)
    pcopy.wait_recv()
    other = par_s[...].astype(F32)
    first = own * lowf + other * (1.0 - lowf)
    second = other * lowf + own * (1.0 - lowf)
    keys = jnp.where(half, first, pltpu.roll(second, 64, 1))
    values = jnp.where(half, pltpu.roll(first, 64, 1), second)
    k_scale = lax.rsqrt(jnp.mean(keys * keys, -1, keepdims=True) + EPS)
    kbf_s[...] = (keys * k_scale * kg).astype(BF16)
    vbf_s[...] = values.astype(BF16)
    live = (
        lax.broadcasted_iota(jnp.int32, (HD, 1), 0) < tc_ref[0] * TILE_ROWS
    ).astype(F32)
    vg_s[...] = jnp.zeros_like(vg_s)
    kg_s[...] = jnp.zeros_like(kg_s)

    def attend(chunk, carry):
        qn = qn_s[wide(chunk), :]
        do = stack(do_s, chunk)
        e = jnp.exp(dot(kbf_s[...], qn, NT) * inverse) * live
        p = e * (1.0 / jnp.sum(e, 0, keepdims=True))
        pb = p.astype(BF16)
        vg_s[...] += dot(pb, do)
        pg = dot(vbf_s[...], do, NT)
        delta = jnp.sum(pb.astype(F32) * pg, 0, keepdims=True)
        ds = (p * (pg - delta)).astype(BF16)
        dsT[:, wide(chunk)] = ds
        kg_s[...] += dot(ds, qn)
        return carry

    lax.fori_loop(0, chunks, attend, 0, unroll=2)

    weighted = kg_s[...] * (inverse * kg)
    key_grad = k_scale * weighted - keys * (
        k_scale * k_scale * k_scale * jnp.mean(weighted * keys, -1, keepdims=True)
    )
    value_grad = vg_s[...]
    low_part = jnp.where(half, key_grad, pltpu.roll(value_grad, 64, 1))
    high_part = jnp.where(half, pltpu.roll(key_grad, 64, 1), value_grad)
    own_grad_s[...] = low_part * lowf + high_part * (1.0 - lowf)
    far_s[...] = (high_part * lowf + low_part * (1.0 - lowf)).astype(BF16)
    fcopy = send(far_s, farr_s.at[0], p_ss.at[1], p_rs.at[1], partner)
    ocopy = send(own_grad_s, other_grad_s, c_ss.at[4], c_rs.at[4], far_core)
    dcopy = send(far_s, farr_s.at[1], p_ss.at[2], p_rs.at[2], diagonal)

    def query_back(chunk, carry):
        xq = stack(q_s, chunk).astype(F32)
        r = lax.rsqrt(jnp.mean(xq * xq, -1, keepdims=True) + EPS)
        u = dot(dsT[:, wide(chunk)], kbf_s[...], TN) * (inverse * qg)
        m = jnp.mean(u * xq, -1, keepdims=True)
        back = (r * u - xq * (r * r * r * m)).astype(BF16)
        at = pl.ds(pl.multiple_of(chunk * CH, CH), CH)
        for h in range(heads):
            dq_s[at, h * HD:(h + 1) * HD] = back[h * CH:(h + 1) * CH]
        return carry

    drain((fcopy, ocopy, dcopy))
    lax.fori_loop(0, 3, query_back, 0)
    for part in range(4):
        shared_copy(part).wait_send()
    fcopy.wait_recv()
    g4_s[zl] = (own_grad_s[...] + farr_s[0].astype(F32)).astype(BF16)
    g = g4_s[zl]
    gz = []
    for k in (1, 2, 0):
        gz.append(send(g4_s.at[zl], g4_s.at[zl], gz_ss.at[k], gz_rs.at[k], z_to[k]))

    ocopy.wait_recv()
    dcopy.wait_recv()
    go = (other_grad_s[...] + farr_s[1].astype(F32)).astype(BF16)
    for part in range(4):
        shared_copy(part).wait_recv()

    def weight_term(step):
        for stream in (1, 0):
            c = c_of(step, stream)
            wterm[c] = (dot(featT[c, core], g) + dot(fx_s[c], go)).astype(BF16)

    def feature_term(xx):
        total = dot(wbuf[zl * X + xx].reshape(480, HD), g, NT)
        for dz in (1, 2, 3):
            src = (zl + dz) % ZL
            total += dot(w2_s[src, xx].reshape(480, HD), g4_s[src], NT)
        return total

    x2, xp, xm = (x + 2) % X, (x + 1) % X, (x + 3) % X
    xs = {}

    def x_send(name, slot, src, dst, dev):
        xs[name] = send(src, dst, x_ss.at[slot], x_rs.at[slot], dev)

    def x_start():
        for copy in gz + wc:
            copy.wait_recv()
        for xx in (x2, xp, xm):
            fterm[xx] = feature_term(xx).astype(BF16).reshape(2, 240, HD)
            if xx is x2:
                x_send("r1", 0, fterm.at[x2, 0], x1_s.at[0], x_right)
                x_send("l1", 1, fterm.at[x2, 1], x1_s.at[1], x_left)
            elif xx is xp:
                x_send("r2", 2, fterm.at[xp, 1], x2_s.at[0, 1], x_right)
            else:
                x_send("l2", 3, fterm.at[xm, 0], x2_s.at[1, 0], x_left)

    wc = []

    def w2_across():
        for dz in (1, 3, 2):
            src = (zl + dz) % ZL
            for i in range(4):
                ref = w2_s.at[src, i, core]
                pltpu.make_async_remote_copy(
                    src_ref=ref, dst_ref=ref, send_sem=zf_ss.at[0], recv_sem=zf_rs.at[src, i],
                    device_id=far_core, device_id_type=pl.DeviceIdType.MESH,
                ).wait_recv()
                wc.append(send(ref, ref, wc_ss.at[dz - 1, i], wc_rs.at[dz - 1, i], far_core))

    slots = {}
    for key in ((0, 0), (1, 1), (0, 1), (1, 0)):
        for hop in range(1, HOPS[key] + 1):
            slots[key + (hop,)] = len(slots)
    ys = {}

    def ring_send(stream, way, hop):
        step = HOPS[stream, way] - hop + 1
        c = c_of(step if way == 0 else -step, stream)
        slot = slots[stream, way, hop]
        if hop > 1:
            ys[stream, way, hop - 1].wait_recv()
            last = slots[stream, way, hop - 1]
            wterm[c] = (wterm[c].astype(F32) + yr_s[last].astype(F32)).astype(BF16)
        ys[stream, way, hop] = send(
            wterm.at[c], yr_s.at[slot], y_ss.at[slot], y_rs.at[slot],
            right if way == 0 else left,
        )

    def x_relay():
        for name, way, xx in (("r", 0, xp), ("l", 1, xm)):
            xs[name + "1"].wait_recv()
            fterm[xx, way] = (
                fterm[xx, way].astype(F32) + x1_s[way].astype(F32)).astype(BF16)
            x_send(name + "3", 4 + way, fterm.at[xx, way], x2_s.at[way, way],
                   x_right if way == 0 else x_left)

    def ring_hop(hop):
        for stream, way in ((1, 1), (1, 0), (0, 0), (0, 1)):
            if hop <= HOPS[stream, way]:
                ring_send(stream, way, hop)

    def final_rows(stream):
        c = c_of(0, stream)
        total = wterm[c].astype(F32)
        for way in (0, 1):
            hop = HOPS[stream, way]
            ys[stream, way, hop].wait_recv()
            total += yr_s[slots[stream, way, hop]].astype(F32)
        return total

    weight_term(4)
    ring_send(1, 1, 1)
    ring_send(0, 0, 1)
    weight_term(3)
    ring_send(1, 0, 1)
    weight_term(5)
    ring_send(0, 1, 1)
    def later_terms(j, carry):
        weight_term(6 + j)
        return carry

    lax.fori_loop(0, 5, later_terms, 0)
    ring_hop(2)
    w2_across()
    ring_hop(3)
    x_start()
    ring_hop(4)
    x_relay()
    hz_s[...] = final_rows(1).astype(BF16)
    hcopy = send(hz_s, hzr_s, h_ss, h_rs, far_z)
    own_term = feature_term(x)
    lax.fori_loop(3, chunks, query_back, 0)
    for name in ("r2", "l2", "r3", "l3"):
        xs[name].wait_recv()
    own_term += x2_s[0].reshape(480, HD).astype(F32) + x2_s[1].reshape(480, HD).astype(F32)
    ft_s[...] = own_term.astype(BF16)
    outs = [
        pltpu.make_async_copy(dq_s, dq_hbm, loc_sem.at[7]),
        pltpu.make_async_copy(ft_s, ft_hbm, loc_sem.at[8]),
        pltpu.make_async_copy(kgw_s, kgw_hbm, loc_sem.at[9]),
        pltpu.make_async_copy(vgw_s, vgw_hbm, loc_sem.at[10]),
    ]
    outs[0].start()
    outs[1].start()

    own_rows = final_rows(0)
    drain((hcopy,))
    for dz in (1, 2, 3):
        for i in range(4):
            z_copy(4 * ((zl + dz) % ZL) + i)[1].wait_send()
    hcopy.wait_recv()
    own_rows += hzr_s[...].astype(F32)
    padded = jnp.concatenate((own_rows, jnp.zeros((256 - rows, HD), F32)), 0)
    turned = jnp.transpose(padded)
    kgw_s[...] = turned[:64, :rows]
    vgw_s[...] = turned[64:, :rows]
    outs[2].start()
    outs[3].start()
    drain()
    for copy in outs:
        copy.wait()


def copy_out(a, b, c, e, a_out, b_out, c_out, e_out, a_s, b_s, c_s, e_s, in_sems, out_sems):
    refs = [(b, b_s, b_out), (c, c_s, c_out), (e, e_s, e_out)]
    step = a_s.shape[0] // 4
    for i in range(4):
        at = pl.ds(i * step, step)
        refs.append((a.at[at], a_s.at[at], a_out.at[at]))
    loads = [
        pltpu.make_async_copy(src, mid, in_sems.at[i]) for i, (src, mid, dst) in enumerate(refs)
    ]
    stores = [
        pltpu.make_async_copy(mid, dst, out_sems.at[i]) for i, (src, mid, dst) in enumerate(refs)
    ]
    for copy in loads:
        copy.start()
    for load, store in zip(loads, stores):
        load.wait()
        store.start()
    for copy in stores:
        copy.wait()


def shards(
    queries, features, key_weight, value_weight, query_gain, key_gain, out_grad, tile_counts
):
    samples, own_rows, feature_width = features.shape
    tokens, q_width = queries.shape
    rows, column_half = key_weight.shape
    anyspec = pl.BlockSpec(memory_space=pl.ANY)
    dma = pltpu.SemaphoreType.DMA
    piece = (rows, HD)
    scratch = [
        pltpu.VMEM((tokens, q_width), BF16),
        pltpu.VMEM((tokens, q_width), BF16),
        pltpu.VMEM((tokens, q_width), BF16),
        pltpu.VMEM((own_rows, feature_width), BF16),
        pltpu.VMEM((16, 2) + piece, BF16),
        pltpu.VMEM((16, 2) + piece, BF16),
        pltpu.VMEM((HD, tokens * q_width // HD), BF16),
        pltpu.VMEM((tokens * q_width // HD, HD), BF16),
        pltpu.VMEM((ZL, X, 2) + piece, BF16),
    ]
    scratch += [pltpu.VMEM((HD, HD), BF16)] * 5
    scratch += [
        pltpu.VMEM((2, HD, HD), BF16),
        pltpu.VMEM((ZL, HD, HD), BF16),
        pltpu.VMEM((HD, HD), F32),
        pltpu.VMEM((HD, HD), F32),
        pltpu.VMEM((X, 2) + piece, BF16),
        pltpu.VMEM((16,) + piece, BF16),
        pltpu.VMEM((16,) + piece, BF16),
        pltpu.VMEM((14,) + piece, BF16),
        pltpu.VMEM((2,) + piece, BF16),
        pltpu.VMEM((2, 2) + piece, BF16),
        pltpu.VMEM(piece, BF16),
        pltpu.VMEM(piece, BF16),
        pltpu.VMEM((HD, HD), F32),
        pltpu.VMEM((HD, HD), F32),
        pltpu.VMEM((column_half, rows), BF16),
        pltpu.VMEM((column_half, rows), BF16),
        pltpu.VMEM((1, HD), F32),
        pltpu.VMEM((1, HD), F32),
        pltpu.VMEM((2 * rows, own_rows), BF16),
        pltpu.VMEM((column_half, rows), F32),
        pltpu.VMEM((column_half, rows), F32),
        dma((11,)),
        dma((3, 2, 4)), dma((3, 2, 4)), dma((2,)), dma((2,)), dma((24,)), dma((24,)), dma((3,)), dma((3,)),
        dma((8,)), dma((8,)), dma((14,)), dma((14,)), dma((6,)), dma((6,)),
        dma((16,)), dma((4, 4)), dma((3, 4)), dma((3, 4)), dma((3,)), dma((3,)), dma, dma,
    ]
    out_shape = (
        jax.ShapeDtypeStruct((tokens, q_width), BF16),
        jax.ShapeDtypeStruct((2 * rows, own_rows), BF16),
        jax.ShapeDtypeStruct((column_half, rows), F32),
        jax.ShapeDtypeStruct((column_half, rows), F32),
    )
    results = pl.pallas_call(
        kernel,
        out_shape=out_shape,
        in_specs=[pl.BlockSpec(memory_space=pltpu.SMEM)] + [anyspec] * 7,
        out_specs=(anyspec,) * 4,
        scratch_shapes=scratch,
        compiler_params=pltpu.CompilerParams(
            collective_id=0, has_side_effects=True, vmem_limit_bytes=62 * 1024 * 1024
        ),
        cost_estimate=pl.CostEstimate(
            flops=1600000000, bytes_accessed=8000000, transcendentals=500000
        ),
    )(
        tile_counts, queries, features.reshape(own_rows, feature_width), key_weight.T,
        value_weight.T, query_gain.reshape(1, HD), key_gain.reshape(1, HD), out_grad,
    )
    query_grad, feature_t, key_t, value_t = pl.pallas_call(
        copy_out,
        out_shape=out_shape,
        in_specs=[anyspec] * 4,
        out_specs=(anyspec,) * 4,
        scratch_shapes=[pltpu.VMEM(o.shape, o.dtype) for o in out_shape] + [dma((7,)), dma((7,))],
        compiler_params=pltpu.CompilerParams(vmem_limit_bytes=62 * 1024 * 1024),
        cost_estimate=pl.CostEstimate(flops=0, bytes_accessed=3000000, transcendentals=0),
    )(*results)
    return (query_grad, feature_t.T.reshape(samples, own_rows, 2 * rows), key_t.T, value_t.T)


def solution(mesh):
    placed = (
        P("dp", "tensor"),
        P("dp", None, None),
        P("dp", "tensor"),
        P("dp", "tensor"),
        P(),
        P(),
        P("dp", "tensor"),
        P("dp"),
    )
    return jax.shard_map(
        shards,
        mesh=mesh,
        in_specs=placed,
        out_specs=(
            P("dp", "tensor"),
            P("dp", None, "tensor"),
            P("dp", "tensor"),
            P("dp", "tensor"),
        ),
        check_vma=False,
    )
```

```python
import functools
import math

import jax
import jax.numpy as jnp
from jax import lax
from jax.experimental import pallas as pl
from jax.experimental.pallas import tpu as pltpu
from jax.sharding import PartitionSpec as P

TILE_ROWS = 32
EPS = 1e-05
HD = 128
Y, X, ZL = 8, 4, 4
CH = 160
HOPS = {(0, 0): 4, (0, 1): 3, (1, 0): 3, (1, 1): 4}
PIECES = ((0, 240), (0, 128), (128, 112))
F32 = jnp.float32
BF16 = jnp.bfloat16
NT = (((1,), (1,)), ((), ()))
TN = (((0,), (0,)), ((), ()))


def dot(a, b, dims=(((1,), (0,)), ((), ()))):
    return lax.dot_general(a, b, dims, preferred_element_type=F32)


def kernel(
    tc_ref, q_hbm, feat_hbm, kwt_hbm, vwt_hbm, qg_hbm, kg_hbm, do_hbm,
    dq_hbm, ft_hbm, kgw_hbm, vgw_hbm,
    q_s, do_s, dq_s, feat_s, featT, wbuf, dsT, qn_s, w2_s, own_s, par_s, kbf_s, vbf_s, far_s,
    farr_s, g4_s, own_grad_s, other_grad_s, fterm, wterm, fx_s, yr_s, x1_s, x2_s, hz_s, hzr_s, vg_s, kg_s,
    kwt_s, vwt_s, qg_s, kg_in_s, ft_s, kgw_s, vgw_s,
    loc_sem, ag_ss, ag_rs, agz_ss, agz_rs, agc_ss, agc_rs, p_ss, p_rs,
    c_ss, c_rs, y_ss, y_rs, x_ss, x_rs, zf_ss, zf_rs, wc_ss, wc_rs, gz_ss, gz_rs, h_ss, h_rs,
):
    d = lax.axis_index("dp")
    t = lax.axis_index("tensor")
    y, zh, core = d // 4, (d // 2) % 2, d % 2
    zl, x = t // 4, t % 4
    low = (t % 2) == 0

    def at_y(step):
        return (((y + step + Y) % Y) * 4 + zh * 2 + core, t)

    right, left = at_y(1), at_y(-1)
    far_core = (d + 1 - 2 * core, t)
    far_z = (d + 2 - 4 * zh, t)
    partner = (d, t + 1 - 2 * (t % 2))
    diagonal = (d + 1 - 2 * core, t + 1 - 2 * (t % 2))
    x_right = (d, zl * 4 + (x + 1) % X)
    x_left = (d, zl * 4 + (x + X - 1) % X)
    z_to = [(d, ((zl + k) % ZL) * 4 + x) for k in (1, 2, 3)]

    barrier = pltpu.get_barrier_semaphore()
    peers = [right, left, far_core, far_z, x_right, x_left, diagonal] + z_to
    for peer in peers:
        pl.semaphore_signal(barrier, inc=1, device_id=peer, device_id_type=pl.DeviceIdType.MESH)

    tokens = q_s.shape[0]
    heads = q_s.shape[1] // HD
    width = CH * heads
    chunks = tokens // CH
    fetched = (
        (kwt_hbm, kwt_s), (vwt_hbm, vwt_s), (feat_hbm, feat_s), (q_hbm, q_s), (do_hbm, do_s),
        (qg_hbm, qg_s), (kg_hbm, kg_in_s),
    )
    copies = [
        pltpu.make_async_copy(src, dst, loc_sem.at[i]) for i, (src, dst) in enumerate(fetched)
    ]
    for copy in copies:
        copy.start()

    sent = []

    def drain(later=()):
        kept = [copy for copy in sent if any(copy is one for one in later)]
        for copy in sent:
            if not any(copy is one for one in later):
                copy.wait_send()
        sent[:] = kept

    def send(src, dst, ssem, rsem, dev):
        copy = pltpu.make_async_remote_copy(
            src_ref=src, dst_ref=dst, send_sem=ssem, recv_sem=rsem,
            device_id=dev, device_id_type=pl.DeviceIdType.MESH,
        )
        copy.start()
        sent.append(copy)
        return copy

    copies[0].wait()
    copies[1].wait()
    shard = jnp.concatenate((kwt_s[...], vwt_s[...]), 0).astype(F32)
    rows = shard.shape[1]
    shard = jnp.concatenate((shard, jnp.zeros((HD, 256 - rows), F32)), 1)
    mine = 2 * y + zh
    wbuf[mine, core] = jnp.transpose(shard)[:rows].astype(BF16)

    pl.semaphore_wait(barrier, len(peers))

    def c_of(step, stream):
        zz = zh if stream == 0 else 1 - zh
        return 2 * ((y + step + Y) % Y) + zz

    def piece_of(c, part):
        return wbuf.at[c, core, pl.ds(*PIECES[part])]

    def gather_send(part, way, hop):
        c = c_of((1 - hop) if way == 0 else (hop - 1), min(part, 1))
        ref = piece_of(c, part)
        return send(ref, ref, ag_ss.at[part, way, hop - 1], ag_rs.at[part, way, hop - 1],
                    right if way == 0 else left)

    across = []

    def core_send(c, part):
        ref = piece_of(c, part)
        i = len(across)
        across.append(send(ref, ref, agc_ss.at[i], agc_rs.at[i], far_core))

    def z_copy(c):
        dest = c // ZL
        return dest, pltpu.make_async_remote_copy(
            src_ref=wbuf.at[c, core], dst_ref=w2_s.at[zl, c % ZL, core],
            send_sem=zf_ss.at[c], recv_sem=zf_rs.at[zl, c % ZL],
            device_id=(d, dest * X + x), device_id_type=pl.DeviceIdType.MESH,
        )

    def z_send(c):
        dest, copy = z_copy(c)

        @pl.when(dest != zl)
        def _():
            copy.start()

    ag = {}
    zcopies = {}
    for part in (1, 2):
        ref = piece_of(mine, part)
        zcopies[part] = send(ref, ref, agz_ss.at[part - 1], agz_rs.at[part - 1], far_z)
    for way in (0, 1):
        ag[0, way, 1] = gather_send(0, way, 1)
    core_send(mine, 0)

    copies[2].wait()
    copies[3].wait()
    copies[5].wait()
    copies[6].wait()
    inverse = 1.0 / math.sqrt(HD)
    qg = qg_s[...]
    kg = kg_in_s[...]

    def shared_copy(part):
        group = pl.ds(part * 4, 4)
        return pltpu.make_async_remote_copy(
            src_ref=featT.at[group, 1 - core], dst_ref=fx_s.at[group],
            send_sem=c_ss.at[part], recv_sem=c_rs.at[part],
            device_id=far_core, device_id_type=pl.DeviceIdType.MESH,
        )

    def transpose_part(part, carry):
        cols = feat_s[:, pl.ds(pl.multiple_of(part * 1920, 1920), 1920)]
        featT[pl.ds(part * 4, 4)] = jnp.transpose(cols).reshape(4, 2, 240, HD)
        return carry

    def stack(ref, chunk):
        at = pl.ds(pl.multiple_of(chunk * CH, CH), CH)
        return jnp.concatenate([ref[at, h * HD:(h + 1) * HD] for h in range(heads)], 0)

    def wide(chunk):
        return pl.ds(pl.multiple_of(chunk * width, width), width)

    def query_norm(chunk, carry):
        xq = stack(q_s, chunk).astype(F32)
        r = lax.rsqrt(jnp.mean(xq * xq, -1, keepdims=True) + EPS)
        qn_s[wide(chunk), :] = (xq * r * qg).astype(BF16)
        return carry

    def gather_step(part, hop):
        for way in (1, 0):
            if hop > HOPS[min(part, 1), way]:
                continue
            ag[part, way, hop].wait_recv()
            if hop < HOPS[min(part, 1), way]:
                ag[part, way, hop + 1] = gather_send(part, way, hop + 1)
            c = c_of(-hop if way == 0 else hop, min(part, 1))
            core_send(c, part)
            if part == 2 or (part == 0 and hop > 1):
                z_send(c)

    arrived = 0
    marks = []

    def project(part, total):
        at = (y // 2 + part) % 4
        cols = feat_s[:, pl.ds(pl.multiple_of(at * 1920, 1920), 1920)]
        return total + dot(cols, wbuf[pl.ds(4 * at, 4)].reshape(1920, HD))

    proj = jnp.zeros((HD, HD), F32)
    for hop in range(1, 6):
        if hop <= 4:
            gather_step(0, hop)
        if hop == 1:
            for part in (1, 2):
                zcopies[part].wait_recv()
                for way in (1, 0):
                    ag[part, way, 1] = gather_send(part, way, 1)
                core_send(c_of(0, 1), part)
            for c in (mine, c_of(-1, 0), c_of(1, 0), c_of(0, 1)):
                z_send(c)
        else:
            gather_step(1, hop - 1)
            gather_step(2, hop - 1)
        if hop <= 4:
            transpose_part(hop - 1, 0)
            query_norm(hop - 1, 0)
        marks.append(len(across))
        if hop >= 4:
            for mark, first_part, end_part in {4: ((2, 4, 5),), 5: ((3, 5, 6), (3, 7, 8), (4, 6, 7))}[hop]:
                for copy in across[arrived:marks[mark]]:
                    copy.wait_recv()
                arrived = max(arrived, marks[mark])
                for part in range(first_part, end_part):
                    proj = project(part, proj)
    own_s[...] = proj.astype(BF16)
    pcopy = send(own_s, par_s, p_ss.at[0], p_rs.at[0], partner)
    for part in range(4):
        shared_copy(part).start()
    copies[4].wait()
    lax.fori_loop(4, chunks, query_norm, 0)
    lane = lax.broadcasted_iota(jnp.int32, (HD, HD), 1)
    half = lane < 64
    lowf = jnp.where(low, 1.0, 0.0).astype(F32)
    own = own_s[...].astype(F32)
    pcopy.wait_recv()
    other = par_s[...].astype(F32)
    first = own * lowf + other * (1.0 - lowf)
    second = other * lowf + own * (1.0 - lowf)
    keys = jnp.where(half, first, pltpu.roll(second, 64, 1))
    values = jnp.where(half, pltpu.roll(first, 64, 1), second)
    k_scale = lax.rsqrt(jnp.mean(keys * keys, -1, keepdims=True) + EPS)
    kbf_s[...] = (keys * k_scale * kg).astype(BF16)
    vbf_s[...] = values.astype(BF16)
    live = (
        lax.broadcasted_iota(jnp.int32, (HD, 1), 0) < tc_ref[0] * TILE_ROWS
    ).astype(F32)
    vg_s[...] = jnp.zeros_like(vg_s)
    kg_s[...] = jnp.zeros_like(kg_s)

    def attend(chunk, carry):
        qn = qn_s[wide(chunk), :]
        do = stack(do_s, chunk)
        e = jnp.exp(dot(kbf_s[...], qn, NT) * inverse) * live
        p = e * (1.0 / jnp.sum(e, 0, keepdims=True))
        pb = p.astype(BF16)
        vg_s[...] += dot(pb, do)
        pg = dot(vbf_s[...], do, NT)
        delta = jnp.sum(pb.astype(F32) * pg, 0, keepdims=True)
        ds = (p * (pg - delta)).astype(BF16)
        dsT[:, wide(chunk)] = ds
        kg_s[...] += dot(ds, qn)
        return carry

    lax.fori_loop(0, chunks, attend, 0, unroll=2)

    weighted = kg_s[...] * (inverse * kg)
    key_grad = k_scale * weighted - keys * (
        k_scale * k_scale * k_scale * jnp.mean(weighted * keys, -1, keepdims=True)
    )
    value_grad = vg_s[...]
    low_part = jnp.where(half, key_grad, pltpu.roll(value_grad, 64, 1))
    high_part = jnp.where(half, pltpu.roll(key_grad, 64, 1), value_grad)
    own_grad_s[...] = low_part * lowf + high_part * (1.0 - lowf)
    far_s[...] = (high_part * lowf + low_part * (1.0 - lowf)).astype(BF16)
    fcopy = send(far_s, farr_s.at[0], p_ss.at[1], p_rs.at[1], partner)
    ocopy = send(own_grad_s, other_grad_s, c_ss.at[4], c_rs.at[4], far_core)
    dcopy = send(far_s, farr_s.at[1], p_ss.at[2], p_rs.at[2], diagonal)

    def query_back(chunk, carry):
        xq = stack(q_s, chunk).astype(F32)
        r = lax.rsqrt(jnp.mean(xq * xq, -1, keepdims=True) + EPS)
        u = dot(dsT[:, wide(chunk)], kbf_s[...], TN) * (inverse * qg)
        m = jnp.mean(u * xq, -1, keepdims=True)
        back = (r * u - xq * (r * r * r * m)).astype(BF16)
        at = pl.ds(pl.multiple_of(chunk * CH, CH), CH)
        for h in range(heads):
            dq_s[at, h * HD:(h + 1) * HD] = back[h * CH:(h + 1) * CH]
        return carry

    drain((fcopy, ocopy, dcopy))
    lax.fori_loop(0, 3, query_back, 0)
    for part in range(4):
        shared_copy(part).wait_send()
    fcopy.wait_recv()
    g4_s[zl] = (own_grad_s[...] + farr_s[0].astype(F32)).astype(BF16)
    g = g4_s[zl]
    gz = []
    for k in (1, 2, 0):
        gz.append(send(g4_s.at[zl], g4_s.at[zl], gz_ss.at[k], gz_rs.at[k], z_to[k]))

    ocopy.wait_recv()
    dcopy.wait_recv()
    go = (other_grad_s[...] + farr_s[1].astype(F32)).astype(BF16)
    for part in range(4):
        shared_copy(part).wait_recv()

    def weight_term(step):
        for stream in (1, 0):
            c = c_of(step, stream)
            wterm[c] = (dot(featT[c, core], g) + dot(fx_s[c], go)).astype(BF16)

    def feature_term(xx):
        total = dot(wbuf[zl * X + xx].reshape(480, HD), g, NT)
        for dz in (1, 2, 3):
            src = (zl + dz) % ZL
            total += dot(w2_s[src, xx].reshape(480, HD), g4_s[src], NT)
        return total

    x2, xp, xm = (x + 2) % X, (x + 1) % X, (x + 3) % X
    xs = {}

    def x_send(name, slot, src, dst, dev):
        xs[name] = send(src, dst, x_ss.at[slot], x_rs.at[slot], dev)

    def x_start():
        for copy in gz + wc:
            copy.wait_recv()
        for xx in (x2, xp, xm):
            fterm[xx] = feature_term(xx).astype(BF16).reshape(2, 240, HD)
            if xx is x2:
                x_send("r1", 0, fterm.at[x2, 0], x1_s.at[0], x_right)
                x_send("l1", 1, fterm.at[x2, 1], x1_s.at[1], x_left)
            elif xx is xp:
                x_send("r2", 2, fterm.at[xp, 1], x2_s.at[0, 1], x_right)
            else:
                x_send("l2", 3, fterm.at[xm, 0], x2_s.at[1, 0], x_left)

    wc = []

    def w2_across():
        for dz in (1, 3, 2):
            src = (zl + dz) % ZL
            for i in range(4):
                ref = w2_s.at[src, i, core]
                pltpu.make_async_remote_copy(
                    src_ref=ref, dst_ref=ref, send_sem=zf_ss.at[0], recv_sem=zf_rs.at[src, i],
                    device_id=far_core, device_id_type=pl.DeviceIdType.MESH,
                ).wait_recv()
                wc.append(send(ref, ref, wc_ss.at[dz - 1, i], wc_rs.at[dz - 1, i], far_core))

    slots = {}
    for part in range(3):
        for way in (0, 1):
            for hop in range(1, HOPS[min(part, 1), way] + 1):
                slots[part, way, hop] = len(slots)
    ys = {}

    def ring_send(part, way, hop):
        stream = min(part, 1)
        step = HOPS[stream, way] - hop + 1
        c = c_of(step if way == 0 else -step, stream)
        slot = slots[part, way, hop]
        at = pl.ds(*PIECES[part])
        count = PIECES[part][1]
        if hop > 1:
            ys[part, way, hop - 1].wait_recv()
            last = slots[part, way, hop - 1]
            wterm[c, at] = (
                wterm[c, at].astype(F32) + yr_s[last, :count].astype(F32)
            ).astype(BF16)
        ys[part, way, hop] = send(
            wterm.at[c, at], yr_s.at[slot, pl.ds(0, count)], y_ss.at[slot], y_rs.at[slot],
            right if way == 0 else left,
        )

    def ring_hop(hop):
        for part, way in ((1, 1), (1, 0), (2, 1), (2, 0), (0, 0), (0, 1)):
            if hop <= HOPS[min(part, 1), way]:
                ring_send(part, way, hop)

    def x_relay():
        for name, way, xx in (("r", 0, xp), ("l", 1, xm)):
            xs[name + "1"].wait_recv()
            fterm[xx, way] = (
                fterm[xx, way].astype(F32) + x1_s[way].astype(F32)).astype(BF16)
            x_send(name + "3", 4 + way, fterm.at[xx, way], x2_s.at[way, way],
                   x_right if way == 0 else x_left)

    def final_rows(part):
        at = pl.ds(*PIECES[part])
        total = wterm[c_of(0, min(part, 1)), at].astype(F32)
        for way in (0, 1):
            last = part, way, HOPS[min(part, 1), way]
            ys[last].wait_recv()
            total += yr_s[slots[last], :PIECES[part][1]].astype(F32)
        return total

    weight_term(4)
    ring_send(1, 1, 1)
    ring_send(2, 1, 1)
    ring_send(0, 0, 1)
    weight_term(3)
    ring_send(1, 0, 1)
    ring_send(2, 0, 1)
    weight_term(5)
    ring_send(0, 1, 1)

    def later_terms(j, carry):
        weight_term(6 + j)
        return carry

    lax.fori_loop(0, 5, later_terms, 0)
    ring_hop(2)
    w2_across()
    ring_hop(3)
    x_start()
    ring_hop(4)
    x_relay()
    hcopies = []
    for part in (1, 2):
        at = pl.ds(*PIECES[part])
        hz_s[at] = final_rows(part).astype(BF16)
        hcopies.append(
            send(hz_s.at[at], hzr_s.at[at], h_ss.at[part - 1], h_rs.at[part - 1], far_z))
    own_term = feature_term(x)
    lax.fori_loop(3, chunks, query_back, 0)
    for name in ("r2", "l2", "r3", "l3"):
        xs[name].wait_recv()
    own_term += x2_s[0].reshape(480, HD).astype(F32) + x2_s[1].reshape(480, HD).astype(F32)
    ft_s[...] = own_term.astype(BF16)
    outs = [
        pltpu.make_async_copy(dq_s, dq_hbm, loc_sem.at[7]),
        pltpu.make_async_copy(ft_s, ft_hbm, loc_sem.at[8]),
        pltpu.make_async_copy(kgw_s, kgw_hbm, loc_sem.at[9]),
        pltpu.make_async_copy(vgw_s, vgw_hbm, loc_sem.at[10]),
    ]
    outs[0].start()
    outs[1].start()

    own_rows = final_rows(0)
    drain(hcopies)
    for dz in (1, 2, 3):
        for i in range(4):
            z_copy(4 * ((zl + dz) % ZL) + i)[1].wait_send()
    for copy in hcopies:
        copy.wait_recv()
    own_rows += hzr_s[...].astype(F32)
    padded = jnp.concatenate((own_rows, jnp.zeros((256 - rows, HD), F32)), 0)
    turned = jnp.transpose(padded)
    kgw_s[...] = turned[:64, :rows]
    vgw_s[...] = turned[64:, :rows]
    outs[2].start()
    outs[3].start()
    drain()
    for copy in outs:
        copy.wait()


def copy_out(a, b, c, e, a_out, b_out, c_out, e_out, a_s, b_s, c_s, e_s, in_sems, out_sems):
    refs = [(b, b_s, b_out), (c, c_s, c_out), (e, e_s, e_out)]
    step = a_s.shape[0] // 4
    for i in range(4):
        at = pl.ds(i * step, step)
        refs.append((a.at[at], a_s.at[at], a_out.at[at]))
    loads = [
        pltpu.make_async_copy(src, mid, in_sems.at[i]) for i, (src, mid, dst) in enumerate(refs)
    ]
    stores = [
        pltpu.make_async_copy(mid, dst, out_sems.at[i]) for i, (src, mid, dst) in enumerate(refs)
    ]
    for copy in loads:
        copy.start()
    for load, store in zip(loads, stores):
        load.wait()
        store.start()
    for copy in stores:
        copy.wait()


def shards(
    queries, features, key_weight, value_weight, query_gain, key_gain, out_grad, tile_counts
):
    samples, own_rows, feature_width = features.shape
    tokens, q_width = queries.shape
    rows, column_half = key_weight.shape
    anyspec = pl.BlockSpec(memory_space=pl.ANY)
    dma = pltpu.SemaphoreType.DMA
    piece = (rows, HD)
    scratch = [
        pltpu.VMEM((tokens, q_width), BF16),
        pltpu.VMEM((tokens, q_width), BF16),
        pltpu.VMEM((tokens, q_width), BF16),
        pltpu.VMEM((own_rows, feature_width), BF16),
        pltpu.VMEM((16, 2) + piece, BF16),
        pltpu.VMEM((16, 2) + piece, BF16),
        pltpu.VMEM((HD, tokens * q_width // HD), BF16),
        pltpu.VMEM((tokens * q_width // HD, HD), BF16),
        pltpu.VMEM((ZL, X, 2) + piece, BF16),
    ]
    scratch += [pltpu.VMEM((HD, HD), BF16)] * 5
    scratch += [
        pltpu.VMEM((2, HD, HD), BF16),
        pltpu.VMEM((ZL, HD, HD), BF16),
        pltpu.VMEM((HD, HD), F32),
        pltpu.VMEM((HD, HD), F32),
        pltpu.VMEM((X, 2) + piece, BF16),
        pltpu.VMEM((16,) + piece, BF16),
        pltpu.VMEM((16,) + piece, BF16),
        pltpu.VMEM((21,) + piece, BF16),
        pltpu.VMEM((2,) + piece, BF16),
        pltpu.VMEM((2, 2) + piece, BF16),
        pltpu.VMEM(piece, BF16),
        pltpu.VMEM(piece, BF16),
        pltpu.VMEM((HD, HD), F32),
        pltpu.VMEM((HD, HD), F32),
        pltpu.VMEM((column_half, rows), BF16),
        pltpu.VMEM((column_half, rows), BF16),
        pltpu.VMEM((1, HD), F32),
        pltpu.VMEM((1, HD), F32),
        pltpu.VMEM((2 * rows, own_rows), BF16),
        pltpu.VMEM((column_half, rows), F32),
        pltpu.VMEM((column_half, rows), F32),
        dma((11,)),
        dma((3, 2, 4)), dma((3, 2, 4)), dma((2,)), dma((2,)), dma((24,)), dma((24,)), dma((3,)), dma((3,)),
        dma((8,)), dma((8,)), dma((21,)), dma((21,)), dma((6,)), dma((6,)),
        dma((16,)), dma((4, 4)), dma((3, 4)), dma((3, 4)), dma((3,)), dma((3,)), dma((2,)), dma((2,)),
    ]
    out_shape = (
        jax.ShapeDtypeStruct((tokens, q_width), BF16),
        jax.ShapeDtypeStruct((2 * rows, own_rows), BF16),
        jax.ShapeDtypeStruct((column_half, rows), F32),
        jax.ShapeDtypeStruct((column_half, rows), F32),
    )
    results = pl.pallas_call(
        kernel,
        out_shape=out_shape,
        in_specs=[pl.BlockSpec(memory_space=pltpu.SMEM)] + [anyspec] * 7,
        out_specs=(anyspec,) * 4,
        scratch_shapes=scratch,
        compiler_params=pltpu.CompilerParams(
            collective_id=0, has_side_effects=True, vmem_limit_bytes=62 * 1024 * 1024
        ),
        cost_estimate=pl.CostEstimate(
            flops=1600000000, bytes_accessed=8000000, transcendentals=500000
        ),
    )(
        tile_counts, queries, features.reshape(own_rows, feature_width), key_weight.T,
        value_weight.T, query_gain.reshape(1, HD), key_gain.reshape(1, HD), out_grad,
    )
    query_grad, feature_t, key_t, value_t = pl.pallas_call(
        copy_out,
        out_shape=out_shape,
        in_specs=[anyspec] * 4,
        out_specs=(anyspec,) * 4,
        scratch_shapes=[pltpu.VMEM(o.shape, o.dtype) for o in out_shape] + [dma((7,)), dma((7,))],
        compiler_params=pltpu.CompilerParams(vmem_limit_bytes=62 * 1024 * 1024),
        cost_estimate=pl.CostEstimate(flops=0, bytes_accessed=3000000, transcendentals=0),
    )(*results)
    return (query_grad, feature_t.T.reshape(samples, own_rows, 2 * rows), key_t.T, value_t.T)


def solution(mesh):
    placed = (
        P("dp", "tensor"),
        P("dp", None, None),
        P("dp", "tensor"),
        P("dp", "tensor"),
        P(),
        P(),
        P("dp", "tensor"),
        P("dp"),
    )
    return jax.shard_map(
        shards,
        mesh=mesh,
        in_specs=placed,
        out_specs=(
            P("dp", "tensor"),
            P("dp", None, "tensor"),
            P("dp", "tensor"),
            P("dp", "tensor"),
        ),
        check_vma=False,
    )
```

```python
import functools
import math

import jax
import jax.numpy as jnp
from jax import lax
from jax.experimental import pallas as pl
from jax.experimental.pallas import tpu as pltpu
from jax.sharding import PartitionSpec as P

TILE_ROWS = 32
EPS = 1e-05
HD = 128
Y, X, ZL = 8, 4, 4
CH = 160
HOPS = {(0, 0): 4, (0, 1): 3, (1, 0): 3, (1, 1): 4}
PIECES = ((0, 240), (0, 128), (128, 112))
F32 = jnp.float32
BF16 = jnp.bfloat16
NT = (((1,), (1,)), ((), ()))
TN = (((0,), (0,)), ((), ()))


def dot(a, b, dims=(((1,), (0,)), ((), ()))):
    return lax.dot_general(a, b, dims, preferred_element_type=F32)


def kernel(
    tc_ref, q_hbm, feat_hbm, kwt_hbm, vwt_hbm, qg_hbm, kg_hbm, do_hbm,
    dq_hbm, ft_hbm, kgw_hbm, vgw_hbm,
    q_s, do_s, dq_s, feat_s, featT, wbuf, dsT, qn_s, w2_s, own_s, par_s, kbf_s, vbf_s, far_s,
    farr_s, g4_s, own_grad_s, other_grad_s, fterm, wterm, fx_s, yr_s, x1_s, x2_s, hz_s, hzr_s, vg_s, kg_s,
    kwt_s, vwt_s, qg_s, kg_in_s, ft_s, kgw_s, vgw_s,
    loc_sem, ag_ss, ag_rs, agz_ss, agz_rs, agc_ss, agc_rs, p_ss, p_rs,
    c_ss, c_rs, y_ss, y_rs, x_ss, x_rs, zf_ss, zf_rs, wc_ss, wc_rs, gz_ss, gz_rs, h_ss, h_rs,
):
    d = lax.axis_index("dp")
    t = lax.axis_index("tensor")
    y, zh, core = d // 4, (d // 2) % 2, d % 2
    zl, x = t // 4, t % 4
    low = (t % 2) == 0

    def at_y(step):
        return (((y + step + Y) % Y) * 4 + zh * 2 + core, t)

    right, left = at_y(1), at_y(-1)
    far_core = (d + 1 - 2 * core, t)
    far_z = (d + 2 - 4 * zh, t)
    partner = (d, t + 1 - 2 * (t % 2))
    diagonal = (d + 1 - 2 * core, t + 1 - 2 * (t % 2))
    x_right = (d, zl * 4 + (x + 1) % X)
    x_left = (d, zl * 4 + (x + X - 1) % X)
    z_to = [(d, ((zl + k) % ZL) * 4 + x) for k in (1, 2, 3)]

    barrier = pltpu.get_barrier_semaphore()
    peers = [right, left, far_core, far_z, x_right, x_left, diagonal] + z_to
    for peer in peers:
        pl.semaphore_signal(barrier, inc=1, device_id=peer, device_id_type=pl.DeviceIdType.MESH)

    tokens = q_s.shape[0]
    heads = q_s.shape[1] // HD
    width = CH * heads
    chunks = tokens // CH
    fetched = (
        (kwt_hbm, kwt_s), (vwt_hbm, vwt_s), (feat_hbm, feat_s), (q_hbm, q_s), (do_hbm, do_s),
        (qg_hbm, qg_s), (kg_hbm, kg_in_s),
    )
    copies = [
        pltpu.make_async_copy(src, dst, loc_sem.at[i]) for i, (src, dst) in enumerate(fetched)
    ]
    for copy in copies:
        copy.start()

    sent = []

    def drain(later=()):
        kept = [copy for copy in sent if any(copy is one for one in later)]
        for copy in sent:
            if not any(copy is one for one in later):
                copy.wait_send()
        sent[:] = kept

    def send(src, dst, ssem, rsem, dev):
        copy = pltpu.make_async_remote_copy(
            src_ref=src, dst_ref=dst, send_sem=ssem, recv_sem=rsem,
            device_id=dev, device_id_type=pl.DeviceIdType.MESH,
        )
        copy.start()
        sent.append(copy)
        return copy

    copies[0].wait()
    copies[1].wait()
    shard = jnp.concatenate((kwt_s[...], vwt_s[...]), 0).astype(F32)
    rows = shard.shape[1]
    shard = jnp.concatenate((shard, jnp.zeros((HD, 256 - rows), F32)), 1)
    mine = 2 * y + zh
    wbuf[mine, core] = jnp.transpose(shard)[:rows].astype(BF16)

    pl.semaphore_wait(barrier, len(peers))

    def c_of(step, stream):
        zz = zh if stream == 0 else 1 - zh
        return 2 * ((y + step + Y) % Y) + zz

    def piece_of(c, part):
        return wbuf.at[c, core, pl.ds(*PIECES[part])]

    def gather_send(part, way, hop):
        c = c_of((1 - hop) if way == 0 else (hop - 1), min(part, 1))
        ref = piece_of(c, part)
        return send(ref, ref, ag_ss.at[part, way, hop - 1], ag_rs.at[part, way, hop - 1],
                    right if way == 0 else left)

    across = []

    def core_send(c, part):
        ref = piece_of(c, part)
        i = len(across)
        across.append(send(ref, ref, agc_ss.at[i], agc_rs.at[i], far_core))

    def z_copy(c):
        dest = c // ZL
        return dest, pltpu.make_async_remote_copy(
            src_ref=wbuf.at[c, core], dst_ref=w2_s.at[zl, c % ZL, core],
            send_sem=zf_ss.at[c], recv_sem=zf_rs.at[zl, c % ZL],
            device_id=(d, dest * X + x), device_id_type=pl.DeviceIdType.MESH,
        )

    def z_send(c):
        dest, copy = z_copy(c)

        @pl.when(dest != zl)
        def _():
            copy.start()

    ag = {}
    zcopies = {}
    for part in (1, 2):
        ref = piece_of(mine, part)
        zcopies[part] = send(ref, ref, agz_ss.at[part - 1], agz_rs.at[part - 1], far_z)
    for way in (0, 1):
        ag[0, way, 1] = gather_send(0, way, 1)
    core_send(mine, 0)

    copies[2].wait()
    copies[3].wait()
    copies[5].wait()
    copies[6].wait()
    inverse = 1.0 / math.sqrt(HD)
    qg = qg_s[...]
    kg = kg_in_s[...]

    def shared_copy(part):
        group = pl.ds(part * 4, 4)
        return pltpu.make_async_remote_copy(
            src_ref=featT.at[group, 1 - core], dst_ref=fx_s.at[group],
            send_sem=c_ss.at[part], recv_sem=c_rs.at[part],
            device_id=far_core, device_id_type=pl.DeviceIdType.MESH,
        )

    def transpose_part(part, carry):
        cols = feat_s[:, pl.ds(pl.multiple_of(part * 1920, 1920), 1920)]
        featT[pl.ds(part * 4, 4)] = jnp.transpose(cols).reshape(4, 2, 240, HD)
        return carry

    def stack(ref, chunk):
        at = pl.ds(pl.multiple_of(chunk * CH, CH), CH)
        return jnp.concatenate([ref[at, h * HD:(h + 1) * HD] for h in range(heads)], 0)

    def wide(chunk):
        return pl.ds(pl.multiple_of(chunk * width, width), width)

    def query_norm(chunk, carry):
        xq = stack(q_s, chunk).astype(F32)
        r = lax.rsqrt(jnp.mean(xq * xq, -1, keepdims=True) + EPS)
        qn_s[wide(chunk), :] = (xq * r * qg).astype(BF16)
        return carry

    def gather_step(part, hop):
        for way in (1, 0):
            if hop > HOPS[min(part, 1), way]:
                continue
            ag[part, way, hop].wait_recv()
            if hop < HOPS[min(part, 1), way]:
                ag[part, way, hop + 1] = gather_send(part, way, hop + 1)
            c = c_of(-hop if way == 0 else hop, min(part, 1))
            core_send(c, part)
            if part == 2 or (part == 0 and hop > 1):
                z_send(c)

    arrived = 0
    marks = []

    def project(part, total):
        at = (y // 2 + part) % 4
        cols = feat_s[:, pl.ds(pl.multiple_of(at * 1920, 1920), 1920)]
        return total + dot(cols, wbuf[pl.ds(4 * at, 4)].reshape(1920, HD))

    proj = jnp.zeros((HD, HD), F32)
    for hop in range(1, 6):
        if hop <= 4:
            gather_step(0, hop)
        if hop == 1:
            for part in (1, 2):
                zcopies[part].wait_recv()
                for way in (1, 0):
                    ag[part, way, 1] = gather_send(part, way, 1)
                core_send(c_of(0, 1), part)
            for c in (mine, c_of(-1, 0), c_of(1, 0), c_of(0, 1)):
                z_send(c)
        else:
            gather_step(1, hop - 1)
            gather_step(2, hop - 1)
        if hop <= 4:
            transpose_part(hop - 1, 0)
            query_norm(hop - 1, 0)
        marks.append(len(across))
        if hop >= 4:
            for mark, first_part, end_part in {4: ((2, 4, 5),), 5: ((3, 5, 6), (3, 7, 8), (4, 6, 7))}[hop]:
                for copy in across[arrived:marks[mark]]:
                    copy.wait_recv()
                arrived = max(arrived, marks[mark])
                for part in range(first_part, end_part):
                    proj = project(part, proj)
    own_s[...] = proj.astype(BF16)
    pcopy = send(own_s, par_s, p_ss.at[0], p_rs.at[0], partner)
    for part in range(4):
        shared_copy(part).start()
    copies[4].wait()
    lax.fori_loop(4, chunks, query_norm, 0)
    lane = lax.broadcasted_iota(jnp.int32, (HD, HD), 1)
    half = lane < 64
    lowf = jnp.where(low, 1.0, 0.0).astype(F32)
    own = own_s[...].astype(F32)
    pcopy.wait_recv()
    other = par_s[...].astype(F32)
    first = own * lowf + other * (1.0 - lowf)
    second = other * lowf + own * (1.0 - lowf)
    keys = jnp.where(half, first, pltpu.roll(second, 64, 1))
    values = jnp.where(half, pltpu.roll(first, 64, 1), second)
    k_scale = lax.rsqrt(jnp.mean(keys * keys, -1, keepdims=True) + EPS)
    kbf_s[...] = (keys * k_scale * kg).astype(BF16)
    vbf_s[...] = values.astype(BF16)
    live = (
        lax.broadcasted_iota(jnp.int32, (HD, 1), 0) < tc_ref[0] * TILE_ROWS
    ).astype(F32)
    vg_s[...] = jnp.zeros_like(vg_s)
    kg_s[...] = jnp.zeros_like(kg_s)

    def attend(chunk, carry):
        qn = qn_s[wide(chunk), :]
        do = stack(do_s, chunk)
        e = jnp.exp(dot(kbf_s[...], qn, NT) * inverse) * live
        p = e * (1.0 / jnp.sum(e, 0, keepdims=True))
        pb = p.astype(BF16)
        vg_s[...] += dot(pb, do)
        pg = dot(vbf_s[...], do, NT)
        delta = jnp.sum(pb.astype(F32) * pg, 0, keepdims=True)
        ds = (p * (pg - delta)).astype(BF16)
        dsT[:, wide(chunk)] = ds
        kg_s[...] += dot(ds, qn)
        return carry

    lax.fori_loop(0, chunks, attend, 0, unroll=3)

    weighted = kg_s[...] * (inverse * kg)
    key_grad = k_scale * weighted - keys * (
        k_scale * k_scale * k_scale * jnp.mean(weighted * keys, -1, keepdims=True)
    )
    value_grad = vg_s[...]
    low_part = jnp.where(half, key_grad, pltpu.roll(value_grad, 64, 1))
    high_part = jnp.where(half, pltpu.roll(key_grad, 64, 1), value_grad)
    own_grad_s[...] = low_part * lowf + high_part * (1.0 - lowf)
    far_s[...] = (high_part * lowf + low_part * (1.0 - lowf)).astype(BF16)
    fcopy = send(far_s, farr_s.at[0], p_ss.at[1], p_rs.at[1], partner)
    ocopy = send(own_grad_s, other_grad_s, c_ss.at[4], c_rs.at[4], far_core)
    dcopy = send(far_s, farr_s.at[1], p_ss.at[2], p_rs.at[2], diagonal)

    def query_back(chunk, carry):
        xq = stack(q_s, chunk).astype(F32)
        r = lax.rsqrt(jnp.mean(xq * xq, -1, keepdims=True) + EPS)
        u = dot(dsT[:, wide(chunk)], kbf_s[...], TN) * (inverse * qg)
        m = jnp.mean(u * xq, -1, keepdims=True)
        back = (r * u - xq * (r * r * r * m)).astype(BF16)
        at = pl.ds(pl.multiple_of(chunk * CH, CH), CH)
        for h in range(heads):
            dq_s[at, h * HD:(h + 1) * HD] = back[h * CH:(h + 1) * CH]
        return carry

    drain((fcopy, ocopy, dcopy))
    lax.fori_loop(0, 3, query_back, 0)
    for part in range(4):
        shared_copy(part).wait_send()
    fcopy.wait_recv()
    g4_s[zl] = (own_grad_s[...] + farr_s[0].astype(F32)).astype(BF16)
    g = g4_s[zl]
    gz = []
    for k in (1, 2, 0):
        gz.append(send(g4_s.at[zl], g4_s.at[zl], gz_ss.at[k], gz_rs.at[k], z_to[k]))

    ocopy.wait_recv()
    dcopy.wait_recv()
    go = (other_grad_s[...] + farr_s[1].astype(F32)).astype(BF16)
    for part in range(4):
        shared_copy(part).wait_recv()

    def weight_term(step):
        for stream in (1, 0):
            c = c_of(step, stream)
            wterm[c] = (dot(featT[c, core], g) + dot(fx_s[c], go)).astype(BF16)

    def feature_term(xx):
        total = dot(wbuf[zl * X + xx].reshape(480, HD), g, NT)
        for dz in (1, 2, 3):
            src = (zl + dz) % ZL
            total += dot(w2_s[src, xx].reshape(480, HD), g4_s[src], NT)
        return total

    x2, xp, xm = (x + 2) % X, (x + 1) % X, (x + 3) % X
    xs = {}

    def x_send(name, slot, src, dst, dev):
        xs[name] = send(src, dst, x_ss.at[slot], x_rs.at[slot], dev)

    def x_start():
        for copy in gz + wc:
            copy.wait_recv()
        for xx in (x2, xp, xm):
            fterm[xx] = feature_term(xx).astype(BF16).reshape(2, 240, HD)
            if xx is x2:
                x_send("r1", 0, fterm.at[x2, 0], x1_s.at[0], x_right)
                x_send("l1", 1, fterm.at[x2, 1], x1_s.at[1], x_left)
            elif xx is xp:
                x_send("r2", 2, fterm.at[xp, 1], x2_s.at[0, 1], x_right)
            else:
                x_send("l2", 3, fterm.at[xm, 0], x2_s.at[1, 0], x_left)

    wc = []

    def w2_across():
        for dz in (1, 3, 2):
            src = (zl + dz) % ZL
            for i in range(4):
                ref = w2_s.at[src, i, core]
                pltpu.make_async_remote_copy(
                    src_ref=ref, dst_ref=ref, send_sem=zf_ss.at[0], recv_sem=zf_rs.at[src, i],
                    device_id=far_core, device_id_type=pl.DeviceIdType.MESH,
                ).wait_recv()
                wc.append(send(ref, ref, wc_ss.at[dz - 1, i], wc_rs.at[dz - 1, i], far_core))

    slots = {}
    for part in range(3):
        for way in (0, 1):
            for hop in range(1, HOPS[min(part, 1), way] + 1):
                slots[part, way, hop] = len(slots)
    ys = {}

    def ring_send(part, way, hop):
        stream = min(part, 1)
        step = HOPS[stream, way] - hop + 1
        c = c_of(step if way == 0 else -step, stream)
        slot = slots[part, way, hop]
        at = pl.ds(*PIECES[part])
        count = PIECES[part][1]
        if hop > 1:
            ys[part, way, hop - 1].wait_recv()
            last = slots[part, way, hop - 1]
            wterm[c, at] = (
                wterm[c, at].astype(F32) + yr_s[last, :count].astype(F32)
            ).astype(BF16)
        ys[part, way, hop] = send(
            wterm.at[c, at], yr_s.at[slot, pl.ds(0, count)], y_ss.at[slot], y_rs.at[slot],
            right if way == 0 else left,
        )

    def ring_hop(hop):
        for part, way in ((1, 1), (1, 0), (2, 1), (2, 0), (0, 0), (0, 1)):
            if hop <= HOPS[min(part, 1), way]:
                ring_send(part, way, hop)

    def x_relay():
        for name, way, xx in (("r", 0, xp), ("l", 1, xm)):
            xs[name + "1"].wait_recv()
            fterm[xx, way] = (
                fterm[xx, way].astype(F32) + x1_s[way].astype(F32)).astype(BF16)
            x_send(name + "3", 4 + way, fterm.at[xx, way], x2_s.at[way, way],
                   x_right if way == 0 else x_left)

    def final_rows(part):
        at = pl.ds(*PIECES[part])
        total = wterm[c_of(0, min(part, 1)), at].astype(F32)
        for way in (0, 1):
            last = part, way, HOPS[min(part, 1), way]
            ys[last].wait_recv()
            total += yr_s[slots[last], :PIECES[part][1]].astype(F32)
        return total

    weight_term(4)
    ring_send(1, 1, 1)
    ring_send(2, 1, 1)
    ring_send(0, 0, 1)
    weight_term(3)
    ring_send(1, 0, 1)
    ring_send(2, 0, 1)
    weight_term(5)
    ring_send(0, 1, 1)

    def later_terms(j, carry):
        weight_term(6 + j)
        return carry

    lax.fori_loop(0, 5, later_terms, 0)
    ring_hop(2)
    ring_hop(3)
    w2_across()
    ring_hop(4)
    x_start()
    hcopies = []
    for part in (1, 2):
        at = pl.ds(*PIECES[part])
        hz_s[at] = final_rows(part).astype(BF16)
        hcopies.append(
            send(hz_s.at[at], hzr_s.at[at], h_ss.at[part - 1], h_rs.at[part - 1], far_z))
    x_relay()
    own_term = feature_term(x)
    lax.fori_loop(3, chunks, query_back, 0)
    for name in ("r2", "l2", "r3", "l3"):
        xs[name].wait_recv()
    own_term += x2_s[0].reshape(480, HD).astype(F32) + x2_s[1].reshape(480, HD).astype(F32)
    ft_s[...] = own_term.astype(BF16)
    outs = [
        pltpu.make_async_copy(dq_s, dq_hbm, loc_sem.at[7]),
        pltpu.make_async_copy(ft_s, ft_hbm, loc_sem.at[8]),
        pltpu.make_async_copy(kgw_s, kgw_hbm, loc_sem.at[9]),
        pltpu.make_async_copy(vgw_s, vgw_hbm, loc_sem.at[10]),
    ]
    outs[0].start()
    outs[1].start()

    own_rows = final_rows(0)
    drain(hcopies)
    for dz in (1, 2, 3):
        for i in range(4):
            z_copy(4 * ((zl + dz) % ZL) + i)[1].wait_send()
    for copy in hcopies:
        copy.wait_recv()
    own_rows += hzr_s[...].astype(F32)
    padded = jnp.concatenate((own_rows, jnp.zeros((256 - rows, HD), F32)), 0)
    turned = jnp.transpose(padded)
    kgw_s[...] = turned[:64, :rows]
    vgw_s[...] = turned[64:, :rows]
    outs[2].start()
    outs[3].start()
    drain()
    for copy in outs:
        copy.wait()


def copy_out(a, b, c, e, a_out, b_out, c_out, e_out, a_s, b_s, c_s, e_s, in_sems, out_sems):
    refs = [(b, b_s, b_out), (c, c_s, c_out), (e, e_s, e_out)]
    step = a_s.shape[0] // 4
    for i in range(4):
        at = pl.ds(i * step, step)
        refs.append((a.at[at], a_s.at[at], a_out.at[at]))
    loads = [
        pltpu.make_async_copy(src, mid, in_sems.at[i]) for i, (src, mid, dst) in enumerate(refs)
    ]
    stores = [
        pltpu.make_async_copy(mid, dst, out_sems.at[i]) for i, (src, mid, dst) in enumerate(refs)
    ]
    for copy in loads:
        copy.start()
    for load, store in zip(loads, stores):
        load.wait()
        store.start()
    for copy in stores:
        copy.wait()


def shards(
    queries, features, key_weight, value_weight, query_gain, key_gain, out_grad, tile_counts
):
    samples, own_rows, feature_width = features.shape
    tokens, q_width = queries.shape
    rows, column_half = key_weight.shape
    anyspec = pl.BlockSpec(memory_space=pl.ANY)
    dma = pltpu.SemaphoreType.DMA
    piece = (rows, HD)
    scratch = [
        pltpu.VMEM((tokens, q_width), BF16),
        pltpu.VMEM((tokens, q_width), BF16),
        pltpu.VMEM((tokens, q_width), BF16),
        pltpu.VMEM((own_rows, feature_width), BF16),
        pltpu.VMEM((16, 2) + piece, BF16),
        pltpu.VMEM((16, 2) + piece, BF16),
        pltpu.VMEM((HD, tokens * q_width // HD), BF16),
        pltpu.VMEM((tokens * q_width // HD, HD), BF16),
        pltpu.VMEM((ZL, X, 2) + piece, BF16),
    ]
    scratch += [pltpu.VMEM((HD, HD), BF16)] * 5
    scratch += [
        pltpu.VMEM((2, HD, HD), BF16),
        pltpu.VMEM((ZL, HD, HD), BF16),
        pltpu.VMEM((HD, HD), F32),
        pltpu.VMEM((HD, HD), F32),
        pltpu.VMEM((X, 2) + piece, BF16),
        pltpu.VMEM((16,) + piece, BF16),
        pltpu.VMEM((16,) + piece, BF16),
        pltpu.VMEM((21,) + piece, BF16),
        pltpu.VMEM((2,) + piece, BF16),
        pltpu.VMEM((2, 2) + piece, BF16),
        pltpu.VMEM(piece, BF16),
        pltpu.VMEM(piece, BF16),
        pltpu.VMEM((HD, HD), F32),
        pltpu.VMEM((HD, HD), F32),
        pltpu.VMEM((column_half, rows), BF16),
        pltpu.VMEM((column_half, rows), BF16),
        pltpu.VMEM((1, HD), F32),
        pltpu.VMEM((1, HD), F32),
        pltpu.VMEM((2 * rows, own_rows), BF16),
        pltpu.VMEM((column_half, rows), F32),
        pltpu.VMEM((column_half, rows), F32),
        dma((11,)),
        dma((3, 2, 4)), dma((3, 2, 4)), dma((2,)), dma((2,)), dma((24,)), dma((24,)), dma((3,)), dma((3,)),
        dma((8,)), dma((8,)), dma((21,)), dma((21,)), dma((6,)), dma((6,)),
        dma((16,)), dma((4, 4)), dma((3, 4)), dma((3, 4)), dma((3,)), dma((3,)), dma((2,)), dma((2,)),
    ]
    out_shape = (
        jax.ShapeDtypeStruct((tokens, q_width), BF16),
        jax.ShapeDtypeStruct((2 * rows, own_rows), BF16),
        jax.ShapeDtypeStruct((column_half, rows), F32),
        jax.ShapeDtypeStruct((column_half, rows), F32),
    )
    results = pl.pallas_call(
        kernel,
        out_shape=out_shape,
        in_specs=[pl.BlockSpec(memory_space=pltpu.SMEM)] + [anyspec] * 7,
        out_specs=(anyspec,) * 4,
        scratch_shapes=scratch,
        compiler_params=pltpu.CompilerParams(
            collective_id=0, has_side_effects=True, vmem_limit_bytes=62 * 1024 * 1024
        ),
        cost_estimate=pl.CostEstimate(
            flops=1600000000, bytes_accessed=8000000, transcendentals=500000
        ),
    )(
        tile_counts, queries, features.reshape(own_rows, feature_width), key_weight.T,
        value_weight.T, query_gain.reshape(1, HD), key_gain.reshape(1, HD), out_grad,
    )
    query_grad, feature_t, key_t, value_t = pl.pallas_call(
        copy_out,
        out_shape=out_shape,
        in_specs=[anyspec] * 4,
        out_specs=(anyspec,) * 4,
        scratch_shapes=[pltpu.VMEM(o.shape, o.dtype) for o in out_shape] + [dma((7,)), dma((7,))],
        compiler_params=pltpu.CompilerParams(vmem_limit_bytes=62 * 1024 * 1024),
        cost_estimate=pl.CostEstimate(flops=0, bytes_accessed=3000000, transcendentals=0),
    )(*results)
    return (query_grad, feature_t.T.reshape(samples, own_rows, 2 * rows), key_t.T, value_t.T)


def solution(mesh):
    placed = (
        P("dp", "tensor"),
        P("dp", None, None),
        P("dp", "tensor"),
        P("dp", "tensor"),
        P(),
        P(),
        P("dp", "tensor"),
        P("dp"),
    )
    return jax.shard_map(
        shards,
        mesh=mesh,
        in_specs=placed,
        out_specs=(
            P("dp", "tensor"),
            P("dp", None, "tensor"),
            P("dp", "tensor"),
            P("dp", "tensor"),
        ),
        check_vma=False,
    )
```

```python
import functools
import math

import jax
import jax.numpy as jnp
from jax import lax
from jax.experimental import pallas as pl
from jax.experimental.pallas import tpu as pltpu
from jax.sharding import PartitionSpec as P

TILE_ROWS = 32
EPS = 1e-05
HD = 128
Y, X, ZL = 8, 4, 4
CH = 160
HOPS = {(0, 0): 4, (0, 1): 3, (1, 0): 3, (1, 1): 4}
PIECES = ((0, 240), (0, 128), (128, 112))
F32 = jnp.float32
BF16 = jnp.bfloat16
NT = (((1,), (1,)), ((), ()))
TN = (((0,), (0,)), ((), ()))


def dot(a, b, dims=(((1,), (0,)), ((), ()))):
    return lax.dot_general(a, b, dims, preferred_element_type=F32)


def kernel(
    tc_ref, q_hbm, feat_hbm, kwt_hbm, vwt_hbm, qg_hbm, kg_hbm, do_hbm,
    dq_hbm, ft_hbm, kgw_hbm, vgw_hbm,
    q_s, do_s, dq_s, feat_s, featT, wbuf, dsT, qn_s, w2_s, own_s, par_s, kbf_s, vbf_s, far_s,
    farr_s, g4_s, own_grad_s, other_grad_s, fterm, wterm, fx_s, yr_s, x1_s, x2_s, hz_s, hzr_s, vg_s, kg_s,
    kwt_s, vwt_s, qg_s, kg_in_s, ft_s, kgw_s, vgw_s,
    loc_sem, ag_ss, ag_rs, agz_ss, agz_rs, agc_ss, agc_rs, p_ss, p_rs,
    c_ss, c_rs, y_ss, y_rs, x_ss, x_rs, zf_ss, zf_rs, wc_ss, wc_rs, gz_ss, gz_rs, h_ss, h_rs,
):
    d = lax.axis_index("dp")
    t = lax.axis_index("tensor")
    y, zh, core = d // 4, (d // 2) % 2, d % 2
    zl, x = t // 4, t % 4
    low = (t % 2) == 0

    def at_y(step):
        return (((y + step + Y) % Y) * 4 + zh * 2 + core, t)

    right, left = at_y(1), at_y(-1)
    far_core = (d + 1 - 2 * core, t)
    far_z = (d + 2 - 4 * zh, t)
    partner = (d, t + 1 - 2 * (t % 2))
    diagonal = (d + 1 - 2 * core, t + 1 - 2 * (t % 2))
    x_right = (d, zl * 4 + (x + 1) % X)
    x_left = (d, zl * 4 + (x + X - 1) % X)
    z_to = [(d, ((zl + k) % ZL) * 4 + x) for k in (1, 2, 3)]

    barrier = pltpu.get_barrier_semaphore()
    peers = [right, left, far_core, far_z, x_right, x_left, diagonal] + z_to
    for peer in peers:
        pl.semaphore_signal(barrier, inc=1, device_id=peer, device_id_type=pl.DeviceIdType.MESH)

    tokens = q_s.shape[0]
    heads = q_s.shape[1] // HD
    width = CH * heads
    chunks = tokens // CH
    fetched = (
        (kwt_hbm, kwt_s), (vwt_hbm, vwt_s), (feat_hbm, feat_s), (q_hbm, q_s), (do_hbm, do_s),
        (qg_hbm, qg_s), (kg_hbm, kg_in_s),
    )
    copies = [
        pltpu.make_async_copy(src, dst, loc_sem.at[i]) for i, (src, dst) in enumerate(fetched)
    ]
    for copy in copies:
        copy.start()

    sent = []

    def drain(later=()):
        kept = [copy for copy in sent if any(copy is one for one in later)]
        for copy in sent:
            if not any(copy is one for one in later):
                copy.wait_send()
        sent[:] = kept

    def send(src, dst, ssem, rsem, dev):
        copy = pltpu.make_async_remote_copy(
            src_ref=src, dst_ref=dst, send_sem=ssem, recv_sem=rsem,
            device_id=dev, device_id_type=pl.DeviceIdType.MESH,
        )
        copy.start()
        sent.append(copy)
        return copy

    copies[0].wait()
    copies[1].wait()
    shard = jnp.concatenate((kwt_s[...], vwt_s[...]), 0).astype(F32)
    rows = shard.shape[1]
    shard = jnp.concatenate((shard, jnp.zeros((HD, 256 - rows), F32)), 1)
    mine = 2 * y + zh
    wbuf[mine, core] = jnp.transpose(shard)[:rows].astype(BF16)

    pl.semaphore_wait(barrier, len(peers))

    def c_of(step, stream):
        zz = zh if stream == 0 else 1 - zh
        return 2 * ((y + step + Y) % Y) + zz

    def piece_of(c, part):
        return wbuf.at[c, core, pl.ds(*PIECES[part])]

    def gather_send(part, way, hop):
        c = c_of((1 - hop) if way == 0 else (hop - 1), min(part, 1))
        ref = piece_of(c, part)
        return send(ref, ref, ag_ss.at[part, way, hop - 1], ag_rs.at[part, way, hop - 1],
                    right if way == 0 else left)

    across = []

    def core_send(c, part):
        ref = piece_of(c, part)
        i = len(across)
        across.append(send(ref, ref, agc_ss.at[i], agc_rs.at[i], far_core))

    def z_copy(c):
        dest = c // ZL
        return dest, pltpu.make_async_remote_copy(
            src_ref=wbuf.at[c, core], dst_ref=w2_s.at[zl, c % ZL, core],
            send_sem=zf_ss.at[c], recv_sem=zf_rs.at[zl, c % ZL],
            device_id=(d, dest * X + x), device_id_type=pl.DeviceIdType.MESH,
        )

    def z_send(c):
        dest, copy = z_copy(c)

        @pl.when(dest != zl)
        def _():
            copy.start()

    ag = {}
    zcopies = {}
    for part in (1, 2):
        ref = piece_of(mine, part)
        zcopies[part] = send(ref, ref, agz_ss.at[part - 1], agz_rs.at[part - 1], far_z)
    for way in (0, 1):
        ag[0, way, 1] = gather_send(0, way, 1)
    core_send(mine, 0)

    copies[2].wait()
    copies[3].wait()
    copies[5].wait()
    copies[6].wait()
    inverse = 1.0 / math.sqrt(HD)
    qg = qg_s[...]
    kg = kg_in_s[...]

    def shared_copy(part):
        group = pl.ds(part * 4, 4)
        return pltpu.make_async_remote_copy(
            src_ref=featT.at[group, 1 - core], dst_ref=fx_s.at[group],
            send_sem=c_ss.at[part], recv_sem=c_rs.at[part],
            device_id=far_core, device_id_type=pl.DeviceIdType.MESH,
        )

    def transpose_part(part, carry):
        cols = feat_s[:, pl.ds(pl.multiple_of(part * 1920, 1920), 1920)]
        featT[pl.ds(part * 4, 4)] = jnp.transpose(cols).reshape(4, 2, 240, HD)
        return carry

    def stack(ref, chunk):
        at = pl.ds(pl.multiple_of(chunk * CH, CH), CH)
        return jnp.concatenate([ref[at, h * HD:(h + 1) * HD] for h in range(heads)], 0)

    def wide(chunk):
        return pl.ds(pl.multiple_of(chunk * width, width), width)

    def query_norm(chunk, carry):
        xq = stack(q_s, chunk).astype(F32)
        r = lax.rsqrt(jnp.mean(xq * xq, -1, keepdims=True) + EPS)
        qn_s[wide(chunk), :] = (xq * r * qg).astype(BF16)
        return carry

    def gather_step(part, hop):
        for way in (1, 0):
            if hop > HOPS[min(part, 1), way]:
                continue
            ag[part, way, hop].wait_recv()
            if hop < HOPS[min(part, 1), way]:
                ag[part, way, hop + 1] = gather_send(part, way, hop + 1)
            c = c_of(-hop if way == 0 else hop, min(part, 1))
            core_send(c, part)
            if part == 2 or (part == 0 and hop > 1):
                if hop <= 2:
                    z_send(c)
                else:
                    z_later.append(c)

    arrived = 0
    marks = []
    z_later = []

    def project(part, total):
        at = (y // 2 + part) % 4
        cols = feat_s[:, pl.ds(pl.multiple_of(at * 1920, 1920), 1920)]
        return total + dot(cols, wbuf[pl.ds(4 * at, 4)].reshape(1920, HD))

    proj = jnp.zeros((HD, HD), F32)
    for hop in range(1, 6):
        if hop <= 4:
            gather_step(0, hop)
        if hop == 1:
            for part in (1, 2):
                zcopies[part].wait_recv()
                for way in (1, 0):
                    ag[part, way, 1] = gather_send(part, way, 1)
                core_send(c_of(0, 1), part)
            for c in (mine, c_of(-1, 0), c_of(1, 0), c_of(0, 1)):
                z_send(c)
        else:
            gather_step(1, hop - 1)
            gather_step(2, hop - 1)
        if hop <= 4:
            transpose_part(hop - 1, 0)
            query_norm(hop - 1, 0)
        marks.append(len(across))
        if hop >= 4:
            for mark, first_part, end_part in {4: ((2, 4, 5),), 5: ((3, 5, 6), (3, 7, 8), (4, 6, 7))}[hop]:
                for copy in across[arrived:marks[mark]]:
                    copy.wait_recv()
                arrived = max(arrived, marks[mark])
                for part in range(first_part, end_part):
                    proj = project(part, proj)
    own_s[...] = proj.astype(BF16)
    pcopy = send(own_s, par_s, p_ss.at[0], p_rs.at[0], partner)
    for c in z_later:
        z_send(c)
    for part in range(4):
        shared_copy(part).start()
    copies[4].wait()
    lax.fori_loop(4, chunks, query_norm, 0)
    lane = lax.broadcasted_iota(jnp.int32, (HD, HD), 1)
    half = lane < 64
    lowf = jnp.where(low, 1.0, 0.0).astype(F32)
    own = own_s[...].astype(F32)
    pcopy.wait_recv()
    other = par_s[...].astype(F32)
    first = own * lowf + other * (1.0 - lowf)
    second = other * lowf + own * (1.0 - lowf)
    keys = jnp.where(half, first, pltpu.roll(second, 64, 1))
    values = jnp.where(half, pltpu.roll(first, 64, 1), second)
    k_scale = lax.rsqrt(jnp.mean(keys * keys, -1, keepdims=True) + EPS)
    kbf_s[...] = (keys * k_scale * kg).astype(BF16)
    vbf_s[...] = values.astype(BF16)
    live = (
        lax.broadcasted_iota(jnp.int32, (HD, 1), 0) < tc_ref[0] * TILE_ROWS
    ).astype(F32)
    vg_s[...] = jnp.zeros_like(vg_s)
    kg_s[...] = jnp.zeros_like(kg_s)

    def attend(chunk, carry):
        qn = qn_s[wide(chunk), :]
        do = stack(do_s, chunk)
        e = jnp.exp(dot(kbf_s[...], qn, NT) * inverse) * live
        p = e * (1.0 / jnp.sum(e, 0, keepdims=True))
        pb = p.astype(BF16)
        vg_s[...] += dot(pb, do)
        pg = dot(vbf_s[...], do, NT)
        delta = jnp.sum(pb.astype(F32) * pg, 0, keepdims=True)
        ds = (p * (pg - delta)).astype(BF16)
        dsT[:, wide(chunk)] = ds
        kg_s[...] += dot(ds, qn)
        return carry

    lax.fori_loop(0, chunks, attend, 0, unroll=3)

    weighted = kg_s[...] * (inverse * kg)
    key_grad = k_scale * weighted - keys * (
        k_scale * k_scale * k_scale * jnp.mean(weighted * keys, -1, keepdims=True)
    )
    value_grad = vg_s[...]
    low_part = jnp.where(half, key_grad, pltpu.roll(value_grad, 64, 1))
    high_part = jnp.where(half, pltpu.roll(key_grad, 64, 1), value_grad)
    own_grad_s[...] = low_part * lowf + high_part * (1.0 - lowf)
    far_s[...] = (high_part * lowf + low_part * (1.0 - lowf)).astype(BF16)
    fcopy = send(far_s, farr_s.at[0], p_ss.at[1], p_rs.at[1], partner)
    ocopy = send(own_grad_s, other_grad_s, c_ss.at[4], c_rs.at[4], far_core)
    dcopy = send(far_s, farr_s.at[1], p_ss.at[2], p_rs.at[2], diagonal)

    def query_back(chunk, carry):
        xq = stack(q_s, chunk).astype(F32)
        r = lax.rsqrt(jnp.mean(xq * xq, -1, keepdims=True) + EPS)
        u = dot(dsT[:, wide(chunk)], kbf_s[...], TN) * (inverse * qg)
        m = jnp.mean(u * xq, -1, keepdims=True)
        back = (r * u - xq * (r * r * r * m)).astype(BF16)
        at = pl.ds(pl.multiple_of(chunk * CH, CH), CH)
        for h in range(heads):
            dq_s[at, h * HD:(h + 1) * HD] = back[h * CH:(h + 1) * CH]
        return carry

    drain((fcopy, ocopy, dcopy))
    lax.fori_loop(0, 3, query_back, 0)
    for part in range(4):
        shared_copy(part).wait_send()
    fcopy.wait_recv()
    g4_s[zl] = (own_grad_s[...] + farr_s[0].astype(F32)).astype(BF16)
    g = g4_s[zl]
    gz = []
    for k in (1, 2, 0):
        gz.append(send(g4_s.at[zl], g4_s.at[zl], gz_ss.at[k], gz_rs.at[k], z_to[k]))

    ocopy.wait_recv()
    dcopy.wait_recv()
    go = (other_grad_s[...] + farr_s[1].astype(F32)).astype(BF16)
    for part in range(4):
        shared_copy(part).wait_recv()

    def weight_term(step):
        for stream in (1, 0):
            c = c_of(step, stream)
            wterm[c] = (dot(featT[c, core], g) + dot(fx_s[c], go)).astype(BF16)

    def feature_term(xx):
        total = dot(wbuf[zl * X + xx].reshape(480, HD), g, NT)
        for dz in (1, 2, 3):
            src = (zl + dz) % ZL
            total += dot(w2_s[src, xx].reshape(480, HD), g4_s[src], NT)
        return total

    x2, xp, xm = (x + 2) % X, (x + 1) % X, (x + 3) % X
    xs = {}

    def x_send(name, slot, src, dst, dev):
        xs[name] = send(src, dst, x_ss.at[slot], x_rs.at[slot], dev)

    def x_start():
        for copy in gz + wc:
            copy.wait_recv()
        for xx in (x2, xp, xm):
            fterm[xx] = feature_term(xx).astype(BF16).reshape(2, 240, HD)
            if xx is x2:
                x_send("r1", 0, fterm.at[x2, 0], x1_s.at[0], x_right)
                x_send("l1", 1, fterm.at[x2, 1], x1_s.at[1], x_left)
            elif xx is xp:
                x_send("r2", 2, fterm.at[xp, 1], x2_s.at[0, 1], x_right)
            else:
                x_send("l2", 3, fterm.at[xm, 0], x2_s.at[1, 0], x_left)

    wc = []

    def w2_across():
        for dz in (1, 3, 2):
            src = (zl + dz) % ZL
            for i in range(4):
                ref = w2_s.at[src, i, core]
                pltpu.make_async_remote_copy(
                    src_ref=ref, dst_ref=ref, send_sem=zf_ss.at[0], recv_sem=zf_rs.at[src, i],
                    device_id=far_core, device_id_type=pl.DeviceIdType.MESH,
                ).wait_recv()
                wc.append(send(ref, ref, wc_ss.at[dz - 1, i], wc_rs.at[dz - 1, i], far_core))

    slots = {}
    for part in range(3):
        for way in (0, 1):
            for hop in range(1, HOPS[min(part, 1), way] + 1):
                slots[part, way, hop] = len(slots)
    ys = {}

    def ring_send(part, way, hop):
        stream = min(part, 1)
        step = HOPS[stream, way] - hop + 1
        c = c_of(step if way == 0 else -step, stream)
        slot = slots[part, way, hop]
        at = pl.ds(*PIECES[part])
        count = PIECES[part][1]
        if hop > 1:
            ys[part, way, hop - 1].wait_recv()
            last = slots[part, way, hop - 1]
            wterm[c, at] = (
                wterm[c, at].astype(F32) + yr_s[last, :count].astype(F32)
            ).astype(BF16)
        ys[part, way, hop] = send(
            wterm.at[c, at], yr_s.at[slot, pl.ds(0, count)], y_ss.at[slot], y_rs.at[slot],
            right if way == 0 else left,
        )

    def ring_hop(hop):
        for part, way in ((1, 1), (1, 0), (2, 1), (2, 0), (0, 0), (0, 1)):
            if hop <= HOPS[min(part, 1), way]:
                ring_send(part, way, hop)

    def x_relay():
        for name, way, xx in (("r", 0, xp), ("l", 1, xm)):
            xs[name + "1"].wait_recv()
            fterm[xx, way] = (
                fterm[xx, way].astype(F32) + x1_s[way].astype(F32)).astype(BF16)
            x_send(name + "3", 4 + way, fterm.at[xx, way], x2_s.at[way, way],
                   x_right if way == 0 else x_left)

    def final_rows(part):
        at = pl.ds(*PIECES[part])
        total = wterm[c_of(0, min(part, 1)), at].astype(F32)
        for way in (0, 1):
            last = part, way, HOPS[min(part, 1), way]
            ys[last].wait_recv()
            total += yr_s[slots[last], :PIECES[part][1]].astype(F32)
        return total

    weight_term(4)
    ring_send(1, 1, 1)
    ring_send(2, 1, 1)
    ring_send(0, 0, 1)
    weight_term(3)
    ring_send(1, 0, 1)
    ring_send(2, 0, 1)
    weight_term(5)
    ring_send(0, 1, 1)

    def later_terms(j, carry):
        weight_term(6 + j)
        return carry

    lax.fori_loop(0, 5, later_terms, 0)
    ring_hop(2)
    ring_hop(3)
    w2_across()
    ring_hop(4)
    x_start()
    hcopies = []
    for part in (1, 2):
        at = pl.ds(*PIECES[part])
        hz_s[at] = final_rows(part).astype(BF16)
        hcopies.append(
            send(hz_s.at[at], hzr_s.at[at], h_ss.at[part - 1], h_rs.at[part - 1], far_z))
    x_relay()
    own_term = feature_term(x)
    lax.fori_loop(3, chunks, query_back, 0)
    for name in ("r2", "l2", "r3", "l3"):
        xs[name].wait_recv()
    own_term += x2_s[0].reshape(480, HD).astype(F32) + x2_s[1].reshape(480, HD).astype(F32)
    ft_s[...] = own_term.astype(BF16)
    outs = [
        pltpu.make_async_copy(dq_s, dq_hbm, loc_sem.at[7]),
        pltpu.make_async_copy(ft_s, ft_hbm, loc_sem.at[8]),
        pltpu.make_async_copy(kgw_s, kgw_hbm, loc_sem.at[9]),
        pltpu.make_async_copy(vgw_s, vgw_hbm, loc_sem.at[10]),
    ]
    outs[0].start()
    outs[1].start()

    own_rows = final_rows(0)
    drain(hcopies)
    for dz in (1, 2, 3):
        for i in range(4):
            z_copy(4 * ((zl + dz) % ZL) + i)[1].wait_send()
    for copy in hcopies:
        copy.wait_recv()
    own_rows += hzr_s[...].astype(F32)
    padded = jnp.concatenate((own_rows, jnp.zeros((256 - rows, HD), F32)), 0)
    turned = jnp.transpose(padded)
    kgw_s[...] = turned[:64, :rows]
    vgw_s[...] = turned[64:, :rows]
    outs[2].start()
    outs[3].start()
    drain()
    for copy in outs:
        copy.wait()


def copy_out(a, b, c, e, a_out, b_out, c_out, e_out, a_s, b_s, c_s, e_s, in_sems, out_sems):
    refs = [(b, b_s, b_out), (c, c_s, c_out), (e, e_s, e_out)]
    step = a_s.shape[0] // 4
    for i in range(4):
        at = pl.ds(i * step, step)
        refs.append((a.at[at], a_s.at[at], a_out.at[at]))
    loads = [
        pltpu.make_async_copy(src, mid, in_sems.at[i]) for i, (src, mid, dst) in enumerate(refs)
    ]
    stores = [
        pltpu.make_async_copy(mid, dst, out_sems.at[i]) for i, (src, mid, dst) in enumerate(refs)
    ]
    for copy in loads:
        copy.start()
    for load, store in zip(loads, stores):
        load.wait()
        store.start()
    for copy in stores:
        copy.wait()


def shards(
    queries, features, key_weight, value_weight, query_gain, key_gain, out_grad, tile_counts
):
    samples, own_rows, feature_width = features.shape
    tokens, q_width = queries.shape
    rows, column_half = key_weight.shape
    anyspec = pl.BlockSpec(memory_space=pl.ANY)
    dma = pltpu.SemaphoreType.DMA
    piece = (rows, HD)
    scratch = [
        pltpu.VMEM((tokens, q_width), BF16),
        pltpu.VMEM((tokens, q_width), BF16),
        pltpu.VMEM((tokens, q_width), BF16),
        pltpu.VMEM((own_rows, feature_width), BF16),
        pltpu.VMEM((16, 2) + piece, BF16),
        pltpu.VMEM((16, 2) + piece, BF16),
        pltpu.VMEM((HD, tokens * q_width // HD), BF16),
        pltpu.VMEM((tokens * q_width // HD, HD), BF16),
        pltpu.VMEM((ZL, X, 2) + piece, BF16),
    ]
    scratch += [pltpu.VMEM((HD, HD), BF16)] * 5
    scratch += [
        pltpu.VMEM((2, HD, HD), BF16),
        pltpu.VMEM((ZL, HD, HD), BF16),
        pltpu.VMEM((HD, HD), F32),
        pltpu.VMEM((HD, HD), F32),
        pltpu.VMEM((X, 2) + piece, BF16),
        pltpu.VMEM((16,) + piece, BF16),
        pltpu.VMEM((16,) + piece, BF16),
        pltpu.VMEM((21,) + piece, BF16),
        pltpu.VMEM((2,) + piece, BF16),
        pltpu.VMEM((2, 2) + piece, BF16),
        pltpu.VMEM(piece, BF16),
        pltpu.VMEM(piece, BF16),
        pltpu.VMEM((HD, HD), F32),
        pltpu.VMEM((HD, HD), F32),
        pltpu.VMEM((column_half, rows), BF16),
        pltpu.VMEM((column_half, rows), BF16),
        pltpu.VMEM((1, HD), F32),
        pltpu.VMEM((1, HD), F32),
        pltpu.VMEM((2 * rows, own_rows), BF16),
        pltpu.VMEM((column_half, rows), F32),
        pltpu.VMEM((column_half, rows), F32),
        dma((11,)),
        dma((3, 2, 4)), dma((3, 2, 4)), dma((2,)), dma((2,)), dma((24,)), dma((24,)), dma((3,)), dma((3,)),
        dma((8,)), dma((8,)), dma((21,)), dma((21,)), dma((6,)), dma((6,)),
        dma((16,)), dma((4, 4)), dma((3, 4)), dma((3, 4)), dma((3,)), dma((3,)), dma((2,)), dma((2,)),
    ]
    out_shape = (
        jax.ShapeDtypeStruct((tokens, q_width), BF16),
        jax.ShapeDtypeStruct((2 * rows, own_rows), BF16),
        jax.ShapeDtypeStruct((column_half, rows), F32),
        jax.ShapeDtypeStruct((column_half, rows), F32),
    )
    results = pl.pallas_call(
        kernel,
        out_shape=out_shape,
        in_specs=[pl.BlockSpec(memory_space=pltpu.SMEM)] + [anyspec] * 7,
        out_specs=(anyspec,) * 4,
        scratch_shapes=scratch,
        compiler_params=pltpu.CompilerParams(
            collective_id=0, has_side_effects=True, vmem_limit_bytes=62 * 1024 * 1024
        ),
        cost_estimate=pl.CostEstimate(
            flops=1600000000, bytes_accessed=8000000, transcendentals=500000
        ),
    )(
        tile_counts, queries, features.reshape(own_rows, feature_width), key_weight.T,
        value_weight.T, query_gain.reshape(1, HD), key_gain.reshape(1, HD), out_grad,
    )
    query_grad, feature_t, key_t, value_t = pl.pallas_call(
        copy_out,
        out_shape=out_shape,
        in_specs=[anyspec] * 4,
        out_specs=(anyspec,) * 4,
        scratch_shapes=[pltpu.VMEM(o.shape, o.dtype) for o in out_shape] + [dma((7,)), dma((7,))],
        compiler_params=pltpu.CompilerParams(vmem_limit_bytes=62 * 1024 * 1024),
        cost_estimate=pl.CostEstimate(flops=0, bytes_accessed=3000000, transcendentals=0),
    )(*results)
    return (query_grad, feature_t.T.reshape(samples, own_rows, 2 * rows), key_t.T, value_t.T)


def solution(mesh):
    placed = (
        P("dp", "tensor"),
        P("dp", None, None),
        P("dp", "tensor"),
        P("dp", "tensor"),
        P(),
        P(),
        P("dp", "tensor"),
        P("dp"),
    )
    return jax.shard_map(
        shards,
        mesh=mesh,
        in_specs=placed,
        out_specs=(
            P("dp", "tensor"),
            P("dp", None, "tensor"),
            P("dp", "tensor"),
            P("dp", "tensor"),
        ),
        check_vma=False,
    )
```
